32 devices in a mesh: grp: 2 (over y), lon: 8 (over z, x), lat: 2 (over core).
Axes of the slice: x: 2, y: 2, z: 4, core: 2. Of those that a mesh axis runs over, the one named last changes fastest.
Arguments:
- right_side: bfloat16 [64, 32768], P(None, ('grp', 'lon', 'lat')), parts along dimension 1, may hold values from -21 to 21
- stiffness_blocks: bfloat16 [768, 128, 128], P(('grp', 'lon', 'lat')), parts along dimension 0, may hold values from -0.21875 to 0.21875
- block_pattern: int32 [768, 2], P(('grp', 'lon', 'lat')), parts along dimension 0, may hold values from 0 to 7
- reaction: float32 [32768], P(('grp', 'lon', 'lat')), parts along dimension 0, may hold values from 1 to 4
- lumped_mass: float32 [32768], P(('grp', 'lon', 'lat')), parts along dimension 0, may hold values from 0.5 to 2
- obs_precision: float32 [32768], P(('grp', 'lon', 'lat')), parts along dimension 0, may hold values from 0.5 to 2
- coupling: bfloat16 [4096, 128], P(('grp', 'lon', 'lat')), parts along dimension 0, may hold values from -0.375 to 0.375
- east_rows: int32 [32, 128], P(('grp', 'lon', 'lat')), parts along dimension 0, may hold values from 0 to 1023
- west_rows: int32 [32, 128], P(('grp', 'lon', 'lat')), parts along dimension 0, may hold values from 0 to 1023
- iface_count: int32 [32], P(('grp', 'lon', 'lat')), parts along dimension 0, may hold values from 32 to 128, as said below
- node_count: int32 [32], P(('grp', 'lon', 'lat')), parts along dimension 0, may hold values from 512 to 1024, as said below
- deflation: bfloat16 [64, 32768], P(None, ('grp', 'lon', 'lat')), parts along dimension 1, may hold values from -0.1875 to 0.1875
- coarse_inverse: bfloat16 [2048, 1024], P(('grp', 'lon', 'lat')), parts along dimension 0, may hold values from -1 to 7, as said below
Outputs:
- solution: float32 [64, 32768], P(None, ('grp', 'lon', 'lat')), parts along dimension 1
The draws below stay inside these ranges and needn't reach their ends.
There are 2 independent parts, one for each index of `grp`. The reference program is written for one: setup_inputs(seed, part) draws one part's arguments, and reference() takes and returns one part's arrays. A program takes and returns all parts, laid end to end along the dimension named above; each array names one. Nothing has to cross between parts.
Inputs may be any that keep to these rules, and one draw needn't show every extreme that they name: `iface_count`: some subdomain uses all 128 interface slots. `node_count`: some subdomain has all of its nodes live. `coarse_inverse`: symmetric positive definite.
All inputs are finite; a program needn't handle non-finite values.
Results may differ from the reference program's by a relative error of at most 0.0046.
Values may be sent and summed in bfloat16 or wider, within the bound.
No kernel may reach another device: no remote copies, remote signals or barrier semaphores. Data moves between devices by JAX's collectives and lax.ppermute only.
A program may use at most 64 MiB of HBM per device.

```python
import math
import jax
import jax.numpy as jnp
from jax import lax

S = 64
BLK = 128
NB = 8
PAT_ROW = 3
KV = 64
IFN = 128
ITERS = 2
SECTORS = 8
BANDS = 2
NPAT = 24
NODES = 16384
N_LON = 8
N_LAT = 2


def draw_right_side(key, part):
    key = jax.random.fold_in(key, 11)
    domain = (jnp.arange(NODES) // (NB * BLK)).astype(jnp.float32)
    fraction = domain / float(max(SECTORS * BANDS - 1, 1))
    base = jnp.clip(jax.random.normal(key, (S, NODES), jnp.float32), -4.0, 4.0)
    growth = 3.0
    return (base * growth ** fraction[None, :]).astype(jnp.bfloat16)


def draw_iface_count(key, part):
    key = jax.random.fold_in(key, 12)
    first, second = jax.random.split(key)
    domains = SECTORS * BANDS
    counts = jax.random.randint(first, (domains,), IFN // 4, IFN + 1)
    chosen = jax.random.randint(second, (), 0, domains)
    return jnp.where(jnp.arange(domains) == chosen, IFN, counts).astype(jnp.int32)


def draw_node_count(key, part):
    key = jax.random.fold_in(key, 13)
    first, second = jax.random.split(key)
    domains = SECTORS * BANDS
    counts = jax.random.randint(first, (domains,), NB * BLK // 2, NB * BLK + 1)
    chosen = jax.random.randint(second, (), 0, domains)
    return jnp.where(jnp.arange(domains) == chosen, NB * BLK, counts).astype(jnp.int32)


def draw_coarse_inverse(key, part):
    key = jax.random.fold_in(key, 14)
    first, second = jax.random.split(key)
    order = KV * SECTORS * BANDS
    scale = 1.0 / math.sqrt(order)
    raw = jnp.clip(jax.random.normal(first, (order, order), jnp.float32), -4.0, 4.0)
    spread = (raw + raw.T) * (scale / math.sqrt(2.0))
    diagonal = jax.random.uniform(second, (order,), jnp.float32, 3.0, 7.0)
    rows = lax.broadcasted_iota(jnp.int32, (order, order), 0)
    cols = lax.broadcasted_iota(jnp.int32, (order, order), 1)
    return jnp.where(rows == cols, diagonal[:, None], spread).astype(jnp.bfloat16)


def plant(array, own_key, smallest, high):
    spot = [jax.random.randint(jax.random.fold_in(own_key, axis), (), 0, length) for axis, length in enumerate(array.shape)]
    main_axis = array.shape.index(max(array.shape))
    beside = spot[:main_axis] + [(spot[main_axis] + 1) % array.shape[main_axis]] + spot[main_axis + 1:]
    return array.at[tuple(spot)].set(smallest).at[tuple(beside)].set(high)


def block_scale(key, dims, pieces, smallest, high):
    gain, own = 1.0, jax.random.fold_in(key, 6)
    for axis_at, parts in pieces:
        steps = jnp.exp(jax.random.uniform(jax.random.fold_in(own, axis_at), (parts,), jnp.float32, smallest / len(pieces), high / len(pieces)))
        gain = gain * jnp.repeat(steps, dims[axis_at] // parts).reshape([-1 if axis == axis_at else 1 for axis in range(len(dims))])
    return gain


def centred(stream_key, shape, scale, reach, cuts=(), kind=jnp.bfloat16):
    drawn = scale * jax.random.normal(stream_key, shape, jnp.float32)
    if cuts:
        drawn = drawn * block_scale(stream_key, shape, cuts, -0.22, 0.18)
    return jnp.clip(drawn, -reach, reach).astype(kind)


def setup_inputs(seed: int = 0, part: int = 0) -> dict:
    key_list = jax.random.split(jax.random.key(seed), 14)
    own_keys = jax.random.split(jax.random.fold_in(key_list[13], part), 14)
    return {
        "right_side": draw_right_side(jax.random.fold_in(jax.random.fold_in(key_list[13], part), 71), part),
        "stiffness_blocks": centred(own_keys[1], (N_LON * N_LAT * NPAT, BLK, BLK), (2 * PAT_ROW * BLK) ** -0.5, 0.21875, ((0, 16),)),
        "block_pattern": plant(jax.random.randint(own_keys[2], (N_LON * N_LAT * NPAT, 2), 0, NB), jax.random.fold_in(own_keys[2], 1), 0, NB - 1).astype(jnp.int32),
        "reaction": jnp.clip(jnp.exp(math.log(4.0) - 1.3862944 * jax.random.uniform(own_keys[3], (NODES,), jnp.float32) ** block_scale(own_keys[3], (NODES,), ((0, 16),), -0.2, 0.2)), 1.0, 4.0),
        "lumped_mass": jnp.clip(jnp.exp(math.log(2.0) - 1.3862944 * jax.random.uniform(own_keys[4], (NODES,), jnp.float32) ** block_scale(own_keys[4], (NODES,), ((0, 16),), -0.2, 0.2)), 0.5, 2.0),
        "obs_precision": jnp.clip(jnp.exp(math.log(2.0) - 1.3862944 * jax.random.uniform(own_keys[5], (NODES,), jnp.float32) ** block_scale(own_keys[5], (NODES,), ((0, 16),), -0.2, 0.2)), 0.5, 2.0),
        "coupling": centred(own_keys[6], (N_LON * N_LAT * IFN, IFN), (2 * IFN) ** -0.5, 0.375, ((0, 16),)),
        "east_rows": plant(jax.random.randint(own_keys[7], (N_LON * N_LAT, IFN), 0, NB * BLK), jax.random.fold_in(own_keys[7], 1), 0, (NB * BLK) - 1).astype(jnp.int32),
        "west_rows": plant(jax.random.randint(own_keys[8], (N_LON * N_LAT, IFN), 0, NB * BLK), jax.random.fold_in(own_keys[8], 1), 0, (NB * BLK) - 1).astype(jnp.int32),
        "iface_count": draw_iface_count(jax.random.fold_in(jax.random.fold_in(key_list[13], part), 71), part),
        "node_count": draw_node_count(jax.random.fold_in(jax.random.fold_in(key_list[13], part), 71), part),
        "deflation": centred(own_keys[11], (KV, NODES), (NB * BLK) ** -0.5, 0.1875, ((1, 16),)),
        "coarse_inverse": draw_coarse_inverse(jax.random.fold_in(jax.random.fold_in(key_list[13], part), 71), part),
    }


def local_blocks(packed):
    rounded_piece, weights, layout = packed
    shaped = rounded_piece.reshape(S, NB, BLK)
    from_cols = shaped[:, layout[:, 1], :].astype(jnp.float32)
    from_rows = shaped[:, layout[:, 0], :].astype(jnp.float32)
    wide = weights.astype(jnp.float32)
    forward = jnp.einsum("skj,kij->ski", from_cols, wide)
    backward = jnp.einsum("ski,kij->skj", from_rows, wide)
    summed = jnp.zeros((S, NB, BLK), jnp.float32)
    summed = summed.at[:, layout[:, 0], :].add(forward)
    summed = summed.at[:, layout[:, 1], :].add(backward)
    return summed.reshape(S, NB * BLK)


def roll_sectors(values, offset):
    shaped = values.reshape((SECTORS, BANDS) + values.shape[1:])
    return jnp.roll(shaped, offset, axis=0).reshape(values.shape)


def reference(right_side, stiffness_blocks, block_pattern, reaction, lumped_mass, obs_precision, coupling, east_rows, west_rows, iface_count, node_count, deflation, coarse_inverse):
    domains = SECTORS * BANDS
    per_domain = NB * BLK

    def split(values):
        return values.reshape(values.shape[0], domains, per_domain).transpose(1, 0, 2)

    active = (jnp.arange(per_domain)[None, None, :] < node_count[:, None, None]).astype(jnp.float32)
    diag_term = reaction.reshape(domains, 1, per_domain)
    lumped = lumped_mass.reshape(domains, 1, per_domain)
    observed = obs_precision.reshape(domains, 1, per_domain)
    live = jnp.arange(IFN)[None, :] < iface_count[:, None]
    coupler = jnp.where(live[:, :, None] & live[:, None, :], coupling.reshape(domains, IFN, IFN).astype(jnp.float32), jnp.float32(0.0))
    weights_all = stiffness_blocks.reshape(domains, NPAT, BLK, BLK)
    layout_all = block_pattern.reshape(domains, NPAT, 2)
    vectors = deflation.reshape(KV, domains, per_domain).transpose(1, 0, 2).astype(jnp.float32)
    jacobi = 1.0 / (observed + diag_term * diag_term / lumped)

    def pick(values, indices):
        return jax.vmap(lambda block_values, where_rows: block_values[:, where_rows])(values, indices)

    def place(values, indices, added):
        return jax.vmap(lambda block_values, where_rows, extra: block_values.at[:, where_rows].add(extra))(values, indices, added)

    def stiffness(field):
        rounded = field.astype(jnp.bfloat16)
        summed = lax.map(local_blocks, (rounded, weights_all, layout_all))
        wide = rounded.astype(jnp.float32)
        east_vals = pick(wide, east_rows)
        west_vals = pick(wide, west_rows)
        outgoing = jnp.einsum("dsa,dab->dsb", east_vals, coupler)
        arrived = roll_sectors(west_vals, -1)
        incoming = roll_sectors(outgoing, 1)
        into_east = jnp.einsum("dsb,dab->dsa", arrived, coupler)
        result = diag_term * field + summed
        result = place(result, east_rows, into_east)
        return place(result, west_rows, incoming)

    def apply_precision(field):
        inner = stiffness(active * field) / lumped
        return active * (stiffness(inner) + observed * field)

    def precondition(residual):
        coarse = jnp.einsum("dsn,dkn->dsk", residual.astype(jnp.bfloat16).astype(jnp.float32), vectors).astype(jnp.bfloat16)
        flat = coarse.transpose(1, 0, 2).reshape(S, domains * KV)
        fix = jnp.dot(flat, coarse_inverse.T, preferred_element_type=jnp.float32).astype(jnp.bfloat16)
        fix_split = fix.reshape(S, domains, KV).transpose(1, 0, 2).astype(jnp.float32)
        spread = jnp.einsum("dsk,dkn->dsn", fix_split, vectors)
        return active * (jacobi * residual + spread)

    def inner_product(first, second):
        return jnp.sum(first * second, axis=(0, 2))[None, :, None]

    residual = active * split(right_side.astype(jnp.float32))
    solution = jnp.zeros_like(residual)
    smoothed = precondition(residual)
    direction = smoothed
    norm_now = inner_product(residual, smoothed)
    for iteration in range(ITERS):
        image = apply_precision(direction)
        step_size = norm_now / inner_product(direction, image)
        solution = solution + step_size * direction
        residual = residual - step_size * image
        if iteration + 1 < ITERS:
            smoothed = precondition(residual)
            norm_next = inner_product(residual, smoothed)
            direction = smoothed + (norm_next / norm_now) * direction
            norm_now = norm_next
    return solution.transpose(1, 0, 2).reshape(S, NODES)
```

```python
import jax
import jax.numpy as jnp
from jax import lax
from jax.sharding import PartitionSpec as P

AXES = ("lon", "lat")


def from_behind(array, axis, by):
    size = lax.axis_size(axis)
    return lax.ppermute(array, axis, [(i, (i + by) % size) for i in range(size)])


def exchange(chunk):
    domains = lax.axis_size("lon") * lax.axis_size("lat")
    copies = jnp.broadcast_to(chunk[None], (domains,) + chunk.shape)
    return lax.all_to_all(copies, AXES, split_axis=0, concat_axis=0, tiled=True)


def body(
    right_side,
    stiffness_blocks,
    block_pattern,
    reaction,
    lumped_mass,
    obs_precision,
    coupling,
    east_rows,
    west_rows,
    iface_count,
    node_count,
    deflation,
    coarse_inverse,
):
    samples, per_domain = right_side.shape
    block = stiffness_blocks.shape[1]
    nblocks = per_domain // block
    slots = coupling.shape[0]
    vectors = deflation.shape[0]
    domains = lax.axis_size("lon") * lax.axis_size("lat")
    active = (jnp.arange(per_domain) < node_count[0]).astype(jnp.float32)
    live = jnp.arange(slots) < iface_count[0]
    coupler = jnp.where(live[:, None] & live[None, :], coupling, jnp.zeros_like(coupling))
    row_onehot = (block_pattern[:, 0:1] == jnp.arange(nblocks)[None, :]).astype(jnp.float32)
    col_onehot = (block_pattern[:, 1:2] == jnp.arange(nblocks)[None, :]).astype(jnp.float32)
    east_index = east_rows[0]
    west_index = west_rows[0]
    jacobi = 1.0 / (obs_precision + reaction * reaction / lumped_mass)
    contract_last = (((1,), (1,)), ((), ()))
    inverse_parts = coarse_inverse.reshape(vectors, domains, vectors)

    def stiffness(field):
        rounded = field.astype(jnp.bfloat16)
        arrived = from_behind(jnp.take(rounded, west_index, axis=1), "lon", -1)
        outgoing = jnp.dot(
            jnp.take(rounded, east_index, axis=1), coupler, preferred_element_type=jnp.float32
        )
        incoming = from_behind(outgoing.astype(jnp.bfloat16), "lon", 1).astype(outgoing.dtype)
        shaped = rounded.reshape(samples, nblocks, block)
        from_cols = jnp.take(shaped, block_pattern[:, 1], axis=1)
        from_rows = jnp.take(shaped, block_pattern[:, 0], axis=1)
        forward = jnp.einsum(
            "skj,kij->ski", from_cols, stiffness_blocks, preferred_element_type=jnp.float32
        )
        backward = jnp.einsum(
            "ski,kij->skj", from_rows, stiffness_blocks, preferred_element_type=jnp.float32
        )
        summed = jnp.einsum("kn,ski->sni", row_onehot, forward, precision=lax.Precision.HIGHEST)
        summed = summed + jnp.einsum(
            "kn,ski->sni", col_onehot, backward, precision=lax.Precision.HIGHEST
        )
        result = reaction * field + summed.reshape(samples, per_domain)
        into_east = lax.dot_general(
            arrived, coupler, contract_last, preferred_element_type=jnp.float32
        )
        result = result.at[:, east_index].add(into_east)
        return result.at[:, west_index].add(incoming)

    def precision(field):
        inner = stiffness(active * field) / lumped_mass
        return active * (stiffness(inner) + obs_precision * field)

    def coarse_of(values):
        return lax.dot_general(
            values.astype(jnp.bfloat16), deflation, contract_last, preferred_element_type=jnp.float32
        )

    def precondition(residual, coarse_all):
        coarse_fix = jnp.einsum(
            "dsk,jdk->sj", coarse_all, inverse_parts, preferred_element_type=jnp.float32
        ).astype(jnp.bfloat16)
        spread = jnp.dot(coarse_fix, deflation, preferred_element_type=jnp.float32)
        return active * (jacobi * residual + spread)

    def local_dot(first, second):
        return jnp.sum(first * second, axis=1)

    residual = active * right_side.astype(jnp.float32)
    coarse0 = exchange(coarse_of(residual).astype(jnp.bfloat16))
    direction = precondition(residual, coarse0)
    image = precision(direction)
    packed = jnp.concatenate(
        [
            coarse_of(image),
            local_dot(residual, direction)[:, None],
            local_dot(direction, image)[:, None],
            jnp.zeros((samples, 62), jnp.float32),
        ],
        axis=1,
    )
    second = exchange(packed)
    sums = jnp.sum(second[:, :, vectors : vectors + 2], axis=0)
    norm0, curved0 = sums[:, 0], sums[:, 1]
    step0 = norm0 / curved0
    residual = residual - step0[:, None] * image
    coarse1 = coarse0.astype(jnp.float32) - step0[None, :, None] * second[:, :, :vectors]
    smoothed = precondition(residual, coarse1.astype(jnp.bfloat16))
    smooth_image = precision(smoothed)
    partial = jnp.stack(
        [
            local_dot(residual, smoothed),
            local_dot(smoothed, smooth_image),
            local_dot(smoothed, image),
        ]
    )
    norm1, curved, cross = jnp.sum(exchange(partial), axis=0)
    beta = norm1 / norm0
    curved1 = curved + beta * (2.0 * cross + beta * curved0)
    step1 = norm1 / curved1
    return (step0 + step1 * beta)[:, None] * direction + step1[:, None] * smoothed


def solution(mesh):
    placed = (
        P(None, ("grp", "lon", "lat")),
        P(("grp", "lon", "lat"), None, None),
        P(("grp", "lon", "lat"), None),
        P(("grp", "lon", "lat")),
        P(("grp", "lon", "lat")),
        P(("grp", "lon", "lat")),
        P(("grp", "lon", "lat"), None),
        P(("grp", "lon", "lat"), None),
        P(("grp", "lon", "lat"), None),
        P(("grp", "lon", "lat")),
        P(("grp", "lon", "lat")),
        P(None, ("grp", "lon", "lat")),
        P(("grp", "lon", "lat"), None),
    )
    return jax.shard_map(
        body, mesh=mesh, in_specs=placed, out_specs=P(None, ("grp", "lon", "lat")), check_vma=False
    )
```

```python
import jax
import jax.numpy as jnp
import numpy as np
from jax import lax
from jax.experimental import pallas as pl
from jax.experimental.pallas import tpu as pltpu
from jax.sharding import PartitionSpec as P

F32 = jnp.float32
BF16 = jnp.bfloat16
VMEM = pl.BlockSpec(memory_space=pltpu.VMEM)
SMEM = pl.BlockSpec(memory_space=pltpu.SMEM)
LANES = 128


def dot(a, b, ca=1, cb=0):
    return lax.dot_general(a, b, (((ca,), (cb,)), ((), ())), preferred_element_type=F32)


def call(kernel, outs, specs, args, flops, scratch=()):
    moved = sum(int(np.prod(a.shape)) * a.dtype.itemsize for a in args)
    return pl.pallas_call(
        kernel,
        out_shape=[jax.ShapeDtypeStruct(s, t) for s, t in outs],
        in_specs=specs,
        out_specs=[VMEM] * len(outs),
        scratch_shapes=list(scratch),
        compiler_params=pltpu.CompilerParams(vmem_limit_bytes=32 * 1024 * 1024),
        cost_estimate=pl.CostEstimate(flops=flops, bytes_accessed=moved, transcendentals=0),
    )(*args)


def active_of(count_ref, nodes):
    return (lax.broadcasted_iota(jnp.int32, (1, nodes), 1) < count_ref[0]).astype(F32)


def fold(values):
    half = values.shape[0] // 2
    return jnp.concatenate([values[:half], values[half:]], axis=1)


def column_of(row):
    return jnp.transpose(jnp.broadcast_to(row, (LANES, LANES)))[:, 0:1]


def row_of(first, second):
    both = jnp.concatenate([first, second], axis=0)
    return jnp.transpose(jnp.broadcast_to(both, (LANES, LANES)))[0:1]


def row_sum(first, second):
    return jnp.sum(first * second, axis=1, keepdims=True)


def coarse_kernel(count_ref, right_ref, vectors_ref, chunk_ref):
    active = active_of(count_ref, right_ref.shape[1]).astype(BF16)
    coarse = dot(vectors_ref[...], right_ref[...] * active, 1, 1)
    chunk_ref[...] = fold(coarse).astype(BF16)


def dense_kernel(pattern_ref, blocks_ref, dense_ref, total_ref):
    count, block, _ = blocks_ref.shape
    nodes = dense_ref.shape[0]

    def clear(i, carry):
        total_ref[pl.ds(pl.multiple_of(i * block, block), block), :] = jnp.zeros((block, nodes), F32)
        return carry

    lax.fori_loop(0, nodes // block, clear, 0)

    def place(k, carry):
        rows = pl.ds(pl.multiple_of(pattern_ref[k, 0] * block, block), block)
        cols = pl.ds(pl.multiple_of(pattern_ref[k, 1] * block, block), block)
        values = blocks_ref[k].astype(F32)
        total_ref[rows, cols] += values
        total_ref[cols, rows] += jnp.transpose(values)
        return carry

    lax.fori_loop(0, count, place, 0)

    def narrow(i, carry):
        rows = pl.ds(pl.multiple_of(i * block, block), block)
        dense_ref[rows, :] = total_ref[rows, :].astype(BF16)
        return carry

    lax.fori_loop(0, nodes // block, narrow, 0)


def edge_kernel(iface_ref, coupling_ref, east_ref, west_ref, mass_ref, edge_ref, to_west_ref, to_east_ref):
    slots = coupling_ref.shape[0]
    nodes = mass_ref.shape[1]
    live_a = lax.broadcasted_iota(jnp.int32, (slots, slots), 0) < iface_ref[0]
    live_b = lax.broadcasted_iota(jnp.int32, (slots, slots), 1) < iface_ref[0]
    link = jnp.where(live_a & live_b, coupling_ref[...], jnp.zeros((slots, slots), BF16))
    node = lax.broadcasted_iota(jnp.int32, (slots, nodes), 1).astype(F32)
    east = column_of(east_ref[...].astype(F32))
    west = column_of(west_ref[...].astype(F32))
    east_hot = jnp.where(node == east, 1.0, 0.0).astype(BF16)
    west_hot = jnp.where(node == west, 1.0, 0.0).astype(BF16)
    spread = dot(link, east_hot, 0, 0).astype(BF16)
    edge_ref[0:slots, :] = spread
    edge_ref[slots : 2 * slots, :] = west_hot
    edges = edge_ref[...]
    scaled = (edges.astype(F32) * (1.0 / mass_ref[...])).astype(BF16)
    both = dot(scaled, edges, 1, 1).astype(BF16)
    to_east_ref[...] = both[:, 0:slots]
    to_west_ref[...] = both[:, slots:]


def unfold(place_ref, count, piece, coarse_ref):
    half = coarse_ref.shape[0] // count // 2

    def move(d, carry):
        values = piece(place_ref[d])
        at = pl.multiple_of(d * 2 * half, 2 * half)
        coarse_ref[pl.ds(at, half), :] = values[:, 0 : LANES // 2]
        coarse_ref[pl.ds(at + half, half), :] = values[:, LANES // 2 :]
        return carry

    lax.fori_loop(0, count, move, 0, unroll=min(count, 16))


def first_level(field, coarse_ref, inverse_ref, vectors_ref, dense_ref, edge_ref, react, mass, obs, active,
                z_ref, scaled_ref, level_ref):
    fix = dot(inverse_ref[...], coarse_ref[...]).astype(BF16)
    spread = dot(fix, vectors_ref[...], 0, 0)
    z = active * (field / (obs + react * react / mass) + spread)
    z_ref[...] = z
    w = z.astype(BF16)
    scaled = (dot(w, dense_ref[...]) + react * z) / mass
    scaled_ref[...] = scaled
    edges = edge_ref[...]
    level1 = dot(w, edges, 1, 1).astype(BF16)
    level2 = dot(scaled.astype(BF16), edges, 1, 1).astype(BF16)
    level_ref[...] = jnp.concatenate([level1, level2], axis=0)
    return z


def start_kernel(place_ref, count_ref, pieces_ref, inverse_ref, right_ref, vectors_ref, dense_ref, edge_ref,
                 react_ref, mass_ref, obs_ref, to_west_ref, to_east_ref,
                 z_ref, scaled_ref, west_msg_ref, east_msg_ref, far_west_ref, far_east_ref,
                 coarse_ref, level_ref):
    samples, nodes = right_ref.shape
    unfold(place_ref, pieces_ref.shape[0], lambda at: pieces_ref[at], coarse_ref)
    active = active_of(count_ref, nodes)
    first_level(active * right_ref[...].astype(F32), coarse_ref, inverse_ref, vectors_ref, dense_ref, edge_ref,
                react_ref[...], mass_ref[...], obs_ref[...], active, z_ref, scaled_ref, level_ref)
    slots = edge_ref.shape[0] // 2
    east_msg_ref[0 : 2 * samples, :] = level_ref[:, 0:slots]
    west_msg_ref[0 : 2 * samples, :] = level_ref[:, slots:]
    east_msg_ref[2 * samples :, :] = to_east_ref[...]
    west_msg_ref[2 * samples :, :] = to_west_ref[...]
    far_east_ref[...] = level_ref[0:samples, 0:slots]
    far_west_ref[...] = level_ref[0:samples, slots:]


def second_level(from_east_ref, from_west_ref, beyond_east_ref, beyond_west_ref, own_west_ref, own_east_ref,
                 corr_east, corr_west, z, scaled_ref, dense_ref, edge_ref, react, mass, obs, active):
    samples = z.shape[0]
    edges = edge_ref[...]
    arrived = jnp.concatenate([from_east_ref[0:samples, :], from_west_ref[0:samples, :]], axis=1)
    inner = scaled_ref[...] + dot(arrived, edges) / mass
    east_terms = jnp.concatenate([beyond_east_ref[...], own_east_ref[...]], axis=1)
    west_terms = jnp.concatenate([own_west_ref[...], beyond_west_ref[...]], axis=1)
    second_east = from_east_ref[samples : 2 * samples, :].astype(F32) + dot(east_terms, corr_east)
    second_west = from_west_ref[samples : 2 * samples, :].astype(F32) + dot(west_terms, corr_west)
    arrived2 = jnp.concatenate([second_east, second_west], axis=1).astype(BF16)
    image = dot(inner.astype(BF16), dense_ref[...]) + dot(arrived2, edges) + react * inner
    return active * (image + obs * z)


def image_kernel(count_ref, from_east_ref, from_west_ref, beyond_east_ref, beyond_west_ref, own_west_ref, own_east_ref,
                 z_ref, scaled_ref, dense_ref, edge_ref, react_ref, mass_ref, obs_ref, right_ref, vectors_ref,
                 image_ref, chunk_ref):
    samples, nodes = z_ref.shape
    active = active_of(count_ref, nodes)
    z = z_ref[...]
    image = second_level(from_east_ref, from_west_ref, beyond_east_ref, beyond_west_ref, own_west_ref, own_east_ref,
                         from_east_ref[2 * samples :, :], from_west_ref[2 * samples :, :], z, scaled_ref, dense_ref,
                         edge_ref, react_ref[...], mass_ref[...], obs_ref[...], active)
    image_ref[...] = image
    coarse = fold(dot(vectors_ref[...], image.astype(BF16), 1, 1))
    half = coarse.shape[0]
    sums = row_of(row_sum(active * right_ref[...].astype(F32), z), row_sum(z, image))
    chunk_ref[0:half, :] = coarse
    chunk_ref[half:, :] = jnp.broadcast_to(sums, (chunk_ref.shape[0] - half, LANES))


def middle_kernel(place_ref, count_ref, pieces_ref, second_ref, inverse_ref, right_ref, image_ref, vectors_ref,
                  dense_ref, edge_ref, react_ref, mass_ref, obs_ref,
                  z_ref, scaled_ref, west_msg_ref, east_msg_ref, far_west_ref, far_east_ref, sums_ref,
                  coarse_ref, level_ref):
    samples, nodes = right_ref.shape
    count, half, _ = pieces_ref.shape

    def add(d, total):
        return total + second_ref[d, half : half + 1, :]

    sums = lax.fori_loop(0, count, add, jnp.zeros((1, LANES), F32), unroll=min(count, 16))
    step = sums[:, 0 : LANES // 2] / sums[:, LANES // 2 :]
    step = jnp.concatenate([step, step], axis=1)

    def piece(at):
        return (pieces_ref[at].astype(F32) - step * second_ref[at, 0:half, :]).astype(BF16)

    unfold(place_ref, count, piece, coarse_ref)
    active = active_of(count_ref, nodes)
    residual = active * right_ref[...].astype(F32) - column_of(step)[0:samples] * image_ref[...]
    z = first_level(residual, coarse_ref, inverse_ref, vectors_ref, dense_ref, edge_ref,
                    react_ref[...], mass_ref[...], obs_ref[...], active, z_ref, scaled_ref, level_ref)
    slots = edge_ref.shape[0] // 2
    east_msg_ref[...] = level_ref[:, 0:slots]
    west_msg_ref[...] = level_ref[:, slots:]
    far_east_ref[...] = level_ref[0:samples, 0:slots]
    far_west_ref[...] = level_ref[0:samples, slots:]
    norm = row_sum(residual, z)
    row = lax.broadcasted_iota(jnp.int32, (8, LANES), 0)
    sums_ref[...] = jnp.where(row == 0, sums, jnp.where(row == 1, row_of(norm, norm), 0.0))


def last_kernel(count_ref, from_east_ref, from_west_ref, beyond_east_ref, beyond_west_ref, own_west_ref, own_east_ref,
                corr_east_ref, corr_west_ref, z_ref, scaled_ref, dense_ref, edge_ref, react_ref, mass_ref, obs_ref,
                first_image_ref, sums_ref, partial_ref):
    samples, nodes = z_ref.shape
    active = active_of(count_ref, nodes)
    z = z_ref[...]
    image = second_level(from_east_ref, from_west_ref, beyond_east_ref, beyond_west_ref, own_west_ref, own_east_ref,
                         corr_east_ref[2 * samples :, :], corr_west_ref[2 * samples :, :], z, scaled_ref, dense_ref,
                         edge_ref, react_ref[...], mass_ref[...], obs_ref[...], active)
    curves = row_of(row_sum(z, image), row_sum(z, first_image_ref[...]))
    row = lax.broadcasted_iota(jnp.int32, (8, LANES), 0)
    partial_ref[...] = jnp.where(row == 0, curves, jnp.where(row == 1, sums_ref[1:2, :], 0.0))


def finish_kernel(sums_ref, totals_ref, first_ref, second_ref, out_ref):
    samples = first_ref.shape[0]
    half = LANES // 2
    norm0, curve0 = sums_ref[0:1, 0:half], sums_ref[0:1, half:]
    curve, cross = totals_ref[0:1, 0:half], totals_ref[0:1, half:]
    norm1 = totals_ref[1:2, 0:half]
    beta = norm1 / norm0
    step0 = norm0 / curve0
    step1 = norm1 / (curve + beta * (2.0 * cross + beta * curve0))
    scales = column_of(jnp.concatenate([step0 + step1 * beta, step1], axis=1))
    out_ref[...] = scales[0:samples] * first_ref[...] + scales[samples : 2 * samples] * second_ref[...]


def shift(array, by):
    size = lax.axis_size("lon")
    return lax.ppermute(array, "lon", [(i, (i + by) % size) for i in range(size)])


def rounds():
    steps = []
    for axis in ("lon", "lat"):
        by = lax.axis_size(axis) // 2
        while by:
            steps.append((axis, by))
            by //= 2
    return steps


def swap(array, axis, by):
    return lax.ppermute(array, axis, [(i, i ^ by) for i in range(lax.axis_size(axis))])


def gather(chunk):
    pieces = chunk[None]
    for axis, by in rounds():
        pieces = jnp.concatenate([pieces, swap(pieces, axis, by)], axis=0)
    return pieces


def total(values):
    for axis, by in rounds():
        values = values + swap(values, axis, by)
    return values


def places():
    lats = lax.axis_size("lat")
    domains = lax.axis_size("lon") * lats
    me = lax.axis_index("lon") * lats + lax.axis_index("lat")
    apart = jnp.arange(domains, dtype=jnp.int32) ^ me
    place = jnp.zeros_like(apart)
    for i, (axis, by) in enumerate(rounds()):
        mask = by * lats if axis == "lon" else by
        place = place + jnp.where((apart & mask) != 0, 1 << i, 0)
    return place


def body(
    right_side,
    stiffness_blocks,
    block_pattern,
    reaction,
    lumped_mass,
    obs_precision,
    coupling,
    east_rows,
    west_rows,
    iface_count,
    node_count,
    deflation,
    coarse_inverse,
):
    samples, nodes = right_side.shape
    slots = coupling.shape[0]
    vectors = deflation.shape[0]
    domains = lax.axis_size("lon") * lax.axis_size("lat")
    half = vectors // 2
    react, mass, obs = reaction[None], lumped_mass[None], obs_precision[None]
    fields = [((samples, nodes), F32)] * 2
    far = [((samples, slots), BF16)] * 2
    coarse_scratch = pltpu.VMEM((domains * vectors, samples), BF16)
    level_scratch = pltpu.VMEM((2 * samples, 2 * slots), BF16)
    apply_cost = 2 * samples * nodes * nodes
    place = places()

    (chunk,) = call(coarse_kernel, [((half, LANES), BF16)], [SMEM, VMEM, VMEM],
                    (node_count, right_side, deflation), 2 * samples * vectors * nodes)
    edge, corr_west, corr_east = call(
        edge_kernel,
        [((2 * slots, nodes), BF16), ((2 * slots, slots), BF16), ((2 * slots, slots), BF16)],
        [SMEM, VMEM, VMEM, VMEM, VMEM],
        (iface_count, coupling, east_rows, west_rows, mass),
        8 * slots * slots * nodes,
    )
    (dense,) = call(dense_kernel, [((nodes, nodes), BF16)], [SMEM, VMEM], (block_pattern, stiffness_blocks),
                    apply_cost, [pltpu.VMEM((nodes, nodes), F32)])

    pieces = gather(chunk)
    z0, scaled, west_msg, east_msg, far_west, far_east = call(
        start_kernel,
        fields + [((2 * samples + 2 * slots, slots), BF16)] * 2 + far,
        [SMEM, SMEM] + [VMEM] * 11,
        (place, node_count, pieces, coarse_inverse, right_side, deflation, dense, edge, react, mass, obs,
         corr_west, corr_east),
        apply_cost,
        [coarse_scratch, level_scratch],
    )
    from_west = shift(east_msg, 1)
    from_east = shift(west_msg, -1)
    beyond_west = shift(far_east, 2)
    beyond_east = shift(far_west, -2)
    image, chunk = call(
        image_kernel,
        [((samples, nodes), F32), ((half + 8, LANES), F32)],
        [SMEM] + [VMEM] * 15,
        (node_count, from_east, from_west, beyond_east, beyond_west, far_west, far_east, z0, scaled, dense, edge,
         react, mass, obs, right_side, deflation),
        apply_cost,
    )
    second = gather(chunk)
    z1, scaled, west_msg, east_msg, far_west, far_east, sums = call(
        middle_kernel,
        fields + [((2 * samples, slots), BF16)] * 2 + far + [((8, LANES), F32)],
        [SMEM, SMEM] + [VMEM] * 11,
        (place, node_count, pieces, second, coarse_inverse, right_side, image, deflation, dense, edge, react, mass,
         obs),
        apply_cost,
        [coarse_scratch, level_scratch],
    )
    corr_from_east, corr_from_west = from_east, from_west
    from_west = shift(east_msg, 1)
    from_east = shift(west_msg, -1)
    beyond_west = shift(far_east, 2)
    beyond_east = shift(far_west, -2)
    (partial,) = call(
        last_kernel,
        [((8, LANES), F32)],
        [SMEM] + [VMEM] * 17,
        (node_count, from_east, from_west, beyond_east, beyond_west, far_west, far_east, corr_from_east,
         corr_from_west, z1, scaled, dense, edge, react, mass, obs, image, sums),
        apply_cost,
    )
    totals = total(partial)
    (out,) = call(finish_kernel, [((samples, nodes), F32)], [VMEM] * 4, (sums, totals, z0, z1), 4 * samples * nodes)
    return out


def solution(mesh):
    placed = (
        P(None, ("grp", "lon", "lat")),
        P(("grp", "lon", "lat"), None, None),
        P(("grp", "lon", "lat"), None),
        P(("grp", "lon", "lat")),
        P(("grp", "lon", "lat")),
        P(("grp", "lon", "lat")),
        P(("grp", "lon", "lat"), None),
        P(("grp", "lon", "lat"), None),
        P(("grp", "lon", "lat"), None),
        P(("grp", "lon", "lat")),
        P(("grp", "lon", "lat")),
        P(None, ("grp", "lon", "lat")),
        P(("grp", "lon", "lat"), None),
    )
    return jax.shard_map(
        body, mesh=mesh, in_specs=placed, out_specs=P(None, ("grp", "lon", "lat")), check_vma=False
    )
```

```python
import jax
import jax.numpy as jnp
import numpy as np
from jax import lax
from jax.experimental import pallas as pl
from jax.experimental.pallas import tpu as pltpu
from jax.sharding import PartitionSpec as P

F32 = jnp.float32
BF16 = jnp.bfloat16
VMEM = pl.BlockSpec(memory_space=pltpu.VMEM)
SMEM = pl.BlockSpec(memory_space=pltpu.SMEM)
HBM = pl.BlockSpec(memory_space=pltpu.HBM)
LANES = 128


def dot(a, b, ca=1, cb=0):
    return lax.dot_general(a, b, (((ca,), (cb,)), ((), ())), preferred_element_type=F32)


def call(kernel, outs, specs, args, flops, scratch=()):
    moved = sum(int(np.prod(a.shape)) * a.dtype.itemsize for a in args)
    return pl.pallas_call(
        kernel,
        out_shape=[jax.ShapeDtypeStruct(s, t) for s, t in outs],
        in_specs=specs,
        out_specs=[VMEM] * len(outs),
        scratch_shapes=list(scratch),
        compiler_params=pltpu.CompilerParams(vmem_limit_bytes=32 * 1024 * 1024),
        cost_estimate=pl.CostEstimate(flops=flops, bytes_accessed=moved, transcendentals=0),
    )(*args)


def active_of(count_ref, nodes):
    return (lax.broadcasted_iota(jnp.int32, (1, nodes), 1) < count_ref[0]).astype(F32)


def fold(values):
    half = values.shape[0] // 2
    return jnp.concatenate([values[:half], values[half:]], axis=1)


def column_of(row):
    return jnp.transpose(jnp.broadcast_to(row, (LANES, LANES)))[:, 0:1]


def row_of(first, second):
    both = jnp.concatenate([first, second], axis=0)
    return jnp.transpose(jnp.broadcast_to(both, (LANES, LANES)))[0:1]


def row_sum(first, second):
    return jnp.sum(first * second, axis=1, keepdims=True)


def coarse_kernel(count_ref, right_hbm, vectors_hbm, chunks_ref, right_ref, vectors_ref, sems):
    copies = [
        pltpu.make_async_copy(right_hbm, right_ref, sems.at[0]),
        pltpu.make_async_copy(vectors_hbm, vectors_ref, sems.at[1]),
    ]
    for copy in copies:
        copy.start()
    for copy in copies:
        copy.wait()
    active = active_of(count_ref, right_ref.shape[1]).astype(BF16)
    coarse = fold(dot(vectors_ref[...], right_ref[...] * active, 1, 1)).astype(BF16)
    chunks_ref[...] = jnp.broadcast_to(coarse[None], chunks_ref.shape)


def dense_kernel(pattern_ref, blocks_ref, dense_ref, total_ref):
    count, block, _ = blocks_ref.shape
    nodes = dense_ref.shape[0]

    def clear(i, carry):
        total_ref[pl.ds(pl.multiple_of(i * block, block), block), :] = jnp.zeros((block, nodes), F32)
        return carry

    lax.fori_loop(0, nodes // block, clear, 0)

    def place(k, carry):
        rows = pl.ds(pl.multiple_of(pattern_ref[k, 0] * block, block), block)
        cols = pl.ds(pl.multiple_of(pattern_ref[k, 1] * block, block), block)
        values = blocks_ref[k].astype(F32)
        total_ref[rows, cols] += values
        total_ref[cols, rows] += jnp.transpose(values)
        return carry

    lax.fori_loop(0, count, place, 0)

    def narrow(i, carry):
        rows = pl.ds(pl.multiple_of(i * block, block), block)
        dense_ref[rows, :] = total_ref[rows, :].astype(BF16)
        return carry

    lax.fori_loop(0, nodes // block, narrow, 0)


def edge_kernel(iface_ref, coupling_ref, east_ref, west_ref, mass_ref, edge_ref, to_west_ref, to_east_ref):
    slots = coupling_ref.shape[0]
    nodes = mass_ref.shape[1]
    live_a = lax.broadcasted_iota(jnp.int32, (slots, slots), 0) < iface_ref[0]
    live_b = lax.broadcasted_iota(jnp.int32, (slots, slots), 1) < iface_ref[0]
    link = jnp.where(live_a & live_b, coupling_ref[...], jnp.zeros((slots, slots), BF16))
    node = lax.broadcasted_iota(jnp.int32, (slots, nodes), 1).astype(F32)
    east = column_of(east_ref[...].astype(F32))
    west = column_of(west_ref[...].astype(F32))
    east_hot = jnp.where(node == east, 1.0, 0.0).astype(BF16)
    west_hot = jnp.where(node == west, 1.0, 0.0).astype(BF16)
    spread = dot(link, east_hot, 0, 0).astype(BF16)
    edge_ref[0:slots, :] = spread
    edge_ref[slots : 2 * slots, :] = west_hot
    edges = edge_ref[...]
    scaled = (edges.astype(F32) * (1.0 / mass_ref[...])).astype(BF16)
    both = dot(scaled, edges, 1, 1).astype(BF16)
    to_east_ref[...] = both[:, 0:slots]
    to_west_ref[...] = both[:, slots:]


def unfold(count, piece, coarse_ref):
    half = coarse_ref.shape[0] // count // 2

    def move(d, carry):
        values = piece(d)
        at = pl.multiple_of(d * 2 * half, 2 * half)
        coarse_ref[pl.ds(at, half), :] = values[:, 0 : LANES // 2]
        coarse_ref[pl.ds(at + half, half), :] = values[:, LANES // 2 :]
        return carry

    lax.fori_loop(0, count, move, 0, unroll=min(count, 16))


def smooth(field, coarse_ref, inverse_ref, vectors_ref, react, mass, obs, active):
    fix = dot(inverse_ref[...], coarse_ref[...]).astype(BF16)
    spread = dot(fix, vectors_ref[...], 0, 0)
    return active * (field / (obs + react * react / mass) + spread)


def start_kernel(at_ref, count_ref, pieces_ref, inverse_ref, right_ref, vectors_ref, dense_ref, edge_ref,
                 react_ref, mass_ref, obs_ref, to_west_ref, to_east_ref,
                 z_ref, scaled_ref, near_ref, across_ref, far_ref, beyond_ref, coarse_ref):
    samples, nodes = right_ref.shape
    unfold(pieces_ref.shape[0], lambda d: pieces_ref[d], coarse_ref)
    active = active_of(count_ref, nodes)
    react, mass = react_ref[...], mass_ref[...]
    z = smooth(active * right_ref[...].astype(F32), coarse_ref, inverse_ref, vectors_ref, react, mass, obs_ref[...],
               active)
    z_ref[...] = z
    w = z.astype(BF16)
    edges = edge_ref[...]
    scaled = (dot(w, dense_ref[...]) + react * z) / mass
    scaled_ref[...] = scaled
    level1 = dot(w, edges, 1, 1).astype(BF16)
    level2 = dot(scaled.astype(BF16), edges, 1, 1).astype(BF16)
    slots = edges.shape[0] // 2

    def send(east_ref, west_ref):
        for ref, cols, corr_ref in (
            (east_ref, slice(0, slots), to_east_ref),
            (west_ref, slice(slots, 2 * slots), to_west_ref),
        ):
            ref[0:samples, :] = level1[:, cols]
            ref[samples : 2 * samples, :] = level2[:, cols]
            ref[2 * samples :, :] = corr_ref[...]

    def send_far(east_ref, west_ref):
        east_ref[...] = level1[:, 0:slots]
        west_ref[...] = level1[:, slots:]

    pl.when(at_ref[0] == 0)(lambda: send(near_ref, across_ref))
    pl.when(at_ref[0] == 1)(lambda: send(across_ref, near_ref))
    pl.when(at_ref[1] == 0)(lambda: send_far(far_ref, beyond_ref))
    pl.when(at_ref[1] == 1)(lambda: send_far(beyond_ref, far_ref))


def pick(flag, first_ref, second_ref):
    first, second = first_ref[...].astype(F32), second_ref[...].astype(F32)
    keep = jnp.full((1, 1), flag, jnp.int32) == 0
    return jnp.where(keep, first, second).astype(BF16), jnp.where(keep, second, first).astype(BF16)


def image_kernel(at_ref, count_ref, near_ref, across_ref, far_ref, beyond_ref, own_far_ref, own_beyond_ref,
                 z_ref, scaled_ref, dense_ref, edge_ref, react_ref, mass_ref, obs_ref, right_ref, vectors_ref,
                 image_ref, chunks_ref):
    samples, nodes = z_ref.shape
    active = active_of(count_ref, nodes)
    z = z_ref[...]
    edges = edge_ref[...]
    from_east, from_west = pick(at_ref[0], near_ref, across_ref)
    beyond_east, beyond_west = pick(at_ref[1], far_ref, beyond_ref)
    own_east, own_west = pick(at_ref[1], own_far_ref, own_beyond_ref)
    arrived = jnp.concatenate([from_east[0:samples], from_west[0:samples]], axis=1)
    inner = scaled_ref[...] + dot(arrived, edges) / mass_ref[...]
    east_terms = jnp.concatenate([beyond_east, own_east], axis=1)
    west_terms = jnp.concatenate([own_west, beyond_west], axis=1)
    second_east = from_east[samples : 2 * samples].astype(F32) + dot(east_terms, from_east[2 * samples :])
    second_west = from_west[samples : 2 * samples].astype(F32) + dot(west_terms, from_west[2 * samples :])
    arrived2 = jnp.concatenate([second_east, second_west], axis=1).astype(BF16)
    stiff = dot(inner.astype(BF16), dense_ref[...]) + dot(arrived2, edges) + react_ref[...] * inner
    image = active * (stiff + obs_ref[...] * z)
    image_ref[...] = image
    coarse = fold(dot(vectors_ref[...], image.astype(BF16), 1, 1))
    half = coarse.shape[0]
    sums = row_of(row_sum(active * right_ref[...].astype(F32), z), row_sum(z, image))
    count, rows, _ = chunks_ref.shape
    chunks_ref[:, 0:half, :] = jnp.broadcast_to(coarse[None], (count, half, LANES))
    chunks_ref[:, half:, :] = jnp.broadcast_to(sums[None], (count, rows - half, LANES))


def middle_kernel(at_ref, count_ref, pieces_ref, second_ref, inverse_ref, right_ref, image_ref, vectors_ref,
                  dense_ref, edge_ref, react_ref, mass_ref, obs_ref,
                  z_ref, scaled_ref, near_ref, across_ref, sums_ref, coarse_ref):
    samples, nodes = right_ref.shape
    count, half, _ = pieces_ref.shape

    def add(d, total):
        return total + second_ref[d, half : half + 1, :]

    sums = lax.fori_loop(0, count, add, jnp.zeros((1, LANES), F32), unroll=min(count, 16))
    step = sums[:, 0 : LANES // 2] / sums[:, LANES // 2 :]
    step = jnp.concatenate([step, step], axis=1)

    def piece(d):
        return (pieces_ref[d].astype(F32) - step * second_ref[d, 0:half, :]).astype(BF16)

    unfold(count, piece, coarse_ref)
    active = active_of(count_ref, nodes)
    react, mass = react_ref[...], mass_ref[...]
    image = image_ref[...]
    residual = active * right_ref[...].astype(F32) - column_of(step)[0:samples] * image
    z = smooth(residual, coarse_ref, inverse_ref, vectors_ref, react, mass, obs_ref[...], active)
    z_ref[...] = z
    w = z.astype(BF16)
    level1 = dot(w, edge_ref[...], 1, 1).astype(BF16)
    slots = edge_ref.shape[0] // 2

    def send(east_ref, west_ref):
        east_ref[...] = level1[:, 0:slots]
        west_ref[...] = level1[:, slots:]

    pl.when(at_ref[0] == 0)(lambda: send(near_ref, across_ref))
    pl.when(at_ref[0] == 1)(lambda: send(across_ref, near_ref))
    scaled_ref[...] = dot(w, dense_ref[...]) + react * z
    products = row_of(row_sum(residual, z), row_sum(z, image))
    row = lax.broadcasted_iota(jnp.int32, (8, LANES), 0)
    sums_ref[...] = jnp.where(row == 0, products, sums)


def last_kernel(at_ref, near_ref, across_ref, z_ref, scaled_ref, edge_ref, mass_ref, obs_ref, sums_ref, chunks_ref):
    z = z_ref[...]
    from_east, from_west = pick(at_ref[0], near_ref, across_ref)
    stiff = scaled_ref[...] + dot(jnp.concatenate([from_east, from_west], axis=1), edge_ref[...])
    curve = jnp.sum(stiff * stiff / mass_ref[...] + obs_ref[...] * z * z, axis=1, keepdims=True)
    row = lax.broadcasted_iota(jnp.int32, (8, LANES), 0)
    chunk = jnp.where(row == 0, sums_ref[0:1, :], row_of(curve, curve))
    chunks_ref[...] = jnp.broadcast_to(chunk[None], chunks_ref.shape)


def finish_kernel(sums_ref, chunks_ref, first_ref, second_ref, out_ref):
    samples = first_ref.shape[0]
    half = LANES // 2
    totals = jnp.sum(chunks_ref[...], axis=0)
    norm0, curve0 = sums_ref[1:2, 0:half], sums_ref[1:2, half:]
    norm1, cross = totals[0:1, 0:half], totals[0:1, half:]
    curve = totals[1:2, 0:half]
    beta = norm1 / norm0
    step0 = norm0 / curve0
    step1 = norm1 / (curve + beta * (2.0 * cross + beta * curve0))
    scales = column_of(jnp.concatenate([step0 + step1 * beta, step1], axis=1))
    out_ref[...] = scales[0:samples] * first_ref[...] + scales[samples : 2 * samples] * second_ref[...]


def exchange(chunks):
    return lax.all_to_all(chunks, ("lon", "lat"), split_axis=0, concat_axis=0, tiled=True)


def swap(array, reach, inner):
    size = lax.axis_size("lon")
    pairs = []
    for i in range(size):
        up = (i // reach) % 2 == (0 if inner else 1)
        pairs.append((i, (i + (reach if up else -reach)) % size))
    return lax.ppermute(array, "lon", pairs)


def body(
    right_side,
    stiffness_blocks,
    block_pattern,
    reaction,
    lumped_mass,
    obs_precision,
    coupling,
    east_rows,
    west_rows,
    iface_count,
    node_count,
    deflation,
    coarse_inverse,
):
    samples, nodes = right_side.shape
    slots = coupling.shape[0]
    vectors = deflation.shape[0]
    domains = lax.axis_size("lon") * lax.axis_size("lat")
    half = vectors // 2
    react, mass, obs = reaction[None], lumped_mass[None], obs_precision[None]
    field = ((samples, nodes), F32)
    coarse_scratch = pltpu.VMEM((domains * vectors, samples), BF16)
    apply_cost = 2 * samples * nodes * nodes
    lon = lax.axis_index("lon")
    at = jnp.stack([lon % 2, (lon // 2) % 2]).astype(jnp.int32)

    (chunks,) = call(
        coarse_kernel,
        [((domains, half, LANES), BF16)],
        [SMEM, HBM, HBM],
        (node_count, right_side, deflation),
        2 * samples * vectors * nodes,
        [pltpu.VMEM((samples, nodes), BF16), pltpu.VMEM((vectors, nodes), BF16), pltpu.SemaphoreType.DMA((2,))],
    )
    edge, corr_west, corr_east = call(
        edge_kernel,
        [((2 * slots, nodes), BF16), ((2 * slots, slots), BF16), ((2 * slots, slots), BF16)],
        [SMEM, VMEM, VMEM, VMEM, VMEM],
        (iface_count, coupling, east_rows, west_rows, mass),
        8 * slots * slots * nodes,
    )
    (dense,) = call(dense_kernel, [((nodes, nodes), BF16)], [SMEM, VMEM], (block_pattern, stiffness_blocks),
                    apply_cost, [pltpu.VMEM((nodes, nodes), F32)])

    pieces = exchange(chunks)
    z0, scaled, near, across, far, beyond = call(
        start_kernel,
        [field] * 2 + [((2 * samples + 2 * slots, slots), BF16)] * 2 + [((samples, slots), BF16)] * 2,
        [SMEM, SMEM] + [VMEM] * 11,
        (at, node_count, pieces, coarse_inverse, right_side, deflation, dense, edge, react, mass, obs,
         corr_west, corr_east),
        apply_cost,
        [coarse_scratch],
    )
    across = swap(across, 1, False)
    got_beyond = swap(beyond, 2, False)
    got_far = swap(far, 2, True)
    near = swap(near, 1, True)
    image, chunks = call(
        image_kernel,
        [field, ((domains, half + 8, LANES), F32)],
        [SMEM, SMEM] + [VMEM] * 15,
        (at, node_count, near, across, got_far, got_beyond, far, beyond, z0, scaled, dense, edge,
         react, mass, obs, right_side, deflation),
        apply_cost,
    )
    second = exchange(chunks)
    z1, scaled, near, across, sums = call(
        middle_kernel,
        [field] * 2 + [((samples, slots), BF16)] * 2 + [((8, LANES), F32)],
        [SMEM, SMEM] + [VMEM] * 11,
        (at, node_count, pieces, second, coarse_inverse, right_side, image, deflation, dense, edge, react, mass, obs),
        apply_cost,
        [coarse_scratch],
    )
    across = swap(across, 1, False)
    near = swap(near, 1, True)
    (chunks,) = call(
        last_kernel,
        [((domains, 8, LANES), F32)],
        [SMEM] + [VMEM] * 8,
        (at, near, across, z1, scaled, edge, mass, obs, sums),
        apply_cost,
    )
    totals = exchange(chunks)
    (out,) = call(finish_kernel, [field], [VMEM] * 4, (sums, totals, z0, z1), 4 * samples * nodes)
    return out


def solution(mesh):
    placed = (
        P(None, ("grp", "lon", "lat")),
        P(("grp", "lon", "lat"), None, None),
        P(("grp", "lon", "lat"), None),
        P(("grp", "lon", "lat")),
        P(("grp", "lon", "lat")),
        P(("grp", "lon", "lat")),
        P(("grp", "lon", "lat"), None),
        P(("grp", "lon", "lat"), None),
        P(("grp", "lon", "lat"), None),
        P(("grp", "lon", "lat")),
        P(("grp", "lon", "lat")),
        P(None, ("grp", "lon", "lat")),
        P(("grp", "lon", "lat"), None),
    )
    return jax.shard_map(
        body, mesh=mesh, in_specs=placed, out_specs=P(None, ("grp", "lon", "lat")), check_vma=False
    )
```

```python
import jax
import jax.numpy as jnp
import numpy as np
from jax import lax
from jax.experimental import pallas as pl
from jax.experimental.pallas import tpu as pltpu
from jax.sharding import PartitionSpec as P

F32 = jnp.float32
BF16 = jnp.bfloat16
VMEM = pl.BlockSpec(memory_space=pltpu.VMEM)
SMEM = pl.BlockSpec(memory_space=pltpu.SMEM)
HBM = pl.BlockSpec(memory_space=pltpu.HBM)
LANES = 128


def dot(a, b, ca=1, cb=0):
    return lax.dot_general(a, b, (((ca,), (cb,)), ((), ())), preferred_element_type=F32)


def call(kernel, outs, specs, args, flops, scratch=(), limit=32):
    moved = sum(int(np.prod(a.shape)) * a.dtype.itemsize for a in args)
    return pl.pallas_call(
        kernel,
        out_shape=[jax.ShapeDtypeStruct(s, t) for s, t in outs],
        in_specs=specs,
        out_specs=[VMEM] * len(outs),
        scratch_shapes=list(scratch),
        compiler_params=pltpu.CompilerParams(vmem_limit_bytes=limit * 1024 * 1024),
        cost_estimate=pl.CostEstimate(flops=flops, bytes_accessed=moved, transcendentals=0),
    )(*args)


def active_of(count_ref, nodes):
    return (lax.broadcasted_iota(jnp.int32, (1, nodes), 1) < count_ref[0]).astype(F32)


def fold(values):
    half = values.shape[0] // 2
    return jnp.concatenate([values[:half], values[half:]], axis=1)


def column_of(row):
    return jnp.transpose(jnp.broadcast_to(row, (LANES, LANES)))[:, 0:1]


def row_of(first, second):
    both = jnp.concatenate([first, second], axis=0)
    return jnp.transpose(jnp.broadcast_to(both, (LANES, LANES)))[0:1]


def row_sum(first, second):
    return jnp.sum(first * second, axis=1, keepdims=True)


def coarse_kernel(count_ref, right_hbm, vectors_hbm, chunks_ref, right_ref, vectors_ref, sems):
    copies = [
        pltpu.make_async_copy(right_hbm, right_ref, sems.at[0]),
        pltpu.make_async_copy(vectors_hbm, vectors_ref, sems.at[1]),
    ]
    for copy in copies:
        copy.start()
    for copy in copies:
        copy.wait()
    active = active_of(count_ref, right_ref.shape[1]).astype(BF16)
    coarse = fold(dot(vectors_ref[...], right_ref[...] * active, 1, 1)).astype(BF16)
    chunks_ref[...] = jnp.broadcast_to(coarse[None], chunks_ref.shape)


def dense_kernel(pattern_ref, blocks_ref, dense_ref, total_ref):
    count, block, _ = blocks_ref.shape
    nodes = dense_ref.shape[0]
    unit = (
        lax.broadcasted_iota(jnp.int32, (block, block), 0) == lax.broadcasted_iota(jnp.int32, (block, block), 1)
    ).astype(F32).astype(BF16)

    def clear(i, carry):
        total_ref[pl.ds(pl.multiple_of(i * block, block), block), :] = jnp.zeros((block, nodes), F32)
        return carry

    lax.fori_loop(0, nodes // block, clear, 0)

    def place(k, carry):
        rows = pl.ds(pl.multiple_of(pattern_ref[k, 0] * block, block), block)
        cols = pl.ds(pl.multiple_of(pattern_ref[k, 1] * block, block), block)
        values = blocks_ref[k]
        total_ref[rows, cols] += values.astype(F32)
        total_ref[cols, rows] += dot(unit, values, 1, 1)
        return carry

    lax.fori_loop(0, count, place, 0, unroll=8)

    def narrow(i, carry):
        rows = pl.ds(pl.multiple_of(i * block, block), block)
        dense_ref[rows, :] = total_ref[rows, :].astype(BF16)
        return carry

    lax.fori_loop(0, nodes // block, narrow, 0)


def edge_kernel(iface_ref, coupling_ref, east_ref, west_ref, mass_ref, edge_ref, to_west_ref, to_east_ref):
    slots = coupling_ref.shape[0]
    nodes = mass_ref.shape[1]
    live_a = lax.broadcasted_iota(jnp.int32, (slots, slots), 0) < iface_ref[0]
    live_b = lax.broadcasted_iota(jnp.int32, (slots, slots), 1) < iface_ref[0]
    link = jnp.where(live_a & live_b, coupling_ref[...], jnp.zeros((slots, slots), BF16))
    node = lax.broadcasted_iota(jnp.int32, (slots, nodes), 1).astype(F32)
    east = column_of(east_ref[...].astype(F32))
    west = column_of(west_ref[...].astype(F32))
    east_hot = jnp.where(node == east, 1.0, 0.0).astype(BF16)
    west_hot = jnp.where(node == west, 1.0, 0.0).astype(BF16)
    spread = dot(link, east_hot, 0, 0).astype(BF16)
    edge_ref[0:slots, :] = spread
    edge_ref[slots : 2 * slots, :] = west_hot
    edges = edge_ref[...]
    scaled = (edges.astype(F32) * (1.0 / mass_ref[...])).astype(BF16)
    both = dot(scaled, edges, 1, 1).astype(BF16)
    to_east_ref[...] = both[:, 0:slots]
    to_west_ref[...] = both[:, slots:]


def unfold(lat, count, piece, coarse_ref):
    half = coarse_ref.shape[0] // count // 4

    def move(d, carry):
        for side in range(2):
            values = piece(side, d)
            at = pl.multiple_of((2 * d + (lat if side == 0 else 1 - lat)) * 2 * half, 2 * half)
            coarse_ref[pl.ds(at, half), :] = values[:, 0 : LANES // 2]
            coarse_ref[pl.ds(at + half, half), :] = values[:, LANES // 2 :]
        return carry

    lax.fori_loop(0, count, move, 0, unroll=min(count, 8))


def smooth(field, coarse_ref, inverse_ref, vectors_ref, react, mass, obs, active):
    fix = dot(inverse_ref[...], coarse_ref[...]).astype(BF16)
    spread = dot(fix, vectors_ref[...], 0, 0)
    return active * (field / (obs + react * react / mass) + spread)


def start_kernel(at_ref, count_ref, pieces_ref, others_ref, inverse_ref, right_ref, vectors_ref, dense_ref, edge_ref,
                 react_ref, mass_ref, obs_ref, to_west_ref, to_east_ref,
                 z_ref, scaled_ref, near_ref, across_ref, far_ref, beyond_ref, coarse_ref):
    samples, nodes = right_ref.shape
    unfold(at_ref[2], pieces_ref.shape[0], lambda side, d: (pieces_ref, others_ref)[side][d], coarse_ref)
    active = active_of(count_ref, nodes)
    react, mass = react_ref[...], mass_ref[...]
    z = smooth(active * right_ref[...].astype(F32), coarse_ref, inverse_ref, vectors_ref, react, mass, obs_ref[...],
               active)
    z_ref[...] = z
    w = z.astype(BF16)
    edges = edge_ref[...]
    scaled = (dot(w, dense_ref[...]) + react * z) / mass
    scaled_ref[...] = scaled
    level1 = dot(w, edges, 1, 1).astype(BF16)
    level2 = dot(scaled.astype(BF16), edges, 1, 1).astype(BF16)
    slots = edges.shape[0] // 2

    def send(east_ref, west_ref):
        for ref, cols, corr_ref in (
            (east_ref, slice(0, slots), to_east_ref),
            (west_ref, slice(slots, 2 * slots), to_west_ref),
        ):
            ref[0:samples, :] = level1[:, cols]
            ref[samples : 2 * samples, :] = level2[:, cols]
            ref[2 * samples :, :] = corr_ref[...]

    def send_far(east_ref, west_ref):
        east_ref[...] = level1[:, 0:slots]
        west_ref[...] = level1[:, slots:]

    pl.when(at_ref[0] == 0)(lambda: send(near_ref, across_ref))
    pl.when(at_ref[0] == 1)(lambda: send(across_ref, near_ref))
    pl.when(at_ref[1] == 0)(lambda: send_far(far_ref, beyond_ref))
    pl.when(at_ref[1] == 1)(lambda: send_far(beyond_ref, far_ref))


def pick(flag, first_ref, second_ref):
    first, second = first_ref[...].astype(F32), second_ref[...].astype(F32)
    keep = jnp.full((1, 1), flag, jnp.int32) == 0
    return jnp.where(keep, first, second).astype(BF16), jnp.where(keep, second, first).astype(BF16)


def image_kernel(at_ref, count_ref, across_ref, beyond_ref, near_ref, far_ref, own_far_ref, own_beyond_ref,
                 z_ref, scaled_ref, dense_ref, edge_ref, react_ref, mass_ref, obs_ref, right_ref, vectors_ref,
                 image_ref, chunks_ref):
    samples, nodes = z_ref.shape
    active = active_of(count_ref, nodes)
    z = z_ref[...]
    edges = edge_ref[...]
    from_east, from_west = pick(at_ref[0], near_ref, across_ref)
    beyond_east, beyond_west = pick(at_ref[1], far_ref, beyond_ref)
    own_east, own_west = pick(at_ref[1], own_far_ref, own_beyond_ref)
    arrived = jnp.concatenate([from_east[0:samples], from_west[0:samples]], axis=1)
    inner = scaled_ref[...] + dot(arrived, edges) / mass_ref[...]
    east_terms = jnp.concatenate([beyond_east, own_east], axis=1)
    west_terms = jnp.concatenate([own_west, beyond_west], axis=1)
    second_east = from_east[samples : 2 * samples].astype(F32) + dot(east_terms, from_east[2 * samples :])
    second_west = from_west[samples : 2 * samples].astype(F32) + dot(west_terms, from_west[2 * samples :])
    arrived2 = jnp.concatenate([second_east, second_west], axis=1).astype(BF16)
    stiff = dot(inner.astype(BF16), dense_ref[...]) + dot(arrived2, edges) + react_ref[...] * inner
    image = active * (stiff + obs_ref[...] * z)
    image_ref[...] = image
    coarse = fold(dot(vectors_ref[...], image.astype(BF16), 1, 1))
    half = coarse.shape[0]
    sums = row_of(row_sum(active * right_ref[...].astype(F32), z), row_sum(z, image))
    count, rows, _ = chunks_ref.shape
    chunks_ref[:, 0:half, :] = jnp.broadcast_to(coarse[None], (count, half, LANES))
    chunks_ref[:, half:, :] = jnp.broadcast_to(sums[None], (count, rows - half, LANES))


def middle_kernel(at_ref, count_ref, pieces_ref, others_ref, second_ref, second_others_ref, inverse_ref, right_ref, image_ref, vectors_ref,
                  dense_ref, edge_ref, react_ref, mass_ref, obs_ref,
                  z_ref, scaled_ref, near_ref, across_ref, sums_ref, coarse_ref):
    samples, nodes = right_ref.shape
    count, half, _ = pieces_ref.shape

    def add(d, total):
        return total + second_ref[d, half : half + 1, :] + second_others_ref[d, half : half + 1, :]

    sums = lax.fori_loop(0, count, add, jnp.zeros((1, LANES), F32), unroll=min(count, 8))
    step = sums[:, 0 : LANES // 2] / sums[:, LANES // 2 :]
    step = jnp.concatenate([step, step], axis=1)

    def piece(side, d):
        first, change = ((pieces_ref, second_ref), (others_ref, second_others_ref))[side]
        return (first[d].astype(F32) - step * change[d, 0:half, :]).astype(BF16)

    unfold(at_ref[2], count, piece, coarse_ref)
    active = active_of(count_ref, nodes)
    react, mass = react_ref[...], mass_ref[...]
    image = image_ref[...]
    residual = active * right_ref[...].astype(F32) - column_of(step)[0:samples] * image
    z = smooth(residual, coarse_ref, inverse_ref, vectors_ref, react, mass, obs_ref[...], active)
    z_ref[...] = z
    w = z.astype(BF16)
    level1 = dot(w, edge_ref[...], 1, 1).astype(BF16)
    slots = edge_ref.shape[0] // 2

    def send(east_ref, west_ref):
        east_ref[...] = level1[:, 0:slots]
        west_ref[...] = level1[:, slots:]

    pl.when(at_ref[0] == 0)(lambda: send(near_ref, across_ref))
    pl.when(at_ref[0] == 1)(lambda: send(across_ref, near_ref))
    scaled_ref[...] = dot(w, dense_ref[...]) + react * z
    products = row_of(row_sum(residual, z), row_sum(z, image))
    row = lax.broadcasted_iota(jnp.int32, (8, LANES), 0)
    sums_ref[...] = jnp.where(row == 0, products, sums)


def last_kernel(at_ref, across_ref, near_ref, z_ref, scaled_ref, edge_ref, mass_ref, obs_ref, sums_ref, chunks_ref):
    z = z_ref[...]
    from_east, from_west = pick(at_ref[0], near_ref, across_ref)
    stiff = scaled_ref[...] + dot(jnp.concatenate([from_east, from_west], axis=1), edge_ref[...])
    curve = jnp.sum(stiff * stiff / mass_ref[...] + obs_ref[...] * z * z, axis=1, keepdims=True)
    row = lax.broadcasted_iota(jnp.int32, (8, LANES), 0)
    chunk = jnp.where(row == 0, sums_ref[0:1, :], row_of(curve, curve))
    chunks_ref[...] = jnp.broadcast_to(chunk[None], chunks_ref.shape)


def finish_kernel(sums_ref, chunks_ref, others_ref, first_ref, second_ref, out_ref):
    samples = first_ref.shape[0]
    half = LANES // 2
    totals = jnp.sum(chunks_ref[...] + others_ref[...], axis=0)
    norm0, curve0 = sums_ref[1:2, 0:half], sums_ref[1:2, half:]
    norm1, cross = totals[0:1, 0:half], totals[0:1, half:]
    curve = totals[1:2, 0:half]
    beta = norm1 / norm0
    step0 = norm0 / curve0
    step1 = norm1 / (curve + beta * (2.0 * cross + beta * curve0))
    scales = column_of(jnp.concatenate([step0 + step1 * beta, step1], axis=1))
    out_ref[...] = scales[0:samples] * first_ref[...] + scales[samples : 2 * samples] * second_ref[...]


def exchange(chunks):
    return lax.all_to_all(chunks, "lon", split_axis=0, concat_axis=0, tiled=True)


def other_band(array):
    return lax.ppermute(array, "lat", [(0, 1), (1, 0)])


def swap(array, reach, inner):
    size = lax.axis_size("lon")
    pairs = []
    for i in range(size):
        up = (i // reach) % 2 == (0 if inner else 1)
        pairs.append((i, (i + (reach if up else -reach)) % size))
    return lax.ppermute(array, "lon", pairs)


def body(
    right_side,
    stiffness_blocks,
    block_pattern,
    reaction,
    lumped_mass,
    obs_precision,
    coupling,
    east_rows,
    west_rows,
    iface_count,
    node_count,
    deflation,
    coarse_inverse,
):
    samples, nodes = right_side.shape
    slots = coupling.shape[0]
    vectors = deflation.shape[0]
    sectors = lax.axis_size("lon")
    domains = sectors * lax.axis_size("lat")
    half = vectors // 2
    react, mass, obs = reaction[None], lumped_mass[None], obs_precision[None]
    field = ((samples, nodes), F32)
    coarse_scratch = pltpu.VMEM((domains * vectors, samples), BF16)
    apply_cost = 2 * samples * nodes * nodes
    lon = lax.axis_index("lon")
    at = jnp.stack([lon & 1, (lon >> 1) & 1, lax.axis_index("lat")]).astype(jnp.int32)

    (chunks,) = call(
        coarse_kernel,
        [((sectors, half, LANES), BF16)],
        [SMEM, HBM, HBM],
        (node_count, right_side, deflation),
        2 * samples * vectors * nodes,
        [pltpu.VMEM((samples, nodes), BF16), pltpu.VMEM((vectors, nodes), BF16), pltpu.SemaphoreType.DMA((2,))],
        64,
    )
    edge, corr_west, corr_east = call(
        edge_kernel,
        [((2 * slots, nodes), BF16), ((2 * slots, slots), BF16), ((2 * slots, slots), BF16)],
        [SMEM, VMEM, VMEM, VMEM, VMEM],
        (iface_count, coupling, east_rows, west_rows, mass),
        8 * slots * slots * nodes,
    )
    (dense,) = call(dense_kernel, [((nodes, nodes), BF16)], [SMEM, VMEM], (block_pattern, stiffness_blocks),
                    apply_cost, [pltpu.VMEM((nodes, nodes), F32)])

    pieces, dense, edge, corr_west, corr_east = lax.optimization_barrier(
        (exchange(chunks), dense, edge, corr_west, corr_east)
    )
    others = other_band(pieces)
    z0, scaled, near, across, far, beyond = call(
        start_kernel,
        [field] * 2 + [((2 * samples + 2 * slots, slots), BF16)] * 2 + [((samples, slots), BF16)] * 2,
        [SMEM, SMEM] + [VMEM] * 12,
        (at, node_count, pieces, others, coarse_inverse, right_side, deflation, dense, edge, react, mass, obs,
         corr_west, corr_east),
        apply_cost,
        [coarse_scratch],
    )
    across = swap(across, 1, False)
    got_beyond = swap(beyond, 2, False)
    got_far = swap(far, 2, True)
    near = swap(near, 1, True)
    image, chunks = call(
        image_kernel,
        [field, ((sectors, half + 8, LANES), F32)],
        [SMEM, SMEM] + [VMEM] * 15,
        (at, node_count, across, got_beyond, near, got_far, far, beyond, z0, scaled, dense, edge,
         react, mass, obs, right_side, deflation),
        apply_cost,
    )
    second = exchange(chunks)
    second_others = other_band(second)
    z1, scaled, near, across, sums = call(
        middle_kernel,
        [field] * 2 + [((samples, slots), BF16)] * 2 + [((8, LANES), F32)],
        [SMEM, SMEM] + [VMEM] * 13,
        (at, node_count, pieces, others, second, second_others, coarse_inverse, right_side, image, deflation, dense,
         edge, react, mass, obs),
        apply_cost,
        [coarse_scratch],
    )
    across = swap(across, 1, False)
    near = swap(near, 1, True)
    (chunks,) = call(
        last_kernel,
        [((sectors, 8, LANES), F32)],
        [SMEM] + [VMEM] * 8,
        (at, across, near, z1, scaled, edge, mass, obs, sums),
        apply_cost,
    )
    totals = exchange(chunks)
    other_totals = other_band(totals)
    (out,) = call(finish_kernel, [field], [VMEM] * 5, (sums, totals, other_totals, z0, z1), 4 * samples * nodes)
    return out


def solution(mesh):
    placed = (
        P(None, ("grp", "lon", "lat")),
        P(("grp", "lon", "lat"), None, None),
        P(("grp", "lon", "lat"), None),
        P(("grp", "lon", "lat")),
        P(("grp", "lon", "lat")),
        P(("grp", "lon", "lat")),
        P(("grp", "lon", "lat"), None),
        P(("grp", "lon", "lat"), None),
        P(("grp", "lon", "lat"), None),
        P(("grp", "lon", "lat")),
        P(("grp", "lon", "lat")),
        P(None, ("grp", "lon", "lat")),
        P(("grp", "lon", "lat"), None),
    )
    return jax.shard_map(
        body, mesh=mesh, in_specs=placed, out_specs=P(None, ("grp", "lon", "lat")), check_vma=False
    )
```

```python
import jax
import jax.numpy as jnp
import numpy as np
from jax import lax
from jax.experimental import pallas as pl
from jax.experimental.pallas import tpu as pltpu
from jax.sharding import PartitionSpec as P

F32 = jnp.float32
BF16 = jnp.bfloat16
VMEM = pl.BlockSpec(memory_space=pltpu.VMEM)
SMEM = pl.BlockSpec(memory_space=pltpu.SMEM)
HBM = pl.BlockSpec(memory_space=pltpu.HBM)
LANES = 128


def dot(a, b, ca=1, cb=0):
    return lax.dot_general(a, b, (((ca,), (cb,)), ((), ())), preferred_element_type=F32)


def call(kernel, outs, specs, args, flops, scratch=(), limit=32, placed=None):
    moved = sum(int(np.prod(a.shape)) * a.dtype.itemsize for a in args)
    return pl.pallas_call(
        kernel,
        out_shape=[jax.ShapeDtypeStruct(s, t) for s, t in outs],
        in_specs=specs,
        out_specs=[(placed or {}).get(i, VMEM) for i in range(len(outs))],
        scratch_shapes=list(scratch),
        compiler_params=pltpu.CompilerParams(vmem_limit_bytes=limit * 1024 * 1024),
        cost_estimate=pl.CostEstimate(flops=flops, bytes_accessed=moved, transcendentals=0),
    )(*args)


def active_of(count_ref, nodes):
    return (lax.broadcasted_iota(jnp.int32, (1, nodes), 1) < count_ref[0]).astype(F32)


def fold(values):
    half = values.shape[0] // 2
    return jnp.concatenate([values[:half], values[half:]], axis=1)


def column_of(row):
    return jnp.transpose(jnp.broadcast_to(row, (LANES, LANES)))[:, 0:1]


def row_of(first, second):
    both = jnp.concatenate([first, second], axis=0)
    return jnp.transpose(jnp.broadcast_to(both, (LANES, LANES)))[0:1]


def row_sum(first, second):
    return jnp.sum(first * second, axis=1, keepdims=True)


def levels(values, edges):
    return dot(values.astype(BF16), edges, 1, 1)


def prep_kernel(at_ref, count_hbm, iface_hbm, pattern_hbm, blocks_hbm, right_hbm, vectors_hbm, coupling_hbm, east_hbm,
                west_hbm, react_hbm, mass_hbm, obs_hbm, inverse_hbm,
                chunks_ref, dense_hbm, edge_ref, to_west_ref, to_east_ref, near_ref, across_ref,
                count_ref, iface_ref, pattern_ref, blocks_ref, right_ref, vectors_ref, coupling_ref, east_ref, west_ref,
                react_ref, mass_ref, obs_ref, inverse_ref, total_ref, dense_ref, in_sems, out_sems):
    pairs = (
        (blocks_hbm, blocks_ref), (right_hbm, right_ref), (vectors_hbm, vectors_ref), (coupling_hbm, coupling_ref),
        (count_hbm, count_ref), (iface_hbm, iface_ref), (pattern_hbm, pattern_ref), (east_hbm, east_ref),
        (west_hbm, west_ref), (react_hbm, react_ref), (mass_hbm, mass_ref), (obs_hbm, obs_ref),
        (inverse_hbm, inverse_ref),
    )
    copies = [pltpu.make_async_copy(src, dst, in_sems.at[i]) for i, (src, dst) in enumerate(pairs)]
    for copy in copies:
        copy.start()
    samples, nodes = right_ref.shape
    count, block, _ = blocks_ref.shape
    slots = coupling_ref.shape[0]
    strips = nodes // block

    def clear(i, carry):
        total_ref[pl.ds(pl.multiple_of(i * block, block), block), :] = jnp.zeros((block, nodes), F32)
        return carry

    lax.fori_loop(0, strips, clear, 0)
    for copy in copies:
        copy.wait()

    active = active_of(count_ref, nodes)
    right = active * right_ref[...].astype(F32)
    coarse = fold(dot(vectors_ref[...], right.astype(BF16), 1, 1)).astype(BF16)
    chunks_ref[...] = jnp.broadcast_to(coarse[None], chunks_ref.shape)

    unit = (
        lax.broadcasted_iota(jnp.int32, (block, block), 0) == lax.broadcasted_iota(jnp.int32, (block, block), 1)
    ).astype(F32).astype(BF16)

    def place(k, carry):
        rows = pl.ds(pl.multiple_of(pattern_ref[k, 0] * block, block), block)
        cols = pl.ds(pl.multiple_of(pattern_ref[k, 1] * block, block), block)
        values = blocks_ref[k]
        total_ref[rows, cols] += values.astype(F32)
        total_ref[cols, rows] += dot(unit, values, 1, 1)
        return carry

    lax.fori_loop(0, count, place, 0, unroll=8)

    def strip_copy(i):
        rows = pl.ds(pl.multiple_of(i * block, block), block)
        return pltpu.make_async_copy(dense_ref.at[rows, :], dense_hbm.at[rows, :], out_sems.at[i])

    def narrow(i, carry):
        rows = pl.ds(pl.multiple_of(i * block, block), block)
        dense_ref[rows, :] = total_ref[rows, :].astype(BF16)
        strip_copy(i).start()
        return carry

    lax.fori_loop(0, strips, narrow, 0)

    live_a = lax.broadcasted_iota(jnp.int32, (slots, slots), 0) < iface_ref[0]
    live_b = lax.broadcasted_iota(jnp.int32, (slots, slots), 1) < iface_ref[0]
    link = jnp.where(live_a & live_b, coupling_ref[...], jnp.zeros((slots, slots), BF16))
    node = lax.broadcasted_iota(jnp.int32, (slots, nodes), 1).astype(F32)
    east_hot = jnp.where(node == column_of(east_ref[...].astype(F32)), 1.0, 0.0).astype(BF16)
    west_hot = jnp.where(node == column_of(west_ref[...].astype(F32)), 1.0, 0.0).astype(BF16)
    spread = dot(link, east_hot, 0, 0).astype(BF16)
    edge_ref[0:slots, :] = spread
    edge_ref[slots : 2 * slots, :] = west_hot
    edges = jnp.concatenate([spread, west_hot], axis=0)
    react, mass = react_ref[...], mass_ref[...]
    scaled = (edges.astype(F32) * (1.0 / mass)).astype(BF16)
    both = dot(scaled, edges, 1, 1).astype(BF16)
    to_east_ref[...] = both[:, 0:slots]
    to_west_ref[...] = both[:, slots:]

    smooth_right = (right / (obs_ref[...] + react * react / mass)).astype(BF16)
    masked = vectors_ref[...] * active.astype(BF16)
    level = levels(jnp.concatenate([masked, smooth_right], axis=0), edges).astype(BF16)
    rows, width = inverse_ref.shape
    for ref in (near_ref, across_ref):
        for j in range(width // LANES):
            ref[j * rows : (j + 1) * rows, :] = inverse_ref[:, j * LANES : (j + 1) * LANES]

    def send(east_ref, west_ref):
        east_ref[width // LANES * rows :, :] = level[:, 0:slots]
        west_ref[width // LANES * rows :, :] = level[:, slots:]

    pl.when(at_ref[0] == 0)(lambda: send(near_ref, across_ref))
    pl.when(at_ref[0] == 1)(lambda: send(across_ref, near_ref))

    def finish(i, carry):
        strip_copy(i).wait()
        return carry

    lax.fori_loop(0, strips, finish, 0)


def unfold(lat, count, piece, coarse_ref):
    half = coarse_ref.shape[0] // count // 4

    def move(d, carry):
        for side in range(2):
            values = piece(side, d)
            at = pl.multiple_of((2 * d + (lat if side == 0 else 1 - lat)) * 2 * half, 2 * half)
            coarse_ref[pl.ds(at, half), :] = values[:, 0 : LANES // 2]
            coarse_ref[pl.ds(at + half, half), :] = values[:, LANES // 2 :]
        return carry

    lax.fori_loop(0, count, move, 0, unroll=min(count, 8))


def smooth(field, coarse_ref, inverse_ref, vectors_ref, react, mass, obs, active):
    fix = dot(inverse_ref[...], coarse_ref[...]).astype(BF16)
    spread = dot(fix, vectors_ref[...], 0, 0)
    return active * (field / (obs + react * react / mass) + spread)


def start_kernel(at_ref, count_ref, pieces_ref, others_ref, inverse_ref, right_ref, vectors_ref, dense_ref, edge_ref,
                 react_ref, mass_ref, obs_ref, to_west_ref, to_east_ref,
                 z_ref, scaled_ref, near_ref, across_ref, far_ref, beyond_ref, coarse_ref):
    samples, nodes = right_ref.shape
    unfold(at_ref[2], pieces_ref.shape[0], lambda side, d: (pieces_ref, others_ref)[side][d], coarse_ref)
    active = active_of(count_ref, nodes)
    react, mass = react_ref[...], mass_ref[...]
    z = smooth(active * right_ref[...].astype(F32), coarse_ref, inverse_ref, vectors_ref, react, mass, obs_ref[...],
               active)
    z_ref[...] = z
    w = z.astype(BF16)
    edges = edge_ref[...]
    scaled = (dot(w, dense_ref[...]) + react * z) / mass
    scaled_ref[...] = scaled
    level1 = dot(w, edges, 1, 1).astype(BF16)
    level2 = dot(scaled.astype(BF16), edges, 1, 1).astype(BF16)
    slots = edges.shape[0] // 2

    def send(east_ref, west_ref):
        for ref, cols, corr_ref in (
            (east_ref, slice(0, slots), to_east_ref),
            (west_ref, slice(slots, 2 * slots), to_west_ref),
        ):
            ref[0:samples, :] = level1[:, cols]
            ref[samples : 2 * samples, :] = level2[:, cols]
            ref[2 * samples :, :] = corr_ref[...]

    def send_far(east_ref, west_ref):
        east_ref[...] = level1[:, 0:slots]
        west_ref[...] = level1[:, slots:]

    pl.when(at_ref[0] == 0)(lambda: send(near_ref, across_ref))
    pl.when(at_ref[0] == 1)(lambda: send(across_ref, near_ref))
    pl.when(at_ref[1] == 0)(lambda: send_far(far_ref, beyond_ref))
    pl.when(at_ref[1] == 1)(lambda: send_far(beyond_ref, far_ref))


def pick(flag, first_ref, second_ref):
    first, second = first_ref[...].astype(F32), second_ref[...].astype(F32)
    keep = jnp.full((1, 1), flag, jnp.int32) == 0
    return jnp.where(keep, first, second).astype(BF16), jnp.where(keep, second, first).astype(BF16)


def image_kernel(at_ref, count_ref, across_ref, beyond_ref, near_ref, far_ref, own_far_ref, own_beyond_ref,
                 z_ref, scaled_ref, dense_ref, edge_ref, react_ref, mass_ref, obs_ref, right_ref, vectors_ref,
                 image_ref, chunks_ref, near_out_ref, across_out_ref):
    samples, nodes = z_ref.shape
    active = active_of(count_ref, nodes)
    z = z_ref[...]
    edges = edge_ref[...]
    from_east, from_west = pick(at_ref[0], near_ref, across_ref)
    beyond_east, beyond_west = pick(at_ref[1], far_ref, beyond_ref)
    own_east, own_west = pick(at_ref[1], own_far_ref, own_beyond_ref)
    arrived = jnp.concatenate([from_east[0:samples], from_west[0:samples]], axis=1)
    inner = scaled_ref[...] + dot(arrived, edges) / mass_ref[...]
    east_terms = jnp.concatenate([beyond_east, own_east], axis=1)
    west_terms = jnp.concatenate([own_west, beyond_west], axis=1)
    second_east = from_east[samples : 2 * samples].astype(F32) + dot(east_terms, from_east[2 * samples :])
    second_west = from_west[samples : 2 * samples].astype(F32) + dot(west_terms, from_west[2 * samples :])
    arrived2 = jnp.concatenate([second_east, second_west], axis=1).astype(BF16)
    react, mass, obs = react_ref[...], mass_ref[...], obs_ref[...]
    stiff = dot(inner.astype(BF16), dense_ref[...]) + dot(arrived2, edges) + react * inner
    image = active * (stiff + obs * z)
    image_ref[...] = image
    level = levels(image / (obs + react * react / mass), edges).astype(BF16)
    slots = edges.shape[0] // 2

    def send(east_ref, west_ref):
        east_ref[...] = level[:, 0:slots]
        west_ref[...] = level[:, slots:]

    pl.when(at_ref[0] == 0)(lambda: send(near_out_ref, across_out_ref))
    pl.when(at_ref[0] == 1)(lambda: send(across_out_ref, near_out_ref))
    coarse = fold(dot(vectors_ref[...], image.astype(BF16), 1, 1))
    half = coarse.shape[0]
    sums = row_of(row_sum(active * right_ref[...].astype(F32), z), row_sum(z, image))
    count, rows, _ = chunks_ref.shape
    chunks_ref[:, 0:half, :] = jnp.broadcast_to(coarse[None], (count, half, LANES))
    chunks_ref[:, half:, :] = jnp.broadcast_to(sums[None], (count, rows - half, LANES))


def middle_kernel(at_ref, count_ref, pieces_ref, others_ref, second_ref, second_others_ref, across_ref, near_ref,
                  across_first_ref, near_first_ref, inverse_ref, right_ref, image_ref, vectors_ref,
                  dense_ref, edge_ref, react_ref, mass_ref, obs_ref,
                  z_ref, sums_ref, chunks_ref, coarse_ref):
    samples, nodes = right_ref.shape
    count, half, _ = pieces_ref.shape

    def add(d, total):
        return total + second_ref[d, half : half + 1, :] + second_others_ref[d, half : half + 1, :]

    sums = lax.fori_loop(0, count, add, jnp.zeros((1, LANES), F32), unroll=min(count, 8))
    step = sums[:, 0 : LANES // 2] / sums[:, LANES // 2 :]
    step = jnp.concatenate([step, step], axis=1)

    def piece(side, d):
        first, change = ((pieces_ref, second_ref), (others_ref, second_others_ref))[side]
        return (first[d].astype(F32) - step * change[d, 0:half, :]).astype(BF16)

    unfold(at_ref[2], count, piece, coarse_ref)
    active = active_of(count_ref, nodes)
    react, mass, obs = react_ref[...], mass_ref[...], obs_ref[...]
    image = image_ref[...]
    edges = edge_ref[...]
    step_column = column_of(step)[0:samples]
    residual = active * right_ref[...].astype(F32) - step_column * image
    z = smooth(residual, coarse_ref, inverse_ref, vectors_ref, react, mass, obs, active)
    z_ref[...] = z

    def arriving(first_ref, change_ref):
        rows, width = inverse_ref.shape
        blocks = width // LANES
        inverse = jnp.concatenate([first_ref[j * rows : (j + 1) * rows, :] for j in range(blocks)], axis=1)
        fix = dot(inverse, coarse_ref[...]).astype(BF16)
        level = first_ref[blocks * rows :, :]
        smooth_level = level[rows:].astype(F32) - step_column * change_ref[...].astype(F32)
        return smooth_level + dot(fix, level[0:rows], 0, 0)

    from_near, from_across = arriving(near_first_ref, near_ref), arriving(across_first_ref, across_ref)
    keep = jnp.full((1, 1), at_ref[0], jnp.int32) == 0
    from_east = jnp.where(keep, from_near, from_across)
    from_west = jnp.where(keep, from_across, from_near)
    arrived = jnp.concatenate([from_east, from_west], axis=1).astype(BF16)
    stiff = dot(z.astype(BF16), dense_ref[...]) + react * z + dot(arrived, edges)
    curve = jnp.sum(stiff * stiff / mass + obs * z * z, axis=1, keepdims=True)
    products = row_of(row_sum(residual, z), row_sum(z, image))
    row = lax.broadcasted_iota(jnp.int32, (8, LANES), 0)
    chunk = jnp.where(row == 0, products, row_of(curve, curve))
    chunks_ref[...] = jnp.broadcast_to(chunk[None], chunks_ref.shape)
    sums_ref[...] = jnp.broadcast_to(sums, sums_ref.shape)


def finish_kernel(sums_ref, chunks_ref, first_ref, second_ref, out_ref):
    samples = first_ref.shape[0]
    half = LANES // 2
    totals = jnp.sum(chunks_ref[...], axis=0)
    norm0, curve0 = sums_ref[1:2, 0:half], sums_ref[1:2, half:]
    norm1, cross = totals[0:1, 0:half], totals[0:1, half:]
    curve = totals[1:2, 0:half]
    beta = norm1 / norm0
    step0 = norm0 / curve0
    step1 = norm1 / (curve + beta * (2.0 * cross + beta * curve0))
    scales = column_of(jnp.concatenate([step0 + step1 * beta, step1], axis=1))
    out_ref[...] = scales[0:samples] * first_ref[...] + scales[samples : 2 * samples] * second_ref[...]


def exchange(chunks, axes):
    return lax.all_to_all(chunks, axes, split_axis=0, concat_axis=0, tiled=True)


def other_band(array):
    return lax.ppermute(array, "lat", [(0, 1), (1, 0)])


def swap(array, reach, inner):
    size = lax.axis_size("lon")
    pairs = []
    for i in range(size):
        up = (i // reach) % 2 == (0 if inner else 1)
        pairs.append((i, (i + (reach if up else -reach)) % size))
    return lax.ppermute(array, "lon", pairs)


def body(
    right_side,
    stiffness_blocks,
    block_pattern,
    reaction,
    lumped_mass,
    obs_precision,
    coupling,
    east_rows,
    west_rows,
    iface_count,
    node_count,
    deflation,
    coarse_inverse,
):
    samples, nodes = right_side.shape
    slots = coupling.shape[0]
    vectors = deflation.shape[0]
    sectors = lax.axis_size("lon")
    domains = sectors * lax.axis_size("lat")
    half = vectors // 2
    react, mass, obs = reaction[None], lumped_mass[None], obs_precision[None]
    field = ((samples, nodes), F32)
    coarse_scratch = pltpu.VMEM((domains * vectors, samples), BF16)
    apply_cost = 2 * samples * nodes * nodes
    lon = lax.axis_index("lon")
    at = jnp.stack([lon & 1, (lon >> 1) & 1, lax.axis_index("lat")]).astype(jnp.int32)

    blocks = coarse_inverse.shape[1] // LANES
    static = ((blocks * vectors + vectors + samples, slots), BF16)
    corr = ((2 * slots, slots), BF16)
    inputs = (
        node_count, iface_count, block_pattern, stiffness_blocks, right_side, deflation, coupling, east_rows, west_rows,
        react, mass, obs, coarse_inverse,
    )
    small = 3
    landing = [
        pltpu.SMEM(a.shape, a.dtype) if i < small else pltpu.VMEM(a.shape, a.dtype) for i, a in enumerate(inputs)
    ]
    chunks, dense, edge, corr_west, corr_east, near_first, across_first = call(
        prep_kernel,
        [((sectors, half, LANES), BF16), ((nodes, nodes), BF16), ((2 * slots, nodes), BF16), corr, corr, static, static],
        [SMEM] + [HBM] * len(inputs),
        (at,) + inputs,
        apply_cost,
        landing + [
            pltpu.VMEM((nodes, nodes), F32),
            pltpu.VMEM((nodes, nodes), BF16),
            pltpu.SemaphoreType.DMA((len(inputs),)),
            pltpu.SemaphoreType.DMA((nodes // stiffness_blocks.shape[1],)),
        ],
        64,
        {1: HBM},
    )
    pieces = exchange(chunks, "lon")
    others = other_band(pieces)
    z0, scaled, near, across, far, beyond = call(
        start_kernel,
        [field] * 2 + [((2 * samples + 2 * slots, slots), BF16)] * 2 + [((samples, slots), BF16)] * 2,
        [SMEM, SMEM] + [VMEM] * 12,
        (at, node_count, pieces, others, coarse_inverse, right_side, deflation, dense, edge, react, mass, obs,
         corr_west, corr_east),
        apply_cost,
        [coarse_scratch],
    )
    across = swap(across, 1, False)
    got_beyond = swap(beyond, 2, False)
    near = swap(near, 1, True)
    got_far = swap(far, 2, True)
    across_first = swap(across_first, 1, False)
    near_first = swap(near_first, 1, True)
    image, chunks, near_change, across_change = call(
        image_kernel,
        [field, ((sectors, half + 8, LANES), F32)] + [((samples, slots), BF16)] * 2,
        [SMEM, SMEM] + [VMEM] * 15,
        (at, node_count, across, got_beyond, near, got_far, far, beyond, z0, scaled, dense, edge,
         react, mass, obs, right_side, deflation),
        apply_cost,
    )
    across_change = swap(across_change, 1, False)
    near_change = swap(near_change, 1, True)
    second = exchange(chunks, "lon")
    second_others = other_band(second)
    z1, sums, chunks = call(
        middle_kernel,
        [field, ((8, LANES), F32), ((domains, 8, LANES), F32)],
        [SMEM, SMEM] + [VMEM] * 17,
        (at, node_count, pieces, others, second, second_others, across_change, near_change, across_first, near_first,
         coarse_inverse, right_side, image, deflation, dense, edge, react, mass, obs),
        apply_cost,
        [coarse_scratch],
    )
    totals = exchange(chunks, ("lon", "lat"))
    (out,) = call(finish_kernel, [field], [VMEM] * 4, (sums, totals, z0, z1), 4 * samples * nodes)
    return out


def solution(mesh):
    placed = (
        P(None, ("grp", "lon", "lat")),
        P(("grp", "lon", "lat"), None, None),
        P(("grp", "lon", "lat"), None),
        P(("grp", "lon", "lat")),
        P(("grp", "lon", "lat")),
        P(("grp", "lon", "lat")),
        P(("grp", "lon", "lat"), None),
        P(("grp", "lon", "lat"), None),
        P(("grp", "lon", "lat"), None),
        P(("grp", "lon", "lat")),
        P(("grp", "lon", "lat")),
        P(None, ("grp", "lon", "lat")),
        P(("grp", "lon", "lat"), None),
    )
    return jax.shard_map(
        body, mesh=mesh, in_specs=placed, out_specs=P(None, ("grp", "lon", "lat")), check_vma=False
    )
```

```python
import jax
import jax.numpy as jnp
import numpy as np
from jax import lax
from jax.experimental import pallas as pl
from jax.experimental.pallas import tpu as pltpu
from jax.sharding import PartitionSpec as P

F32 = jnp.float32
BF16 = jnp.bfloat16
VMEM = pl.BlockSpec(memory_space=pltpu.VMEM)
HBM = pl.BlockSpec(memory_space=pltpu.HBM)
SMEM = pl.BlockSpec(memory_space=pltpu.SMEM)
LANES = 128


def dot(a, b, ca=1, cb=0):
    return lax.dot_general(a, b, (((ca,), (cb,)), ((), ())), preferred_element_type=F32)


def call(kernel, outs, specs, args, flops, scratch=(), keep=False):
    moved = sum(int(np.prod(a.shape)) * a.dtype.itemsize for a in args)
    return pl.pallas_call(
        kernel,
        out_shape=[pltpu.VMEM(s, t) if keep else jax.ShapeDtypeStruct(s, t) for s, t in outs],
        in_specs=specs,
        out_specs=[VMEM] * len(outs),
        scratch_shapes=list(scratch),
        compiler_params=pltpu.CompilerParams(vmem_limit_bytes=32 * 1024 * 1024),
        cost_estimate=pl.CostEstimate(flops=flops, bytes_accessed=moved, transcendentals=0),
    )(*args)


def fold(values):
    half = values.shape[0] // 2
    return jnp.concatenate([values[:half], values[half:]], axis=1)


def column_of(row):
    return jnp.transpose(jnp.broadcast_to(row, (LANES, LANES)))[:, 0:1]


def row_of(first, second):
    both = jnp.concatenate([first, second], axis=0)
    return jnp.transpose(jnp.broadcast_to(both, (LANES, LANES)))[0:1]


def row_sum(first, second):
    return jnp.sum(first * second, axis=1, keepdims=True)


def levels(values, edges):
    return dot(values.astype(BF16), edges, 1, 1)


def by_lon(shift_by, first_ref, second_ref, write):
    bit = (lax.axis_index("lon") >> shift_by) & 1
    pl.when(bit == 0)(lambda: write(first_ref, second_ref))
    pl.when(bit == 1)(lambda: write(second_ref, first_ref))


def pick(shift_by, first, second):
    bit = (lax.axis_index("lon") >> shift_by) & 1
    keep = jnp.full((1, 1), bit, jnp.int32) == 0
    first, second = first.astype(F32), second.astype(F32)
    return jnp.where(keep, first, second).astype(BF16), jnp.where(keep, second, first).astype(BF16)


def load_kernel(count_ref, right_hbm, vectors_hbm, react_hbm, mass_hbm, obs_hbm,
                coupling_hbm, blocks_hbm, east_hbm, west_hbm, inverse_hbm,
                chunks_ref, diag_ref, right_ref, vectors_ref, coupling_ref, blocks_ref, east_ref, west_ref,
                inverse_ref, react_ref, mass_ref, obs_ref, sems):
    pairs = (
        (right_hbm, right_ref), (vectors_hbm, vectors_ref), (react_hbm, react_ref), (mass_hbm, mass_ref),
        (obs_hbm, obs_ref), (coupling_hbm, coupling_ref), (blocks_hbm, blocks_ref), (east_hbm, east_ref),
        (west_hbm, west_ref), (inverse_hbm, inverse_ref),
    )
    copies = [pltpu.make_async_copy(src, dst, sems.at[i]) for i, (src, dst) in enumerate(pairs)]
    for copy in copies:
        copy.start()
    for copy in copies[:5]:
        copy.wait()
    nodes = right_ref.shape[1]
    active = (lax.broadcasted_iota(jnp.int32, (1, nodes), 1) < count_ref[0]).astype(F32)
    coarse = fold(dot(vectors_ref[...], right_ref[...] * active.astype(BF16), 1, 1)).astype(BF16)
    chunks_ref[...] = jnp.broadcast_to(coarse[None], chunks_ref.shape)
    react, mass, obs = react_ref[...], mass_ref[...], obs_ref[...]
    row = lax.broadcasted_iota(jnp.int32, (8, nodes), 0)
    diag = jnp.zeros((8, nodes), F32)
    for i, line in enumerate((active, react, 1.0 / mass, obs, 1.0 / (obs + react * react / mass))):
        diag = jnp.where(row == i, line, diag)
    diag_ref[...] = diag
    for copy in copies[5:]:
        copy.wait()


def lines(diag_ref):
    return tuple(diag_ref[i : i + 1, :] for i in range(5))


def prep_kernel(iface_ref, pattern_ref, blocks_ref, right_ref, vectors_ref, coupling_ref, east_ref, west_ref, diag_ref,
                inverse_ref, dense_ref, edge_ref, to_west_ref, to_east_ref, near_ref, across_ref, total_ref):
    samples, nodes = right_ref.shape
    count, block, _ = blocks_ref.shape
    slots = coupling_ref.shape[0]

    def clear(i, carry):
        total_ref[pl.ds(pl.multiple_of(i * block, block), block), :] = jnp.zeros((block, nodes), F32)
        return carry

    lax.fori_loop(0, nodes // block, clear, 0)
    unit = (
        lax.broadcasted_iota(jnp.int32, (block, block), 0) == lax.broadcasted_iota(jnp.int32, (block, block), 1)
    ).astype(F32).astype(BF16)

    def place(k, carry):
        rows = pl.ds(pl.multiple_of(pattern_ref[k, 0] * block, block), block)
        cols = pl.ds(pl.multiple_of(pattern_ref[k, 1] * block, block), block)
        values = blocks_ref[k]
        total_ref[rows, cols] += values.astype(F32)
        total_ref[cols, rows] += dot(unit, values, 1, 1)
        return carry

    lax.fori_loop(0, count, place, 0, unroll=8)

    def narrow(i, carry):
        rows = pl.ds(pl.multiple_of(i * block, block), block)
        dense_ref[rows, :] = total_ref[rows, :].astype(BF16)
        return carry

    lax.fori_loop(0, nodes // block, narrow, 0)

    active, react, inverse_mass, obs, jacobi = lines(diag_ref)
    node = lax.broadcasted_iota(jnp.int32, (slots, nodes), 1).astype(F32)
    east_hot = jnp.where(node == column_of(east_ref[...].astype(F32)), 1.0, 0.0).astype(BF16)
    west_hot = jnp.where(node == column_of(west_ref[...].astype(F32)), 1.0, 0.0).astype(BF16)
    live_a = lax.broadcasted_iota(jnp.int32, (slots, slots), 0) < iface_ref[0]
    live_b = lax.broadcasted_iota(jnp.int32, (slots, slots), 1) < iface_ref[0]
    link = jnp.where(live_a & live_b, coupling_ref[...], jnp.zeros((slots, slots), BF16))
    spread = dot(link, east_hot, 0, 0).astype(BF16)
    edge_ref[0:slots, :] = spread
    edge_ref[slots : 2 * slots, :] = west_hot
    edges = jnp.concatenate([spread, west_hot], axis=0)
    both = dot((edges.astype(F32) * inverse_mass).astype(BF16), edges, 1, 1).astype(BF16)
    to_east_ref[...] = both[:, 0:slots]
    to_west_ref[...] = both[:, slots:]

    masked = vectors_ref[...] * active.astype(BF16)
    smooth_right = (active * jacobi * right_ref[...].astype(F32)).astype(BF16)
    level = levels(jnp.concatenate([masked, smooth_right], axis=0), edges).astype(BF16)
    rows, width = inverse_ref.shape
    for ref in (near_ref, across_ref):
        for j in range(width // LANES):
            ref[j * rows : (j + 1) * rows, :] = inverse_ref[:, j * LANES : (j + 1) * LANES]

    def send(east_ref, west_ref):
        east_ref[width // LANES * rows :, :] = level[:, 0:slots]
        west_ref[width // LANES * rows :, :] = level[:, slots:]

    by_lon(0, near_ref, across_ref, send)


def unfold(count, piece, coarse_ref):
    half = coarse_ref.shape[0] // count // 4
    lat = lax.axis_index("lat")

    def move(d, carry):
        for side in range(2):
            values = piece(side, d)
            at = pl.multiple_of((2 * d + (lat if side == 0 else 1 - lat)) * 2 * half, 2 * half)
            coarse_ref[pl.ds(at, half), :] = values[:, 0 : LANES // 2]
            coarse_ref[pl.ds(at + half, half), :] = values[:, LANES // 2 :]
        return carry

    lax.fori_loop(0, count, move, 0, unroll=min(count, 8))


def smooth(field, coarse_ref, inverse_ref, vectors_ref, active, jacobi):
    fix = dot(inverse_ref[...], coarse_ref[...]).astype(BF16)
    return active * (field * jacobi + dot(fix, vectors_ref[...], 0, 0))


def start_kernel(pieces_ref, others_ref, inverse_ref, right_ref, vectors_ref, dense_ref, edge_ref, diag_ref,
                 to_west_ref, to_east_ref,
                 z_ref, scaled_ref, near_ref, across_ref, far_ref, beyond_ref, coarse_ref):
    samples, nodes = right_ref.shape
    unfold(pieces_ref.shape[0], lambda side, d: (pieces_ref, others_ref)[side][d], coarse_ref)
    active, react, inverse_mass, obs, jacobi = lines(diag_ref)
    z = smooth(right_ref[...].astype(F32), coarse_ref, inverse_ref, vectors_ref, active, jacobi)
    z_ref[...] = z
    edges = edge_ref[...]
    scaled = (dot(z.astype(BF16), dense_ref[...]) + react * z) * inverse_mass
    scaled_ref[...] = scaled
    level1 = levels(z, edges).astype(BF16)
    level2 = levels(scaled, edges).astype(BF16)
    slots = edges.shape[0] // 2

    def send(east_ref, west_ref):
        for ref, cols, corr_ref in (
            (east_ref, slice(0, slots), to_east_ref),
            (west_ref, slice(slots, 2 * slots), to_west_ref),
        ):
            ref[0:samples, :] = level1[:, cols]
            ref[samples : 2 * samples, :] = level2[:, cols]
            ref[2 * samples :, :] = corr_ref[...]

    def send_far(east_ref, west_ref):
        east_ref[...] = level1[:, 0:slots]
        west_ref[...] = level1[:, slots:]

    by_lon(0, near_ref, across_ref, send)
    by_lon(1, far_ref, beyond_ref, send_far)


def image_kernel(across_ref, beyond_ref, near_ref, far_ref, own_far_ref, own_beyond_ref,
                 z_ref, scaled_ref, dense_ref, edge_ref, diag_ref, right_ref, vectors_ref,
                 image_ref, chunks_ref, near_out_ref, across_out_ref):
    samples, nodes = z_ref.shape
    active, react, inverse_mass, obs, jacobi = lines(diag_ref)
    z = z_ref[...]
    edges = edge_ref[...]
    from_east, from_west = pick(0, near_ref[...], across_ref[...])
    beyond_east, beyond_west = pick(1, far_ref[...], beyond_ref[...])
    own_east, own_west = pick(1, own_far_ref[...], own_beyond_ref[...])
    arrived = jnp.concatenate([from_east[0:samples], from_west[0:samples]], axis=1)
    inner = scaled_ref[...] + dot(arrived, edges) * inverse_mass
    east_terms = jnp.concatenate([beyond_east, own_east], axis=1)
    west_terms = jnp.concatenate([own_west, beyond_west], axis=1)
    second_east = from_east[samples : 2 * samples].astype(F32) + dot(east_terms, from_east[2 * samples :])
    second_west = from_west[samples : 2 * samples].astype(F32) + dot(west_terms, from_west[2 * samples :])
    arrived2 = jnp.concatenate([second_east, second_west], axis=1).astype(BF16)
    stiff = dot(inner.astype(BF16), dense_ref[...]) + dot(arrived2, edges) + react * inner
    image = active * (stiff + obs * z)
    image_ref[...] = image
    level = levels(image * jacobi, edges).astype(BF16)
    slots = edges.shape[0] // 2

    def send(east_ref, west_ref):
        east_ref[...] = level[:, 0:slots]
        west_ref[...] = level[:, slots:]

    by_lon(0, near_out_ref, across_out_ref, send)
    coarse = fold(dot(vectors_ref[...], image.astype(BF16), 1, 1))
    half = coarse.shape[0]
    sums = row_of(row_sum(active * right_ref[...].astype(F32), z), row_sum(z, image))
    count, rows, _ = chunks_ref.shape
    chunks_ref[:, 0:half, :] = jnp.broadcast_to(coarse[None], (count, half, LANES))
    chunks_ref[:, half:, :] = jnp.broadcast_to(sums[None], (count, rows - half, LANES))


def middle_kernel(pieces_ref, others_ref, second_ref, second_others_ref, across_ref, near_ref,
                  across_first_ref, near_first_ref, inverse_ref, right_ref, image_ref, vectors_ref,
                  dense_ref, edge_ref, diag_ref, z_ref, sums_ref, chunks_ref, coarse_ref):
    samples, nodes = right_ref.shape
    count, half, _ = pieces_ref.shape

    def add(d, total):
        return total + second_ref[d, half : half + 1, :] + second_others_ref[d, half : half + 1, :]

    sums = lax.fori_loop(0, count, add, jnp.zeros((1, LANES), F32), unroll=min(count, 8))
    step = sums[:, 0 : LANES // 2] / sums[:, LANES // 2 :]
    step = jnp.concatenate([step, step], axis=1)

    def piece(side, d):
        first, change = ((pieces_ref, second_ref), (others_ref, second_others_ref))[side]
        return (first[d].astype(F32) - step * change[d, 0:half, :]).astype(BF16)

    unfold(count, piece, coarse_ref)
    active, react, inverse_mass, obs, jacobi = lines(diag_ref)
    image = image_ref[...]
    edges = edge_ref[...]
    step_column = column_of(step)[0:samples]
    residual = active * right_ref[...].astype(F32) - step_column * image
    z = smooth(residual, coarse_ref, inverse_ref, vectors_ref, active, jacobi)
    z_ref[...] = z

    def arriving(first_ref, change_ref):
        rows, width = inverse_ref.shape
        blocks = width // LANES
        inverse = jnp.concatenate([first_ref[j * rows : (j + 1) * rows, :] for j in range(blocks)], axis=1)
        fix = dot(inverse, coarse_ref[...]).astype(BF16)
        level = first_ref[blocks * rows :, :]
        smooth_level = level[rows:].astype(F32) - step_column * change_ref[...].astype(F32)
        return smooth_level + dot(fix, level[0:rows], 0, 0)

    from_east, from_west = pick(0, arriving(near_first_ref, near_ref), arriving(across_first_ref, across_ref))
    arrived = jnp.concatenate([from_east, from_west], axis=1)
    stiff = dot(z.astype(BF16), dense_ref[...]) + react * z + dot(arrived, edges)
    curve = jnp.sum(stiff * stiff * inverse_mass + obs * z * z, axis=1, keepdims=True)
    products = row_of(row_sum(residual, z), row_sum(z, image))
    row = lax.broadcasted_iota(jnp.int32, (8, LANES), 0)
    chunk = jnp.where(row == 0, products, row_of(curve, curve))
    chunks_ref[...] = jnp.broadcast_to(chunk[None], chunks_ref.shape)
    sums_ref[...] = jnp.broadcast_to(sums, sums_ref.shape)


def finish_kernel(sums_ref, chunks_ref, first_ref, second_ref, out_ref):
    samples = first_ref.shape[0]
    half = LANES // 2
    totals = jnp.sum(chunks_ref[...], axis=0)
    norm0, curve0 = sums_ref[1:2, 0:half], sums_ref[1:2, half:]
    norm1, cross = totals[0:1, 0:half], totals[0:1, half:]
    curve = totals[1:2, 0:half]
    beta = norm1 / norm0
    step0 = norm0 / curve0
    step1 = norm1 / (curve + beta * (2.0 * cross + beta * curve0))
    scales = column_of(jnp.concatenate([step0 + step1 * beta, step1], axis=1))
    out_ref[...] = scales[0:samples] * first_ref[...] + scales[samples : 2 * samples] * second_ref[...]


def exchange(chunks, axes):
    return lax.all_to_all(chunks, axes, split_axis=0, concat_axis=0, tiled=True)


def other_band(array):
    return lax.ppermute(array, "lat", [(0, 1), (1, 0)])


def swap(array, reach, inner):
    size = lax.axis_size("lon")
    pairs = []
    for i in range(size):
        up = (i // reach) % 2 == (0 if inner else 1)
        pairs.append((i, (i + (reach if up else -reach)) % size))
    return lax.ppermute(array, "lon", pairs)


def body(
    right_side,
    stiffness_blocks,
    block_pattern,
    reaction,
    lumped_mass,
    obs_precision,
    coupling,
    east_rows,
    west_rows,
    iface_count,
    node_count,
    deflation,
    coarse_inverse,
):
    samples, nodes = right_side.shape
    slots = coupling.shape[0]
    vectors = deflation.shape[0]
    sectors = lax.axis_size("lon")
    domains = sectors * lax.axis_size("lat")
    half = vectors // 2
    react, mass, obs = reaction[None], lumped_mass[None], obs_precision[None]
    field = ((samples, nodes), F32)
    coarse_scratch = pltpu.VMEM((domains * vectors, samples), BF16)
    apply_cost = 2 * samples * nodes * nodes
    blocks = coarse_inverse.shape[1] // LANES
    static = ((blocks * vectors + vectors + samples, slots), BF16)
    corr = ((2 * slots, slots), BF16)
    kept = (right_side, deflation, coupling, stiffness_blocks, east_rows, west_rows, coarse_inverse)
    inputs = (right_side, deflation, react, mass, obs, coupling, stiffness_blocks, east_rows, west_rows, coarse_inverse)
    line = pltpu.VMEM((1, nodes), F32)
    chunks, diag, right, basis, link, stored, east, west, inverse = call(
        load_kernel,
        [((sectors, half, LANES), BF16), ((8, nodes), F32)] + [(a.shape, a.dtype) for a in kept],
        [SMEM] + [HBM] * len(inputs),
        [node_count] + [pltpu.with_memory_space_constraint(a, pltpu.HBM) for a in inputs],
        2 * samples * vectors * nodes,
        [line, line, line, pltpu.SemaphoreType.DMA((len(inputs),))],
        keep=True,
    )
    dense, edge, corr_west, corr_east, near_first, across_first = call(
        prep_kernel,
        [((nodes, nodes), BF16), ((2 * slots, nodes), BF16), corr, corr, static, static],
        [SMEM, SMEM] + [VMEM] * 8,
        (iface_count, block_pattern, stored, right, basis, link, east, west, diag, inverse),
        apply_cost,
        [pltpu.VMEM((nodes, nodes), F32)],
        keep=True,
    )
    pieces, dense, edge, corr_west, corr_east, near_first, across_first = lax.optimization_barrier(
        (exchange(chunks, "lon"), dense, edge, corr_west, corr_east, near_first, across_first)
    )
    others = other_band(pieces)
    z0, scaled, near, across, far, beyond = call(
        start_kernel,
        [field] * 2 + [((2 * samples + 2 * slots, slots), BF16)] * 2 + [((samples, slots), BF16)] * 2,
        [VMEM] * 10,
        (pieces, others, inverse, right, basis, dense, edge, diag, corr_west, corr_east),
        apply_cost,
        [coarse_scratch],
    )
    across = swap(across, 1, False)
    got_beyond = swap(beyond, 2, False)
    near = swap(near, 1, True)
    got_far = swap(far, 2, True)
    across_first = swap(across_first, 1, False)
    near_first = swap(near_first, 1, True)
    image, chunks, near_change, across_change = call(
        image_kernel,
        [field, ((sectors, half + 8, LANES), F32)] + [((samples, slots), BF16)] * 2,
        [VMEM] * 13,
        (across, got_beyond, near, got_far, far, beyond, z0, scaled, dense, edge, diag, right, basis),
        apply_cost,
    )
    second, across_change, near_change, across_first, near_first = lax.optimization_barrier(
        (exchange(chunks, "lon"), swap(across_change, 1, False), swap(near_change, 1, True), across_first, near_first)
    )
    second_others = other_band(second)
    z1, sums, chunks = call(
        middle_kernel,
        [field, ((8, LANES), F32), ((domains, 8, LANES), F32)],
        [VMEM] * 15,
        (pieces, others, second, second_others, across_change, near_change, across_first, near_first,
         inverse, right, image, basis, dense, edge, diag),
        apply_cost,
        [coarse_scratch],
    )
    totals = exchange(chunks, ("lon", "lat"))
    (out,) = call(finish_kernel, [field], [VMEM] * 4, (sums, totals, z0, z1), 4 * samples * nodes)
    return out


def solution(mesh):
    placed = (
        P(None, ("grp", "lon", "lat")),
        P(("grp", "lon", "lat"), None, None),
        P(("grp", "lon", "lat"), None),
        P(("grp", "lon", "lat")),
        P(("grp", "lon", "lat")),
        P(("grp", "lon", "lat")),
        P(("grp", "lon", "lat"), None),
        P(("grp", "lon", "lat"), None),
        P(("grp", "lon", "lat"), None),
        P(("grp", "lon", "lat")),
        P(("grp", "lon", "lat")),
        P(None, ("grp", "lon", "lat")),
        P(("grp", "lon", "lat"), None),
    )
    return jax.shard_map(
        body, mesh=mesh, in_specs=placed, out_specs=P(None, ("grp", "lon", "lat")), check_vma=False
    )
```

```python
import jax
import jax.numpy as jnp
import numpy as np
from jax import lax
from jax.experimental import pallas as pl
from jax.experimental.pallas import tpu as pltpu
from jax.sharding import PartitionSpec as P

F32 = jnp.float32
BF16 = jnp.bfloat16
VMEM = pl.BlockSpec(memory_space=pltpu.VMEM)
HBM = pl.BlockSpec(memory_space=pltpu.HBM)
SMEM = pl.BlockSpec(memory_space=pltpu.SMEM)
LANES = 128


def dot(a, b, ca=1, cb=0):
    return lax.dot_general(a, b, (((ca,), (cb,)), ((), ())), preferred_element_type=F32)


def call(kernel, outs, specs, args, flops, scratch=(), keep=False):
    moved = sum(int(np.prod(a.shape)) * a.dtype.itemsize for a in args)
    return pl.pallas_call(
        kernel,
        out_shape=[pltpu.VMEM(s, t) if keep else jax.ShapeDtypeStruct(s, t) for s, t in outs],
        in_specs=specs,
        out_specs=[VMEM] * len(outs),
        scratch_shapes=list(scratch),
        compiler_params=pltpu.CompilerParams(vmem_limit_bytes=32 * 1024 * 1024),
        cost_estimate=pl.CostEstimate(flops=flops, bytes_accessed=moved, transcendentals=0),
    )(*args)


def fold(values):
    half = values.shape[0] // 2
    return jnp.concatenate([values[:half], values[half:]], axis=1)


def column_of(row):
    return jnp.transpose(jnp.broadcast_to(row, (LANES, LANES)))[:, 0:1]


def row_of(first, second):
    both = jnp.concatenate([first, second], axis=0)
    return jnp.transpose(jnp.broadcast_to(both, (LANES, LANES)))[0:1]


def row_sum(first, second):
    return jnp.sum(first * second, axis=1, keepdims=True)


def levels(values, edges):
    return dot(values.astype(BF16), edges, 1, 1)


def by_lon(shift_by, first_ref, second_ref, write):
    bit = (lax.axis_index("lon") >> shift_by) & 1
    pl.when(bit == 0)(lambda: write(first_ref, second_ref))
    pl.when(bit == 1)(lambda: write(second_ref, first_ref))


def pick(shift_by, first, second):
    bit = (lax.axis_index("lon") >> shift_by) & 1
    keep = jnp.full((1, 1), bit, jnp.int32) == 0
    first, second = first.astype(F32), second.astype(F32)
    return jnp.where(keep, first, second).astype(BF16), jnp.where(keep, second, first).astype(BF16)


def load_kernel(count_ref, right_hbm, vectors_hbm, react_hbm, mass_hbm, obs_hbm,
                coupling_hbm, blocks_hbm, east_hbm, west_hbm, inverse_hbm,
                chunks_ref, diag_ref, right_ref, vectors_ref, coupling_ref, blocks_ref, east_ref, west_ref,
                inverse_ref, react_ref, mass_ref, obs_ref, sems):
    pairs = (
        (right_hbm, right_ref), (vectors_hbm, vectors_ref), (react_hbm, react_ref), (mass_hbm, mass_ref),
        (obs_hbm, obs_ref), (coupling_hbm, coupling_ref), (blocks_hbm, blocks_ref), (east_hbm, east_ref),
        (west_hbm, west_ref), (inverse_hbm, inverse_ref),
    )
    copies = [pltpu.make_async_copy(src, dst, sems.at[i]) for i, (src, dst) in enumerate(pairs)]
    for copy in copies:
        copy.start()
    for copy in copies[:5]:
        copy.wait()
    nodes = right_ref.shape[1]
    active = (lax.broadcasted_iota(jnp.int32, (1, nodes), 1) < count_ref[0]).astype(F32)
    coarse = fold(dot(vectors_ref[...], right_ref[...] * active.astype(BF16), 1, 1)).astype(BF16)
    chunks_ref[...] = jnp.broadcast_to(coarse[None], chunks_ref.shape)
    react, mass, obs = react_ref[...], mass_ref[...], obs_ref[...]
    row = lax.broadcasted_iota(jnp.int32, (8, nodes), 0)
    diag = jnp.zeros((8, nodes), F32)
    for i, line in enumerate((active, react, 1.0 / mass, obs, 1.0 / (obs + react * react / mass))):
        diag = jnp.where(row == i, line, diag)
    diag_ref[...] = diag
    for copy in copies[5:]:
        copy.wait()


def lines(diag_ref):
    return tuple(diag_ref[i : i + 1, :] for i in range(5))


def prep_kernel(iface_ref, pattern_ref, blocks_ref, right_ref, vectors_ref, coupling_ref, east_ref, west_ref, diag_ref,
                inverse_ref, dense_ref, edge_ref, to_west_ref, to_east_ref, near_ref, across_ref, total_ref):
    samples, nodes = right_ref.shape
    count, block, _ = blocks_ref.shape
    slots = coupling_ref.shape[0]

    def clear(i, carry):
        total_ref[pl.ds(pl.multiple_of(i * block, block), block), :] = jnp.zeros((block, nodes), F32)
        return carry

    lax.fori_loop(0, nodes // block, clear, 0)
    unit = (
        lax.broadcasted_iota(jnp.int32, (block, block), 0) == lax.broadcasted_iota(jnp.int32, (block, block), 1)
    ).astype(F32).astype(BF16)

    def place(k, carry):
        rows = pl.ds(pl.multiple_of(pattern_ref[k, 0] * block, block), block)
        cols = pl.ds(pl.multiple_of(pattern_ref[k, 1] * block, block), block)
        values = blocks_ref[k]
        total_ref[rows, cols] += values.astype(F32)
        total_ref[cols, rows] += dot(unit, values, 1, 1)
        return carry

    lax.fori_loop(0, count, place, 0, unroll=8)

    def narrow(i, carry):
        rows = pl.ds(pl.multiple_of(i * block, block), block)
        dense_ref[rows, :] = total_ref[rows, :].astype(BF16)
        return carry

    lax.fori_loop(0, nodes // block, narrow, 0)

    active, react, inverse_mass, obs, jacobi = lines(diag_ref)
    node = lax.broadcasted_iota(jnp.int32, (slots, nodes), 1).astype(F32)
    east_hot = jnp.where(node == column_of(east_ref[...].astype(F32)), 1.0, 0.0).astype(BF16)
    west_hot = jnp.where(node == column_of(west_ref[...].astype(F32)), 1.0, 0.0).astype(BF16)
    live_a = lax.broadcasted_iota(jnp.int32, (slots, slots), 0) < iface_ref[0]
    live_b = lax.broadcasted_iota(jnp.int32, (slots, slots), 1) < iface_ref[0]
    link = jnp.where(live_a & live_b, coupling_ref[...], jnp.zeros((slots, slots), BF16))
    spread = dot(link, east_hot, 0, 0).astype(BF16)
    edge_ref[0:slots, :] = spread
    edge_ref[slots : 2 * slots, :] = west_hot
    edges = jnp.concatenate([spread, west_hot], axis=0)
    both = dot((edges.astype(F32) * inverse_mass).astype(BF16), edges, 1, 1).astype(BF16)
    to_east_ref[...] = both[:, 0:slots]
    to_west_ref[...] = both[:, slots:]

    masked = vectors_ref[...] * active.astype(BF16)
    smooth_right = (active * jacobi * right_ref[...].astype(F32)).astype(BF16)
    level = levels(jnp.concatenate([masked, smooth_right], axis=0), edges).astype(BF16)
    rows, width = inverse_ref.shape
    for ref in (near_ref, across_ref):
        for j in range(width // LANES):
            ref[j * rows : (j + 1) * rows, :] = inverse_ref[:, j * LANES : (j + 1) * LANES]

    def send(east_ref, west_ref):
        east_ref[width // LANES * rows :, :] = level[:, 0:slots]
        west_ref[width // LANES * rows :, :] = level[:, slots:]

    by_lon(0, near_ref, across_ref, send)


def unfold(count, piece, coarse_ref):
    half = coarse_ref.shape[0] // count // 4
    lat = lax.axis_index("lat")

    def move(d, carry):
        for side in range(2):
            values = piece(side, d)
            at = pl.multiple_of((2 * d + (lat if side == 0 else 1 - lat)) * 2 * half, 2 * half)
            coarse_ref[pl.ds(at, half), :] = values[:, 0 : LANES // 2]
            coarse_ref[pl.ds(at + half, half), :] = values[:, LANES // 2 :]
        return carry

    lax.fori_loop(0, count, move, 0, unroll=min(count, 8))


def smooth(field, coarse_ref, inverse_ref, vectors_ref, active, jacobi):
    fix = dot(inverse_ref[...], coarse_ref[...]).astype(BF16)
    return active * (field * jacobi + dot(fix, vectors_ref[...], 0, 0))


def start_kernel(pieces_ref, others_ref, inverse_ref, right_ref, vectors_ref, dense_ref, edge_ref, diag_ref,
                 to_west_ref, to_east_ref,
                 z_ref, scaled_ref, near_ref, across_ref, far_ref, beyond_ref, coarse_ref):
    samples, nodes = right_ref.shape
    unfold(pieces_ref.shape[0], lambda side, d: (pieces_ref, others_ref)[side][d], coarse_ref)
    active, react, inverse_mass, obs, jacobi = lines(diag_ref)
    z = smooth(right_ref[...].astype(F32), coarse_ref, inverse_ref, vectors_ref, active, jacobi)
    z_ref[...] = z
    edges = edge_ref[...]
    scaled = (dot(z.astype(BF16), dense_ref[...]) + react * z) * inverse_mass
    scaled_ref[...] = scaled
    level1 = levels(z, edges).astype(BF16)
    level2 = levels(scaled, edges).astype(BF16)
    slots = edges.shape[0] // 2

    def send(east_ref, west_ref):
        for ref, cols, corr_ref in (
            (east_ref, slice(0, slots), to_east_ref),
            (west_ref, slice(slots, 2 * slots), to_west_ref),
        ):
            ref[0:samples, :] = level1[:, cols]
            ref[samples : 2 * samples, :] = level2[:, cols]
            ref[2 * samples :, :] = corr_ref[...]

    def send_far(east_ref, west_ref):
        east_ref[...] = level1[:, 0:slots]
        west_ref[...] = level1[:, slots:]

    by_lon(0, near_ref, across_ref, send)
    by_lon(1, far_ref, beyond_ref, send_far)


def image_kernel(across_ref, beyond_ref, near_ref, far_ref, own_far_ref, own_beyond_ref,
                 z_ref, scaled_ref, dense_ref, edge_ref, diag_ref, right_ref, vectors_ref,
                 image_ref, chunks_ref, near_out_ref, across_out_ref):
    samples, nodes = z_ref.shape
    active, react, inverse_mass, obs, jacobi = lines(diag_ref)
    z = z_ref[...]
    edges = edge_ref[...]
    from_east, from_west = pick(0, near_ref[...], across_ref[...])
    beyond_east, beyond_west = pick(1, far_ref[...], beyond_ref[...])
    own_east, own_west = pick(1, own_far_ref[...], own_beyond_ref[...])
    arrived = jnp.concatenate([from_east[0:samples], from_west[0:samples]], axis=1)
    inner = scaled_ref[...] + dot(arrived, edges) * inverse_mass
    east_terms = jnp.concatenate([beyond_east, own_east], axis=1)
    west_terms = jnp.concatenate([own_west, beyond_west], axis=1)
    second_east = from_east[samples : 2 * samples].astype(F32) + dot(east_terms, from_east[2 * samples :])
    second_west = from_west[samples : 2 * samples].astype(F32) + dot(west_terms, from_west[2 * samples :])
    arrived2 = jnp.concatenate([second_east, second_west], axis=1).astype(BF16)
    stiff = dot(inner.astype(BF16), dense_ref[...]) + dot(arrived2, edges) + react * inner
    image = active * (stiff + obs * z)
    image_ref[...] = image
    level = levels(image * jacobi, edges).astype(BF16)
    slots = edges.shape[0] // 2

    def send(east_ref, west_ref):
        east_ref[...] = level[:, 0:slots]
        west_ref[...] = level[:, slots:]

    by_lon(0, near_out_ref, across_out_ref, send)
    coarse = fold(dot(vectors_ref[...], image.astype(BF16), 1, 1))
    half = coarse.shape[0]
    sums = row_of(row_sum(active * right_ref[...].astype(F32), z), row_sum(z, image))
    count, rows, _ = chunks_ref.shape
    chunks_ref[:, 0:half, :] = jnp.broadcast_to(coarse[None], (count, half, LANES))
    chunks_ref[:, half:, :] = jnp.broadcast_to(sums[None], (count, rows - half, LANES))


def middle_kernel(pieces_ref, others_ref, second_ref, second_others_ref, across_ref, near_ref,
                  across_first_ref, near_first_ref, inverse_ref, right_ref, image_ref, vectors_ref,
                  dense_ref, edge_ref, diag_ref, z_ref, sums_ref, chunks_ref, coarse_ref):
    samples, nodes = right_ref.shape
    count, half, _ = pieces_ref.shape

    def add(d, total):
        return total + second_ref[d, half : half + 1, :] + second_others_ref[d, half : half + 1, :]

    sums = lax.fori_loop(0, count, add, jnp.zeros((1, LANES), F32), unroll=min(count, 8))
    step = sums[:, 0 : LANES // 2] / sums[:, LANES // 2 :]
    step = jnp.concatenate([step, step], axis=1)

    def piece(side, d):
        first, change = ((pieces_ref, second_ref), (others_ref, second_others_ref))[side]
        return (first[d].astype(F32) - step * change[d, 0:half, :]).astype(BF16)

    unfold(count, piece, coarse_ref)
    active, react, inverse_mass, obs, jacobi = lines(diag_ref)
    image = image_ref[...]
    edges = edge_ref[...]
    step_column = column_of(step)[0:samples]
    residual = active * right_ref[...].astype(F32) - step_column * image
    z = smooth(residual, coarse_ref, inverse_ref, vectors_ref, active, jacobi)
    z_ref[...] = z

    def arriving(first_ref, change_ref):
        rows, width = inverse_ref.shape
        blocks = width // LANES
        inverse = jnp.concatenate([first_ref[j * rows : (j + 1) * rows, :] for j in range(blocks)], axis=1)
        fix = dot(inverse, coarse_ref[...]).astype(BF16)
        level = first_ref[blocks * rows :, :]
        smooth_level = level[rows:].astype(F32) - step_column * change_ref[...].astype(F32)
        return smooth_level + dot(fix, level[0:rows], 0, 0)

    from_east, from_west = pick(0, arriving(near_first_ref, near_ref), arriving(across_first_ref, across_ref))
    arrived = jnp.concatenate([from_east, from_west], axis=1)
    stiff = dot(z.astype(BF16), dense_ref[...]) + react * z + dot(arrived, edges)
    curve = jnp.sum(stiff * stiff * inverse_mass + obs * z * z, axis=1, keepdims=True)
    products = row_of(row_sum(residual, z), row_sum(z, image))
    row = lax.broadcasted_iota(jnp.int32, (8, LANES), 0)
    chunk = jnp.where(row == 0, products, row_of(curve, curve))
    chunks_ref[...] = jnp.broadcast_to(chunk[None], chunks_ref.shape)
    sums_ref[...] = jnp.broadcast_to(sums, sums_ref.shape)


def finish_kernel(sums_ref, chunks_ref, first_ref, second_ref, out_ref):
    samples = first_ref.shape[0]
    half = LANES // 2
    totals = jnp.sum(chunks_ref[...], axis=0)
    norm0, curve0 = sums_ref[1:2, 0:half], sums_ref[1:2, half:]
    norm1, cross = totals[0:1, 0:half], totals[0:1, half:]
    curve = totals[1:2, 0:half]
    beta = norm1 / norm0
    step0 = norm0 / curve0
    step1 = norm1 / (curve + beta * (2.0 * cross + beta * curve0))
    scales = column_of(jnp.concatenate([step0 + step1 * beta, step1], axis=1))
    out_ref[...] = scales[0:samples] * first_ref[...] + scales[samples : 2 * samples] * second_ref[...]


def exchange(chunks, axes):
    return lax.all_to_all(chunks, axes, split_axis=0, concat_axis=0, tiled=True)


def other_band(array):
    return lax.ppermute(array, "lat", [(0, 1), (1, 0)])


def swap(array, reach, inner):
    size = lax.axis_size("lon")
    pairs = []
    for i in range(size):
        up = (i // reach) % 2 == (0 if inner else 1)
        pairs.append((i, (i + (reach if up else -reach)) % size))
    return lax.ppermute(array, "lon", pairs)


def body(
    right_side,
    stiffness_blocks,
    block_pattern,
    reaction,
    lumped_mass,
    obs_precision,
    coupling,
    east_rows,
    west_rows,
    iface_count,
    node_count,
    deflation,
    coarse_inverse,
):
    samples, nodes = right_side.shape
    slots = coupling.shape[0]
    vectors = deflation.shape[0]
    sectors = lax.axis_size("lon")
    domains = sectors * lax.axis_size("lat")
    half = vectors // 2
    react, mass, obs = reaction[None], lumped_mass[None], obs_precision[None]
    field = ((samples, nodes), F32)
    coarse_scratch = pltpu.VMEM((domains * vectors, samples), BF16)
    apply_cost = 2 * samples * nodes * nodes
    blocks = coarse_inverse.shape[1] // LANES
    static = ((blocks * vectors + vectors + samples, slots), BF16)
    corr = ((2 * slots, slots), BF16)
    kept = (right_side, deflation, coupling, stiffness_blocks, east_rows, west_rows, coarse_inverse)
    inputs = (right_side, deflation, react, mass, obs, coupling, stiffness_blocks, east_rows, west_rows, coarse_inverse)
    line = pltpu.VMEM((1, nodes), F32)
    chunks, diag, right, basis, link, stored, east, west, inverse = call(
        load_kernel,
        [((sectors, half, LANES), BF16), ((8, nodes), F32)] + [(a.shape, a.dtype) for a in kept],
        [SMEM] + [HBM] * len(inputs),
        [node_count] + [pltpu.with_memory_space_constraint(a, pltpu.HBM) for a in inputs],
        2 * samples * vectors * nodes,
        [line, line, line, pltpu.SemaphoreType.DMA((len(inputs),))],
    )
    dense, edge, corr_west, corr_east, near_first, across_first = call(
        prep_kernel,
        [((nodes, nodes), BF16), ((2 * slots, nodes), BF16), corr, corr, static, static],
        [SMEM, SMEM] + [VMEM] * 8,
        (iface_count, block_pattern, stored, right, basis, link, east, west, diag, inverse),
        apply_cost,
        [pltpu.VMEM((nodes, nodes), F32)],
    )
    pieces, dense, edge, corr_west, corr_east, near_first, across_first = lax.optimization_barrier(
        (exchange(chunks, "lon"), dense, edge, corr_west, corr_east, near_first, across_first)
    )
    others = other_band(pieces)
    z0, scaled, near, across, far, beyond = call(
        start_kernel,
        [field] * 2 + [((2 * samples + 2 * slots, slots), BF16)] * 2 + [((samples, slots), BF16)] * 2,
        [VMEM] * 10,
        (pieces, others, inverse, right, basis, dense, edge, diag, corr_west, corr_east),
        apply_cost,
        [coarse_scratch],
    )
    across = swap(across, 1, False)
    got_beyond = swap(beyond, 2, False)
    near = swap(near, 1, True)
    got_far = swap(far, 2, True)
    across_first = swap(across_first, 1, False)
    near_first = swap(near_first, 1, True)
    image, chunks, near_change, across_change = call(
        image_kernel,
        [field, ((sectors, half + 8, LANES), F32)] + [((samples, slots), BF16)] * 2,
        [VMEM] * 13,
        (across, got_beyond, near, got_far, far, beyond, z0, scaled, dense, edge, diag, right, basis),
        apply_cost,
    )
    second, across_change, near_change, across_first, near_first = lax.optimization_barrier(
        (exchange(chunks, "lon"), swap(across_change, 1, False), swap(near_change, 1, True), across_first, near_first)
    )
    second_others = other_band(second)
    z1, sums, chunks = call(
        middle_kernel,
        [field, ((8, LANES), F32), ((domains, 8, LANES), F32)],
        [VMEM] * 15,
        (pieces, others, second, second_others, across_change, near_change, across_first, near_first,
         inverse, right, image, basis, dense, edge, diag),
        apply_cost,
        [coarse_scratch],
    )
    totals = exchange(chunks, ("lon", "lat"))
    (out,) = call(finish_kernel, [field], [VMEM] * 4, (sums, totals, z0, z1), 4 * samples * nodes)
    return out


def solution(mesh):
    placed = (
        P(None, ("grp", "lon", "lat")),
        P(("grp", "lon", "lat"), None, None),
        P(("grp", "lon", "lat"), None),
        P(("grp", "lon", "lat")),
        P(("grp", "lon", "lat")),
        P(("grp", "lon", "lat")),
        P(("grp", "lon", "lat"), None),
        P(("grp", "lon", "lat"), None),
        P(("grp", "lon", "lat"), None),
        P(("grp", "lon", "lat")),
        P(("grp", "lon", "lat")),
        P(None, ("grp", "lon", "lat")),
        P(("grp", "lon", "lat"), None),
    )
    return jax.shard_map(
        body, mesh=mesh, in_specs=placed, out_specs=P(None, ("grp", "lon", "lat")), check_vma=False
    )
```

```python
import jax
import jax.numpy as jnp
import numpy as np
from jax import lax
from jax.experimental import pallas as pl
from jax.experimental.pallas import tpu as pltpu
from jax.sharding import PartitionSpec as P

F32 = jnp.float32
BF16 = jnp.bfloat16
VMEM = pl.BlockSpec(memory_space=pltpu.VMEM)
HBM = pl.BlockSpec(memory_space=pltpu.HBM)
SMEM = pl.BlockSpec(memory_space=pltpu.SMEM)
LANES = 128
SUM_ROWS = 16


def dot(a, b, ca=1, cb=0):
    return lax.dot_general(a, b, (((ca,), (cb,)), ((), ())), preferred_element_type=F32)


def call(kernel, outs, specs, args, flops, scratch=()):
    moved = sum(int(np.prod(a.shape)) * a.dtype.itemsize for a in args)
    return pl.pallas_call(
        kernel,
        out_shape=[jax.ShapeDtypeStruct(s, t) for s, t in outs],
        in_specs=specs,
        out_specs=[VMEM] * len(outs),
        scratch_shapes=list(scratch),
        compiler_params=pltpu.CompilerParams(vmem_limit_bytes=32 * 1024 * 1024),
        cost_estimate=pl.CostEstimate(flops=flops, bytes_accessed=moved, transcendentals=0),
    )(*args)


def fold(values):
    half = values.shape[0] // 2
    return jnp.concatenate([values[:half], values[half:]], axis=1)


def column_of(row):
    return jnp.transpose(jnp.broadcast_to(row, (LANES, LANES)))[:, 0:1]


def row_of(first, second):
    both = jnp.concatenate([first, second], axis=0)
    return jnp.transpose(jnp.broadcast_to(both, (LANES, LANES)))[0:1]


def row_sum(first, second):
    return jnp.sum(first * second, axis=1, keepdims=True)


def levels(values, edges):
    return dot(values.astype(BF16), edges, 1, 1)


def by_lon(shift_by, first_ref, second_ref, write):
    bit = (lax.axis_index("lon") >> shift_by) & 1
    pl.when(bit == 0)(lambda: write(first_ref, second_ref))
    pl.when(bit == 1)(lambda: write(second_ref, first_ref))


def pick(shift_by, first, second):
    bit = (lax.axis_index("lon") >> shift_by) & 1
    keep = jnp.full((1, 1), bit, jnp.int32) == 0
    first, second = first.astype(F32), second.astype(F32)
    return jnp.where(keep, first, second).astype(BF16), jnp.where(keep, second, first).astype(BF16)


def load_kernel(count_ref, right_hbm, vectors_hbm, react_hbm, mass_hbm, obs_hbm,
                coupling_hbm, blocks_hbm, east_hbm, west_hbm, inverse_hbm,
                chunks_ref, diag_ref, link_ref, right_ref, vectors_ref, blocks_ref, east_ref, west_ref,
                inverse_ref, react_ref, mass_ref, obs_ref, coupling_ref, sems):
    pairs = (
        (right_hbm, right_ref), (vectors_hbm, vectors_ref), (react_hbm, react_ref), (mass_hbm, mass_ref),
        (obs_hbm, obs_ref), (coupling_hbm, coupling_ref), (blocks_hbm, blocks_ref), (east_hbm, east_ref),
        (west_hbm, west_ref), (inverse_hbm, inverse_ref),
    )
    copies = [pltpu.make_async_copy(src, dst, sems.at[i]) for i, (src, dst) in enumerate(pairs)]
    for copy in copies:
        copy.start()
    for copy in copies[:6]:
        copy.wait()
    nodes = right_ref.shape[1]
    active = (lax.broadcasted_iota(jnp.int32, (1, nodes), 1) < count_ref[0]).astype(F32)
    coarse = fold(dot(vectors_ref[...], right_ref[...] * active.astype(BF16), 1, 1)).astype(BF16)
    chunks_ref[...] = jnp.broadcast_to(coarse[None], chunks_ref.shape)
    react, mass, obs = react_ref[...], mass_ref[...], obs_ref[...]
    row = lax.broadcasted_iota(jnp.int32, (8, nodes), 0)
    diag = jnp.zeros((8, nodes), F32)
    for i, line in enumerate((active, react, 1.0 / mass, obs, 1.0 / (obs + react * react / mass))):
        diag = jnp.where(row == i, line, diag)
    diag_ref[...] = diag
    slots = coupling_ref.shape[0]
    live_a = lax.broadcasted_iota(jnp.int32, (slots, slots), 0) < count_ref[1]
    live_b = lax.broadcasted_iota(jnp.int32, (slots, slots), 1) < count_ref[1]
    link_ref[...] = jnp.where(live_a & live_b, coupling_ref[...], jnp.zeros((slots, slots), BF16))
    for copy in copies[6:]:
        copy.wait()


def lines(diag_ref):
    return tuple(diag_ref[i : i + 1, :] for i in range(5))


def prep_kernel(pattern_hbm, blocks_ref, right_ref, vectors_ref, link_ref, east_ref, west_ref, diag_ref, inverse_ref,
                dense_ref, edge_ref, to_west_ref, to_east_ref, near_ref, across_ref, pattern_ref, total_ref, sem):
    copy = pltpu.make_async_copy(pattern_hbm, pattern_ref, sem)
    copy.start()
    samples, nodes = right_ref.shape
    count, block, _ = blocks_ref.shape
    slots = link_ref.shape[0]

    def clear(i, carry):
        total_ref[pl.ds(pl.multiple_of(i * block, block), block), :] = jnp.zeros((block, nodes), F32)
        return carry

    lax.fori_loop(0, nodes // block, clear, 0)
    copy.wait()
    unit = (
        lax.broadcasted_iota(jnp.int32, (block, block), 0) == lax.broadcasted_iota(jnp.int32, (block, block), 1)
    ).astype(F32).astype(BF16)

    def place(k, carry):
        rows = pl.ds(pl.multiple_of(pattern_ref[0, k] * block, block), block)
        cols = pl.ds(pl.multiple_of(pattern_ref[1, k] * block, block), block)
        values = blocks_ref[k]
        total_ref[rows, cols] += values.astype(F32)
        total_ref[cols, rows] += dot(unit, values, 1, 1)
        return carry

    lax.fori_loop(0, count, place, 0, unroll=8)

    def narrow(i, carry):
        rows = pl.ds(pl.multiple_of(i * block, block), block)
        dense_ref[rows, :] = total_ref[rows, :].astype(BF16)
        return carry

    lax.fori_loop(0, nodes // block, narrow, 0)

    active, react, inverse_mass, obs, jacobi = lines(diag_ref)
    node = lax.broadcasted_iota(jnp.int32, (slots, nodes), 1).astype(F32)
    east_hot = jnp.where(node == column_of(east_ref[...].astype(F32)), 1.0, 0.0).astype(BF16)
    west_hot = jnp.where(node == column_of(west_ref[...].astype(F32)), 1.0, 0.0).astype(BF16)
    spread = dot(link_ref[...], east_hot, 0, 0).astype(BF16)
    edge_ref[0:slots, :] = spread
    edge_ref[slots : 2 * slots, :] = west_hot
    edges = jnp.concatenate([spread, west_hot], axis=0)
    both = dot((edges.astype(F32) * inverse_mass).astype(BF16), edges, 1, 1).astype(BF16)
    to_east_ref[...] = both[:, 0:slots]
    to_west_ref[...] = both[:, slots:]

    masked = vectors_ref[...] * active.astype(BF16)
    smooth_right = (active * jacobi * right_ref[...].astype(F32)).astype(BF16)
    level = levels(jnp.concatenate([masked, smooth_right], axis=0), edges).astype(BF16)
    rows, width = inverse_ref.shape
    for ref in (near_ref, across_ref):
        for j in range(width // LANES):
            ref[j * rows : (j + 1) * rows, :] = inverse_ref[:, j * LANES : (j + 1) * LANES]

    def send(east_ref, west_ref):
        east_ref[width // LANES * rows :, :] = level[:, 0:slots]
        west_ref[width // LANES * rows :, :] = level[:, slots:]

    by_lon(0, near_ref, across_ref, send)


def unfold(count, piece, coarse_ref):
    half = coarse_ref.shape[0] // count // 4
    lat = lax.axis_index("lat")

    def move(d, carry):
        for side in range(2):
            values = piece(side, d)
            at = pl.multiple_of((2 * d + (lat if side == 0 else 1 - lat)) * 2 * half, 2 * half)
            coarse_ref[pl.ds(at, half), :] = values[:, 0 : LANES // 2]
            coarse_ref[pl.ds(at + half, half), :] = values[:, LANES // 2 :]
        return carry

    lax.fori_loop(0, count, move, 0, unroll=min(count, 8))


def smooth(field, coarse_ref, inverse_ref, vectors_ref, active, jacobi):
    fix = dot(inverse_ref[...], coarse_ref[...]).astype(BF16)
    return active * (field * jacobi + dot(fix, vectors_ref[...], 0, 0))


def start_kernel(pieces_ref, others_ref, inverse_ref, right_ref, vectors_ref, dense_ref, edge_ref, diag_ref,
                 to_west_ref, to_east_ref,
                 z_ref, scaled_ref, near_ref, across_ref, far_ref, beyond_ref, coarse_ref):
    samples, nodes = right_ref.shape
    unfold(pieces_ref.shape[0], lambda side, d: (pieces_ref, others_ref)[side][d], coarse_ref)
    active, react, inverse_mass, obs, jacobi = lines(diag_ref)
    z = smooth(right_ref[...].astype(F32), coarse_ref, inverse_ref, vectors_ref, active, jacobi)
    z_ref[...] = z
    edges = edge_ref[...]
    scaled = (dot(z.astype(BF16), dense_ref[...]) + react * z) * inverse_mass
    scaled_ref[...] = scaled
    level1 = levels(z, edges).astype(BF16)
    level2 = levels(scaled, edges).astype(BF16)
    slots = edges.shape[0] // 2

    def send(east_ref, west_ref):
        for ref, cols, corr_ref in (
            (east_ref, slice(0, slots), to_east_ref),
            (west_ref, slice(slots, 2 * slots), to_west_ref),
        ):
            ref[0:samples, :] = level1[:, cols]
            ref[samples : 2 * samples, :] = level2[:, cols]
            ref[2 * samples :, :] = corr_ref[...]

    def send_far(east_ref, west_ref):
        east_ref[...] = level1[:, 0:slots]
        west_ref[...] = level1[:, slots:]

    by_lon(0, near_ref, across_ref, send)
    by_lon(1, far_ref, beyond_ref, send_far)


def image_kernel(across_ref, beyond_ref, near_ref, far_ref, own_far_ref, own_beyond_ref,
                 z_ref, scaled_ref, dense_ref, edge_ref, diag_ref, right_ref, vectors_ref,
                 image_ref, chunks_ref):
    samples, nodes = z_ref.shape
    active, react, inverse_mass, obs, jacobi = lines(diag_ref)
    z = z_ref[...]
    edges = edge_ref[...]
    from_east, from_west = pick(0, near_ref[...], across_ref[...])
    beyond_east, beyond_west = pick(1, far_ref[...], beyond_ref[...])
    own_east, own_west = pick(1, own_far_ref[...], own_beyond_ref[...])
    arrived = jnp.concatenate([from_east[0:samples], from_west[0:samples]], axis=1)
    inner = scaled_ref[...] + dot(arrived, edges) * inverse_mass
    east_terms = jnp.concatenate([beyond_east, own_east], axis=1)
    west_terms = jnp.concatenate([own_west, beyond_west], axis=1)
    second_east = from_east[samples : 2 * samples].astype(F32) + dot(east_terms, from_east[2 * samples :])
    second_west = from_west[samples : 2 * samples].astype(F32) + dot(west_terms, from_west[2 * samples :])
    arrived2 = jnp.concatenate([second_east, second_west], axis=1).astype(BF16)
    stiff = dot(inner.astype(BF16), dense_ref[...]) + dot(arrived2, edges) + react * inner
    image = active * (stiff + obs * z)
    image_ref[...] = image
    level = levels(image * jacobi, edges).astype(BF16)
    coarse = fold(dot(vectors_ref[...], image.astype(BF16), 1, 1))
    high = coarse.astype(BF16)
    low = (coarse - high.astype(F32)).astype(BF16)
    sums = row_of(row_sum(active * right_ref[...].astype(F32), z), row_sum(z, image))
    row = lax.broadcasted_iota(jnp.int32, (SUM_ROWS, LANES), 0)
    tail = jnp.zeros((SUM_ROWS, LANES), F32)
    for i in range(3):
        part = sums.astype(BF16).astype(F32)
        tail = jnp.where(row == i, part, tail)
        sums = sums - part
    count, rows, _ = chunks_ref.shape
    slots = level.shape[1] // 2
    common = jnp.concatenate([high, low, tail.astype(BF16), level[:, 0:slots]], axis=0)
    chunks_ref[...] = jnp.broadcast_to(common[None], chunks_ref.shape)
    before = lax.rem(lax.axis_index("lon") + count - 1, count)
    chunks_ref[before, rows - samples :, :] = level[:, slots:]


def middle_kernel(pieces_ref, others_ref, second_ref, second_others_ref,
                  across_first_ref, near_first_ref, inverse_ref, right_ref, image_ref, vectors_ref,
                  dense_ref, edge_ref, diag_ref, z_ref, sums_ref, chunks_ref, coarse_ref):
    samples, nodes = right_ref.shape
    count, half, _ = pieces_ref.shape
    tail = slice(2 * half, 2 * half + SUM_ROWS)

    def add(d, total):
        return total + second_ref[d, tail, :].astype(F32) + second_others_ref[d, tail, :].astype(F32)

    parts = lax.fori_loop(0, count, add, jnp.zeros((SUM_ROWS, LANES), F32), unroll=min(count, 8))
    sums = parts[2:3] + parts[1:2] + parts[0:1]
    step = sums[:, 0 : LANES // 2] / sums[:, LANES // 2 :]
    step = jnp.concatenate([step, step], axis=1)

    def piece(side, d):
        first, change = ((pieces_ref, second_ref), (others_ref, second_others_ref))[side]
        moved = change[d, 0:half, :].astype(F32) + change[d, half : 2 * half, :].astype(F32)
        return (first[d].astype(F32) - step * moved).astype(BF16)

    unfold(count, piece, coarse_ref)
    active, react, inverse_mass, obs, jacobi = lines(diag_ref)
    image = image_ref[...]
    edges = edge_ref[...]
    step_column = column_of(step)[0:samples]
    residual = active * right_ref[...].astype(F32) - step_column * image
    z = smooth(residual, coarse_ref, inverse_ref, vectors_ref, active, jacobi)
    z_ref[...] = z

    def arriving(first, change):
        rows, width = inverse_ref.shape
        blocks = width // LANES
        inverse = jnp.concatenate([first[j * rows : (j + 1) * rows] for j in range(blocks)], axis=1)
        fix = dot(inverse, coarse_ref[...]).astype(BF16)
        level = first[blocks * rows :]
        smooth_level = level[rows:].astype(F32) - step_column * change.astype(F32)
        return (smooth_level + dot(fix, level[0:rows], 0, 0)).astype(BF16)

    lon = lax.axis_index("lon")
    ahead, before = lax.rem(lon + 1, count), lax.rem(lon + count - 1, count)
    east_first, west_first = pick(0, near_first_ref[...], across_first_ref[...])
    from_east = arriving(east_first, second_ref[ahead, 2 * half + SUM_ROWS :, :])
    from_west = arriving(west_first, second_ref[before, 2 * half + SUM_ROWS :, :])
    arrived = jnp.concatenate([from_east, from_west], axis=1)
    stiff = dot(z.astype(BF16), dense_ref[...]) + react * z + dot(arrived, edges)
    curve = jnp.sum(stiff * stiff * inverse_mass + obs * z * z, axis=1, keepdims=True)
    products = row_of(row_sum(residual, z), row_sum(z, image))
    row = lax.broadcasted_iota(jnp.int32, (8, LANES), 0)
    chunk = jnp.where(row == 0, products, row_of(curve, curve))
    chunks_ref[...] = jnp.broadcast_to(chunk[None], chunks_ref.shape)
    sums_ref[...] = jnp.broadcast_to(sums, sums_ref.shape)


def finish_kernel(sums_ref, chunks_ref, first_ref, second_ref, out_ref):
    samples = first_ref.shape[0]
    half = LANES // 2
    totals = jnp.sum(chunks_ref[...], axis=0)
    norm0, curve0 = sums_ref[1:2, 0:half], sums_ref[1:2, half:]
    norm1, cross = totals[0:1, 0:half], totals[0:1, half:]
    curve = totals[1:2, 0:half]
    beta = norm1 / norm0
    step0 = norm0 / curve0
    step1 = norm1 / (curve + beta * (2.0 * cross + beta * curve0))
    scales = column_of(jnp.concatenate([step0 + step1 * beta, step1], axis=1))
    out_ref[...] = scales[0:samples] * first_ref[...] + scales[samples : 2 * samples] * second_ref[...]


def exchange(chunks, axes):
    return lax.all_to_all(chunks, axes, split_axis=0, concat_axis=0, tiled=True)


def other_band(array):
    return lax.ppermute(array, "lat", [(0, 1), (1, 0)])


def swap(array, reach, inner):
    size = lax.axis_size("lon")
    pairs = []
    for i in range(size):
        up = (i // reach) % 2 == (0 if inner else 1)
        pairs.append((i, (i + (reach if up else -reach)) % size))
    return lax.ppermute(array, "lon", pairs)


def body(
    right_side,
    stiffness_blocks,
    block_pattern,
    reaction,
    lumped_mass,
    obs_precision,
    coupling,
    east_rows,
    west_rows,
    iface_count,
    node_count,
    deflation,
    coarse_inverse,
):
    samples, nodes = right_side.shape
    slots = coupling.shape[0]
    vectors = deflation.shape[0]
    sectors = lax.axis_size("lon")
    domains = sectors * lax.axis_size("lat")
    half = vectors // 2
    react, mass, obs = reaction[None], lumped_mass[None], obs_precision[None]
    field = ((samples, nodes), F32)
    coarse_scratch = pltpu.VMEM((domains * vectors, samples), BF16)
    apply_cost = 2 * samples * nodes * nodes
    blocks = coarse_inverse.shape[1] // LANES
    static = ((blocks * vectors + vectors + samples, slots), BF16)
    corr = ((2 * slots, slots), BF16)
    kept = (right_side, deflation, stiffness_blocks, east_rows, west_rows, coarse_inverse)
    inputs = (right_side, deflation, react, mass, obs, coupling, stiffness_blocks, east_rows, west_rows, coarse_inverse)
    line = pltpu.VMEM((1, nodes), F32)
    chunks, diag, link, right, basis, stored, east, west, inverse = call(
        load_kernel,
        [((sectors, half, LANES), BF16), ((8, nodes), F32), (coupling.shape, BF16)] + [(a.shape, a.dtype) for a in kept],
        [SMEM] + [HBM] * len(inputs),
        [jnp.concatenate([node_count, iface_count])] + [pltpu.with_memory_space_constraint(a, pltpu.HBM) for a in inputs],
        2 * samples * vectors * nodes,
        [line, line, line, pltpu.VMEM(coupling.shape, BF16), pltpu.SemaphoreType.DMA((len(inputs),))],
    )
    pieces, stored = lax.optimization_barrier((exchange(chunks, "lon"), stored))
    pattern = pltpu.with_memory_space_constraint(block_pattern.T, pltpu.HBM)
    dense, edge, corr_west, corr_east, near_first, across_first = call(
        prep_kernel,
        [((nodes, nodes), BF16), ((2 * slots, nodes), BF16), corr, corr, static, static],
        [HBM] + [VMEM] * 8,
        (pattern, stored, right, basis, link, east, west, diag, inverse),
        apply_cost,
        [pltpu.SMEM((2, block_pattern.shape[0]), jnp.int32), pltpu.VMEM((nodes, nodes), F32), pltpu.SemaphoreType.DMA],
    )
    others = other_band(pieces)
    z0, scaled, near, across, far, beyond = call(
        start_kernel,
        [field] * 2 + [((2 * samples + 2 * slots, slots), BF16)] * 2 + [((samples, slots), BF16)] * 2,
        [VMEM] * 10,
        (pieces, others, inverse, right, basis, dense, edge, diag, corr_west, corr_east),
        apply_cost,
        [coarse_scratch],
    )
    across = swap(across, 1, False)
    got_beyond = swap(beyond, 2, False)
    near = swap(near, 1, True)
    got_far = swap(far, 2, True)
    across_first = swap(across_first, 1, False)
    near_first = swap(near_first, 1, True)
    image, chunks = call(
        image_kernel,
        [field, ((sectors, 2 * half + SUM_ROWS + samples, LANES), BF16)],
        [VMEM] * 13,
        (across, got_beyond, near, got_far, far, beyond, z0, scaled, dense, edge, diag, right, basis),
        apply_cost,
    )
    chunks, across_first, near_first = lax.optimization_barrier((chunks, across_first, near_first))
    second = exchange(chunks, "lon")
    second_others = other_band(second)
    z1, sums, chunks = call(
        middle_kernel,
        [field, ((8, LANES), F32), ((domains, 8, LANES), F32)],
        [VMEM] * 13,
        (pieces, others, second, second_others, across_first, near_first,
         inverse, right, image, basis, dense, edge, diag),
        apply_cost,
        [coarse_scratch],
    )
    totals = exchange(chunks, ("lon", "lat"))
    (out,) = call(finish_kernel, [field], [VMEM] * 4, (sums, totals, z0, z1), 4 * samples * nodes)
    return out


def solution(mesh):
    placed = (
        P(None, ("grp", "lon", "lat")),
        P(("grp", "lon", "lat"), None, None),
        P(("grp", "lon", "lat"), None),
        P(("grp", "lon", "lat")),
        P(("grp", "lon", "lat")),
        P(("grp", "lon", "lat")),
        P(("grp", "lon", "lat"), None),
        P(("grp", "lon", "lat"), None),
        P(("grp", "lon", "lat"), None),
        P(("grp", "lon", "lat")),
        P(("grp", "lon", "lat")),
        P(None, ("grp", "lon", "lat")),
        P(("grp", "lon", "lat"), None),
    )
    return jax.shard_map(
        body, mesh=mesh, in_specs=placed, out_specs=P(None, ("grp", "lon", "lat")), check_vma=False
    )
```

```python
import jax
import jax.numpy as jnp
import numpy as np
from jax import lax
from jax.experimental import pallas as pl
from jax.experimental.pallas import tpu as pltpu
from jax.sharding import PartitionSpec as P

F32 = jnp.float32
BF16 = jnp.bfloat16
VMEM = pl.BlockSpec(memory_space=pltpu.VMEM)
HBM = pl.BlockSpec(memory_space=pltpu.HBM)
SMEM = pl.BlockSpec(memory_space=pltpu.SMEM)
LANES = 128
SUM_ROWS = 16


def dot(a, b, ca=1, cb=0):
    return lax.dot_general(a, b, (((ca,), (cb,)), ((), ())), preferred_element_type=F32)


def call(kernel, outs, specs, args, flops, scratch=()):
    moved = sum(int(np.prod(a.shape)) * a.dtype.itemsize for a in args)
    return pl.pallas_call(
        kernel,
        out_shape=[jax.ShapeDtypeStruct(s, t) for s, t in outs],
        in_specs=specs,
        out_specs=[VMEM] * len(outs),
        scratch_shapes=list(scratch),
        compiler_params=pltpu.CompilerParams(vmem_limit_bytes=32 * 1024 * 1024),
        cost_estimate=pl.CostEstimate(flops=flops, bytes_accessed=moved, transcendentals=0),
    )(*args)


def fold(values):
    half = values.shape[0] // 2
    return jnp.concatenate([values[:half], values[half:]], axis=1)


def column_of(row):
    return jnp.transpose(jnp.broadcast_to(row, (LANES, LANES)))[:, 0:1]


def row_of(first, second):
    both = jnp.concatenate([first, second], axis=0)
    return jnp.transpose(jnp.broadcast_to(both, (LANES, LANES)))[0:1]


def row_sum(first, second):
    return jnp.sum(first * second, axis=1, keepdims=True)


def levels(values, edges):
    return dot(values.astype(BF16), edges, 1, 1)


def by_lon(shift_by, first_ref, second_ref, write):
    bit = (lax.axis_index("lon") >> shift_by) & 1
    pl.when(bit == 0)(lambda: write(first_ref, second_ref))
    pl.when(bit == 1)(lambda: write(second_ref, first_ref))


def pick(shift_by, first, second):
    bit = (lax.axis_index("lon") >> shift_by) & 1
    keep = jnp.full((1, 1), bit, jnp.int32) == 0
    first, second = first.astype(F32), second.astype(F32)
    return jnp.where(keep, first, second).astype(BF16), jnp.where(keep, second, first).astype(BF16)


def load_kernel(count_ref, right_hbm, vectors_hbm, react_hbm, mass_hbm, obs_hbm,
                coupling_hbm, blocks_hbm, east_hbm, west_hbm, inverse_hbm,
                chunks_ref, diag_ref, right_ref, vectors_ref, coupling_ref, blocks_ref, east_ref, west_ref,
                inverse_ref, react_ref, mass_ref, obs_ref, sems):
    pairs = (
        (right_hbm, right_ref), (vectors_hbm, vectors_ref), (react_hbm, react_ref), (mass_hbm, mass_ref),
        (obs_hbm, obs_ref), (coupling_hbm, coupling_ref), (blocks_hbm, blocks_ref), (east_hbm, east_ref),
        (west_hbm, west_ref), (inverse_hbm, inverse_ref),
    )
    copies = [pltpu.make_async_copy(src, dst, sems.at[i]) for i, (src, dst) in enumerate(pairs)]
    for copy in copies:
        copy.start()
    for copy in copies[:5]:
        copy.wait()
    nodes = right_ref.shape[1]
    active = (lax.broadcasted_iota(jnp.int32, (1, nodes), 1) < count_ref[0]).astype(F32)
    coarse = fold(dot(vectors_ref[...], right_ref[...] * active.astype(BF16), 1, 1)).astype(BF16)
    chunks_ref[...] = jnp.broadcast_to(coarse[None], chunks_ref.shape)
    react, mass, obs = react_ref[...], mass_ref[...], obs_ref[...]
    row = lax.broadcasted_iota(jnp.int32, (8, nodes), 0)
    diag = jnp.zeros((8, nodes), F32)
    for i, line in enumerate((active, react, 1.0 / mass, obs, 1.0 / (obs + react * react / mass))):
        diag = jnp.where(row == i, line, diag)
    diag_ref[...] = diag
    for copy in copies[5:]:
        copy.wait()


def lines(diag_ref):
    return tuple(diag_ref[i : i + 1, :] for i in range(5))


def prep_kernel(iface_ref, pattern_hbm, blocks_ref, right_ref, vectors_ref, coupling_ref, east_ref, west_ref, diag_ref,
                dense_ref, edge_ref, to_west_ref, to_east_ref, pattern_ref, total_ref, sem):
    copy = pltpu.make_async_copy(pattern_hbm, pattern_ref, sem)
    copy.start()
    samples, nodes = right_ref.shape
    count, block, _ = blocks_ref.shape
    slots = coupling_ref.shape[0]

    def clear(i, carry):
        total_ref[pl.ds(pl.multiple_of(i * block, block), block), :] = jnp.zeros((block, nodes), F32)
        return carry

    lax.fori_loop(0, nodes // block, clear, 0)
    copy.wait()
    unit = (
        lax.broadcasted_iota(jnp.int32, (block, block), 0) == lax.broadcasted_iota(jnp.int32, (block, block), 1)
    ).astype(F32).astype(BF16)

    def place(k, carry):
        rows = pl.ds(pl.multiple_of(pattern_ref[0, k] * block, block), block)
        cols = pl.ds(pl.multiple_of(pattern_ref[1, k] * block, block), block)
        values = blocks_ref[k]
        total_ref[rows, cols] += values.astype(F32)
        total_ref[cols, rows] += dot(unit, values, 1, 1)
        return carry

    lax.fori_loop(0, count, place, 0, unroll=8)

    def narrow(i, carry):
        rows = pl.ds(pl.multiple_of(i * block, block), block)
        dense_ref[rows, :] = total_ref[rows, :].astype(BF16)
        return carry

    lax.fori_loop(0, nodes // block, narrow, 0)

    active, react, inverse_mass, obs, jacobi = lines(diag_ref)
    node = lax.broadcasted_iota(jnp.int32, (slots, nodes), 1).astype(F32)
    east_hot = jnp.where(node == column_of(east_ref[...].astype(F32)), 1.0, 0.0).astype(BF16)
    west_hot = jnp.where(node == column_of(west_ref[...].astype(F32)), 1.0, 0.0).astype(BF16)
    live_a = lax.broadcasted_iota(jnp.int32, (slots, slots), 0) < iface_ref[0]
    live_b = lax.broadcasted_iota(jnp.int32, (slots, slots), 1) < iface_ref[0]
    link = jnp.where(live_a & live_b, coupling_ref[...], jnp.zeros((slots, slots), BF16))
    spread = dot(link, east_hot, 0, 0).astype(BF16)
    edge_ref[0:slots, :] = spread
    edge_ref[slots : 2 * slots, :] = west_hot
    edges = jnp.concatenate([spread, west_hot], axis=0)
    both = dot((edges.astype(F32) * inverse_mass).astype(BF16), edges, 1, 1).astype(BF16)
    masked = vectors_ref[...] * active.astype(BF16)
    smooth_right = (active * jacobi * right_ref[...].astype(F32)).astype(BF16)
    level = levels(jnp.concatenate([masked, smooth_right], axis=0), edges).astype(BF16)
    to_east_ref[0 : 2 * slots, :] = both[:, 0:slots]
    to_west_ref[0 : 2 * slots, :] = both[:, slots:]
    to_east_ref[2 * slots :, :] = level[:, 0:slots]
    to_west_ref[2 * slots :, :] = level[:, slots:]


def unfold(count, piece, coarse_ref):
    half = coarse_ref.shape[0] // count // 4
    lat = lax.axis_index("lat")

    def move(d, carry):
        for side in range(2):
            values = piece(side, d)
            at = pl.multiple_of((2 * d + (lat if side == 0 else 1 - lat)) * 2 * half, 2 * half)
            coarse_ref[pl.ds(at, half), :] = values[:, 0 : LANES // 2]
            coarse_ref[pl.ds(at + half, half), :] = values[:, LANES // 2 :]
        return carry

    lax.fori_loop(0, count, move, 0, unroll=min(count, 8))


def smooth(field, coarse_ref, inverse_ref, vectors_ref, active, jacobi):
    fix = dot(inverse_ref[...], coarse_ref[...]).astype(BF16)
    return active * (field * jacobi + dot(fix, vectors_ref[...], 0, 0))


def start_kernel(pieces_ref, others_ref, inverse_ref, right_ref, vectors_ref, dense_ref, edge_ref, diag_ref,
                 to_west_ref, to_east_ref,
                 z_ref, scaled_ref, near_ref, across_ref, far_ref, beyond_ref, coarse_ref):
    samples, nodes = right_ref.shape
    unfold(pieces_ref.shape[0], lambda side, d: (pieces_ref, others_ref)[side][d], coarse_ref)
    active, react, inverse_mass, obs, jacobi = lines(diag_ref)
    z = smooth(right_ref[...].astype(F32), coarse_ref, inverse_ref, vectors_ref, active, jacobi)
    z_ref[...] = z
    edges = edge_ref[...]
    scaled = (dot(z.astype(BF16), dense_ref[...]) + react * z) * inverse_mass
    scaled_ref[...] = scaled
    level1 = levels(z, edges).astype(BF16)
    level2 = levels(scaled, edges).astype(BF16)
    slots = edges.shape[0] // 2

    def send(east_ref, west_ref):
        for ref, cols, corr_ref in (
            (east_ref, slice(0, slots), to_east_ref),
            (west_ref, slice(slots, 2 * slots), to_west_ref),
        ):
            ref[0:samples, :] = level1[:, cols]
            ref[samples : 2 * samples, :] = level2[:, cols]
            ref[2 * samples :, :] = corr_ref[...]

    def send_far(east_ref, west_ref):
        east_ref[...] = level1[:, 0:slots]
        west_ref[...] = level1[:, slots:]

    by_lon(0, near_ref, across_ref, send)
    by_lon(1, far_ref, beyond_ref, send_far)


def image_kernel(across_ref, beyond_ref, near_ref, far_ref, own_far_ref, own_beyond_ref,
                 z_ref, scaled_ref, dense_ref, edge_ref, diag_ref, right_ref, vectors_ref,
                 image_ref, chunks_ref):
    samples, nodes = z_ref.shape
    active, react, inverse_mass, obs, jacobi = lines(diag_ref)
    z = z_ref[...]
    edges = edge_ref[...]
    fixed = 2 * samples + edges.shape[0]
    from_east, from_west = pick(0, near_ref[0:fixed, :], across_ref[0:fixed, :])
    beyond_east, beyond_west = pick(1, far_ref[...], beyond_ref[...])
    own_east, own_west = pick(1, own_far_ref[...], own_beyond_ref[...])
    arrived = jnp.concatenate([from_east[0:samples], from_west[0:samples]], axis=1)
    inner = scaled_ref[...] + dot(arrived, edges) * inverse_mass
    east_terms = jnp.concatenate([beyond_east, own_east], axis=1)
    west_terms = jnp.concatenate([own_west, beyond_west], axis=1)
    second_east = from_east[samples : 2 * samples].astype(F32) + dot(east_terms, from_east[2 * samples : fixed])
    second_west = from_west[samples : 2 * samples].astype(F32) + dot(west_terms, from_west[2 * samples : fixed])
    arrived2 = jnp.concatenate([second_east, second_west], axis=1).astype(BF16)
    stiff = dot(inner.astype(BF16), dense_ref[...]) + dot(arrived2, edges) + react * inner
    image = active * (stiff + obs * z)
    image_ref[...] = image
    level = levels(image * jacobi, edges).astype(BF16)
    coarse = fold(dot(vectors_ref[...], image.astype(BF16), 1, 1))
    high = coarse.astype(BF16)
    low = (coarse - high.astype(F32)).astype(BF16)
    sums = row_of(row_sum(active * right_ref[...].astype(F32), z), row_sum(z, image))
    row = lax.broadcasted_iota(jnp.int32, (SUM_ROWS, LANES), 0)
    tail = jnp.zeros((SUM_ROWS, LANES), F32)
    for i in range(3):
        part = sums.astype(BF16).astype(F32)
        tail = jnp.where(row == i, part, tail)
        sums = sums - part
    count, rows, _ = chunks_ref.shape
    slots = level.shape[1] // 2
    common = jnp.concatenate([high, low, tail.astype(BF16), level[:, 0:slots]], axis=0)
    chunks_ref[...] = jnp.broadcast_to(common[None], chunks_ref.shape)
    before = lax.rem(lax.axis_index("lon") + count - 1, count)
    chunks_ref[before, rows - samples :, :] = level[:, slots:]


def middle_kernel(pieces_ref, others_ref, second_ref, second_others_ref,
                  across_ref, near_ref, across_inverse_ref, near_inverse_ref, inverse_ref, right_ref, image_ref, vectors_ref,
                  dense_ref, edge_ref, diag_ref, z_ref, sums_ref, chunks_ref, coarse_ref):
    samples, nodes = right_ref.shape
    count, half, _ = pieces_ref.shape
    tail = slice(2 * half, 2 * half + SUM_ROWS)

    def add(d, total):
        return total + second_ref[d, tail, :].astype(F32) + second_others_ref[d, tail, :].astype(F32)

    parts = lax.fori_loop(0, count, add, jnp.zeros((SUM_ROWS, LANES), F32), unroll=min(count, 8))
    sums = parts[2:3] + parts[1:2] + parts[0:1]
    step = sums[:, 0 : LANES // 2] / sums[:, LANES // 2 :]
    step = jnp.concatenate([step, step], axis=1)

    def piece(side, d):
        first, change = ((pieces_ref, second_ref), (others_ref, second_others_ref))[side]
        moved = change[d, 0:half, :].astype(F32) + change[d, half : 2 * half, :].astype(F32)
        return (first[d].astype(F32) - step * moved).astype(BF16)

    unfold(count, piece, coarse_ref)
    active, react, inverse_mass, obs, jacobi = lines(diag_ref)
    image = image_ref[...]
    edges = edge_ref[...]
    step_column = column_of(step)[0:samples]
    residual = active * right_ref[...].astype(F32) - step_column * image
    z = smooth(residual, coarse_ref, inverse_ref, vectors_ref, active, jacobi)
    z_ref[...] = z

    def arriving(level, inverse, change):
        fix = dot(inverse, coarse_ref[...]).astype(BF16)
        spread = dot(fix, level[0 : fix.shape[0]], 0, 0)
        return (level[fix.shape[0] :].astype(F32) - step_column * change.astype(F32) + spread).astype(BF16)

    lon = lax.axis_index("lon")
    ahead, before = lax.rem(lon + 1, count), lax.rem(lon + count - 1, count)
    fixed = 2 * samples + edges.shape[0]
    east_level, west_level = pick(0, near_ref[fixed:, :], across_ref[fixed:, :])
    east_inverse, west_inverse = pick(0, near_inverse_ref[...], across_inverse_ref[...])
    from_east = arriving(east_level, east_inverse, second_ref[ahead, 2 * half + SUM_ROWS :, :])
    from_west = arriving(west_level, west_inverse, second_ref[before, 2 * half + SUM_ROWS :, :])
    arrived = jnp.concatenate([from_east, from_west], axis=1)
    stiff = dot(z.astype(BF16), dense_ref[...]) + react * z + dot(arrived, edges)
    curve = jnp.sum(stiff * stiff * inverse_mass + obs * z * z, axis=1, keepdims=True)
    products = row_of(row_sum(residual, z), row_sum(z, image))
    row = lax.broadcasted_iota(jnp.int32, (8, LANES), 0)
    chunk = jnp.where(row == 0, products, row_of(curve, curve))
    chunks_ref[...] = jnp.broadcast_to(chunk[None], chunks_ref.shape)
    sums_ref[...] = jnp.broadcast_to(sums, sums_ref.shape)


def finish_kernel(sums_ref, chunks_ref, first_ref, second_ref, out_ref):
    samples = first_ref.shape[0]
    half = LANES // 2
    totals = jnp.sum(chunks_ref[...], axis=0)
    norm0, curve0 = sums_ref[1:2, 0:half], sums_ref[1:2, half:]
    norm1, cross = totals[0:1, 0:half], totals[0:1, half:]
    curve = totals[1:2, 0:half]
    beta = norm1 / norm0
    step0 = norm0 / curve0
    step1 = norm1 / (curve + beta * (2.0 * cross + beta * curve0))
    scales = column_of(jnp.concatenate([step0 + step1 * beta, step1], axis=1))
    out_ref[...] = scales[0:samples] * first_ref[...] + scales[samples : 2 * samples] * second_ref[...]


def exchange(chunks, axes):
    return lax.all_to_all(chunks, axes, split_axis=0, concat_axis=0, tiled=True)


def other_band(array):
    return lax.ppermute(array, "lat", [(0, 1), (1, 0)])


def swap(array, reach, inner):
    size = lax.axis_size("lon")
    pairs = []
    for i in range(size):
        up = (i // reach) % 2 == (0 if inner else 1)
        pairs.append((i, (i + (reach if up else -reach)) % size))
    return lax.ppermute(array, "lon", pairs)


def body(
    right_side,
    stiffness_blocks,
    block_pattern,
    reaction,
    lumped_mass,
    obs_precision,
    coupling,
    east_rows,
    west_rows,
    iface_count,
    node_count,
    deflation,
    coarse_inverse,
):
    samples, nodes = right_side.shape
    slots = coupling.shape[0]
    vectors = deflation.shape[0]
    sectors = lax.axis_size("lon")
    domains = sectors * lax.axis_size("lat")
    half = vectors // 2
    react, mass, obs = reaction[None], lumped_mass[None], obs_precision[None]
    field = ((samples, nodes), F32)
    coarse_scratch = pltpu.VMEM((domains * vectors, samples), BF16)
    apply_cost = 2 * samples * nodes * nodes
    corr = ((2 * slots + vectors + samples, slots), BF16)
    kept = (right_side, deflation, coupling, stiffness_blocks, east_rows, west_rows, coarse_inverse)
    inputs = (right_side, deflation, react, mass, obs, coupling, stiffness_blocks, east_rows, west_rows, coarse_inverse)
    line = pltpu.VMEM((1, nodes), F32)
    chunks, diag, right, basis, link, stored, east, west, inverse = call(
        load_kernel,
        [((sectors, half, LANES), BF16), ((8, nodes), F32)] + [(a.shape, a.dtype) for a in kept],
        [SMEM] + [HBM] * len(inputs),
        [node_count] + [pltpu.with_memory_space_constraint(a, pltpu.HBM) for a in inputs],
        2 * samples * vectors * nodes,
        [line, line, line, pltpu.SemaphoreType.DMA((len(inputs),))],
    )
    across_inverse, near_inverse = swap(coarse_inverse, 1, False), swap(coarse_inverse, 1, True)
    pieces, stored, iface, across_inverse, near_inverse = lax.optimization_barrier(
        (exchange(chunks, "lon"), stored, iface_count, across_inverse, near_inverse)
    )
    pattern = pltpu.with_memory_space_constraint(block_pattern.T, pltpu.HBM)
    dense, edge, corr_west, corr_east = call(
        prep_kernel,
        [((nodes, nodes), BF16), ((2 * slots, nodes), BF16), corr, corr],
        [SMEM, HBM] + [VMEM] * 7,
        (iface, pattern, stored, right, basis, link, east, west, diag),
        apply_cost,
        [pltpu.SMEM((2, block_pattern.shape[0]), jnp.int32), pltpu.VMEM((nodes, nodes), F32), pltpu.SemaphoreType.DMA],
    )
    others = other_band(pieces)
    z0, scaled, near, across, far, beyond = call(
        start_kernel,
        [field] * 2 + [((2 * samples + corr[0][0], slots), BF16)] * 2 + [((samples, slots), BF16)] * 2,
        [VMEM] * 10,
        (pieces, others, inverse, right, basis, dense, edge, diag, corr_west, corr_east),
        apply_cost,
        [coarse_scratch],
    )
    across = swap(across, 1, False)
    got_beyond = swap(beyond, 2, False)
    near = swap(near, 1, True)
    got_far = swap(far, 2, True)
    image, chunks = call(
        image_kernel,
        [field, ((sectors, 2 * half + SUM_ROWS + samples, LANES), BF16)],
        [VMEM] * 13,
        (across, got_beyond, near, got_far, far, beyond, z0, scaled, dense, edge, diag, right, basis),
        apply_cost,
    )
    second = exchange(chunks, "lon")
    second_others = other_band(second)
    z1, sums, chunks = call(
        middle_kernel,
        [field, ((8, LANES), F32), ((domains, 8, LANES), F32)],
        [VMEM] * 15,
        (pieces, others, second, second_others, across, near, across_inverse, near_inverse,
         inverse, right, image, basis, dense, edge, diag),
        apply_cost,
        [coarse_scratch],
    )
    totals = exchange(chunks, ("lon", "lat"))
    (out,) = call(finish_kernel, [field], [VMEM] * 4, (sums, totals, z0, z1), 4 * samples * nodes)
    return out


def solution(mesh):
    placed = (
        P(None, ("grp", "lon", "lat")),
        P(("grp", "lon", "lat"), None, None),
        P(("grp", "lon", "lat"), None),
        P(("grp", "lon", "lat")),
        P(("grp", "lon", "lat")),
        P(("grp", "lon", "lat")),
        P(("grp", "lon", "lat"), None),
        P(("grp", "lon", "lat"), None),
        P(("grp", "lon", "lat"), None),
        P(("grp", "lon", "lat")),
        P(("grp", "lon", "lat")),
        P(None, ("grp", "lon", "lat")),
        P(("grp", "lon", "lat"), None),
    )
    return jax.shard_map(
        body, mesh=mesh, in_specs=placed, out_specs=P(None, ("grp", "lon", "lat")), check_vma=False
    )
```

```python
import jax
import jax.numpy as jnp
import numpy as np
from jax import lax
from jax.experimental import pallas as pl
from jax.experimental.pallas import tpu as pltpu
from jax.sharding import PartitionSpec as P

F32 = jnp.float32
BF16 = jnp.bfloat16
VMEM = pl.BlockSpec(memory_space=pltpu.VMEM)
HBM = pl.BlockSpec(memory_space=pltpu.HBM)
SMEM = pl.BlockSpec(memory_space=pltpu.SMEM)
LANES = 128
SUM_ROWS = 16


def dot(a, b, ca=1, cb=0):
    return lax.dot_general(a, b, (((ca,), (cb,)), ((), ())), preferred_element_type=F32)


def call(kernel, outs, specs, args, flops, scratch=()):
    moved = sum(int(np.prod(a.shape)) * a.dtype.itemsize for a in args)
    return pl.pallas_call(
        kernel,
        out_shape=[jax.ShapeDtypeStruct(s, t) for s, t in outs],
        in_specs=specs,
        out_specs=[VMEM] * len(outs),
        scratch_shapes=list(scratch),
        compiler_params=pltpu.CompilerParams(vmem_limit_bytes=32 * 1024 * 1024),
        cost_estimate=pl.CostEstimate(flops=flops, bytes_accessed=moved, transcendentals=0),
    )(*args)


def fold(values):
    half = values.shape[0] // 2
    return jnp.concatenate([values[:half], values[half:]], axis=1)


def column_of(row):
    return jnp.transpose(jnp.broadcast_to(row, (LANES, LANES)))[:, 0:1]


def row_of(first, second):
    both = jnp.concatenate([first, second], axis=0)
    return jnp.transpose(jnp.broadcast_to(both, (LANES, LANES)))[0:1]


def row_sum(first, second):
    return jnp.sum(first * second, axis=1, keepdims=True)


def levels(values, edges):
    return dot(values.astype(BF16), edges, 1, 1)


def by_lon(shift_by, first_ref, second_ref, write):
    bit = (lax.axis_index("lon") >> shift_by) & 1
    pl.when(bit == 0)(lambda: write(first_ref, second_ref))
    pl.when(bit == 1)(lambda: write(second_ref, first_ref))


def pick(shift_by, first, second):
    bit = (lax.axis_index("lon") >> shift_by) & 1
    keep = jnp.full((1, 1), bit, jnp.int32) == 0
    first, second = first.astype(F32), second.astype(F32)
    return jnp.where(keep, first, second).astype(BF16), jnp.where(keep, second, first).astype(BF16)


def lines(diag_ref):
    return tuple(diag_ref[i : i + 1, :] for i in range(5))


def load_kernel(count_ref, right_hbm, vectors_hbm, react_hbm, mass_hbm, obs_hbm, coupling_hbm, east_hbm, west_hbm,
                blocks_hbm, inverse_hbm,
                chunks_ref, diag_ref, edge_ref, near_ref, across_ref, right_ref, vectors_ref, blocks_ref, inverse_ref,
                react_ref, mass_ref, obs_ref, coupling_ref, east_ref, west_ref, sems):
    pairs = (
        (right_hbm, right_ref), (vectors_hbm, vectors_ref), (react_hbm, react_ref), (mass_hbm, mass_ref),
        (obs_hbm, obs_ref), (coupling_hbm, coupling_ref), (east_hbm, east_ref), (west_hbm, west_ref),
        (inverse_hbm, inverse_ref), (blocks_hbm, blocks_ref),
    )
    copies = [pltpu.make_async_copy(src, dst, sems.at[i]) for i, (src, dst) in enumerate(pairs)]
    for copy in copies:
        copy.start()
    for copy in copies[:9]:
        copy.wait()
    nodes = right_ref.shape[1]
    slots = coupling_ref.shape[0]
    active = (lax.broadcasted_iota(jnp.int32, (1, nodes), 1) < count_ref[0]).astype(F32)
    right = active * right_ref[...].astype(F32)
    coarse = fold(dot(vectors_ref[...], right.astype(BF16), 1, 1)).astype(BF16)
    chunks_ref[...] = jnp.broadcast_to(coarse[None], chunks_ref.shape)
    react, mass, obs = react_ref[...], mass_ref[...], obs_ref[...]
    inverse_mass, jacobi = 1.0 / mass, 1.0 / (obs + react * react / mass)
    row = lax.broadcasted_iota(jnp.int32, (8, nodes), 0)
    diag = jnp.zeros((8, nodes), F32)
    for i, line in enumerate((active, react, inverse_mass, obs, jacobi)):
        diag = jnp.where(row == i, line, diag)
    diag_ref[...] = diag

    node = lax.broadcasted_iota(jnp.int32, (slots, nodes), 1).astype(F32)
    east_hot = jnp.where(node == column_of(east_ref[...].astype(F32)), 1.0, 0.0).astype(BF16)
    west_hot = jnp.where(node == column_of(west_ref[...].astype(F32)), 1.0, 0.0).astype(BF16)
    live_a = lax.broadcasted_iota(jnp.int32, (slots, slots), 0) < count_ref[1]
    live_b = lax.broadcasted_iota(jnp.int32, (slots, slots), 1) < count_ref[1]
    link = jnp.where(live_a & live_b, coupling_ref[...], jnp.zeros((slots, slots), BF16))
    edges = jnp.concatenate([dot(link, east_hot, 0, 0).astype(BF16), west_hot], axis=0)
    edge_ref[...] = edges
    rows = [
        (edges.astype(F32) * inverse_mass).astype(BF16),
        vectors_ref[...] * active.astype(BF16),
        (jacobi * right).astype(BF16),
    ]
    level = dot(jnp.concatenate(rows, axis=0), edges, 1, 1).astype(BF16)
    kept, width = inverse_ref.shape
    fixed = width // LANES * kept

    def send(east_ref, west_ref):
        for ref, cols in ((east_ref, slice(0, slots)), (west_ref, slice(slots, 2 * slots))):
            for j in range(width // LANES):
                ref[j * kept : (j + 1) * kept, :] = inverse_ref[:, j * LANES : (j + 1) * LANES]
            ref[fixed:, :] = level[:, cols]

    by_lon(0, near_ref, across_ref, send)
    copies[9].wait()


def prep_kernel(pattern_hbm, blocks_ref, dense_ref, pattern_ref, total_ref, sem):
    copy = pltpu.make_async_copy(pattern_hbm, pattern_ref, sem)
    copy.start()
    nodes = dense_ref.shape[0]
    count, block, _ = blocks_ref.shape

    def clear(i, carry):
        total_ref[pl.ds(pl.multiple_of(i * block, block), block), :] = jnp.zeros((block, nodes), F32)
        return carry

    lax.fori_loop(0, nodes // block, clear, 0)
    copy.wait()
    unit = (
        lax.broadcasted_iota(jnp.int32, (block, block), 0) == lax.broadcasted_iota(jnp.int32, (block, block), 1)
    ).astype(F32).astype(BF16)

    def place(k, carry):
        rows = pl.ds(pl.multiple_of(pattern_ref[0, k] * block, block), block)
        cols = pl.ds(pl.multiple_of(pattern_ref[1, k] * block, block), block)
        values = blocks_ref[k]
        total_ref[rows, cols] += values.astype(F32)
        total_ref[cols, rows] += dot(unit, values, 1, 1)
        return carry

    lax.fori_loop(0, count, place, 0, unroll=8)

    def narrow(i, carry):
        rows = pl.ds(pl.multiple_of(i * block, block), block)
        dense_ref[rows, :] = total_ref[rows, :].astype(BF16)
        return carry

    lax.fori_loop(0, nodes // block, narrow, 0)


def unfold(count, piece, coarse_ref):
    half = coarse_ref.shape[0] // count // 4
    lat = lax.axis_index("lat")

    def move(d, carry):
        for side in range(2):
            values = piece(side, d)
            at = pl.multiple_of((2 * d + (lat if side == 0 else 1 - lat)) * 2 * half, 2 * half)
            coarse_ref[pl.ds(at, half), :] = values[:, 0 : LANES // 2]
            coarse_ref[pl.ds(at + half, half), :] = values[:, LANES // 2 :]
        return carry

    lax.fori_loop(0, count, move, 0, unroll=min(count, 8))


def smooth(field, coarse_ref, inverse_ref, vectors_ref, active, jacobi):
    fix = dot(inverse_ref[...], coarse_ref[...]).astype(BF16)
    return active * (field * jacobi + dot(fix, vectors_ref[...], 0, 0))


def start_kernel(pieces_ref, others_ref, inverse_ref, right_ref, vectors_ref, dense_ref, edge_ref, diag_ref,
                 z_ref, scaled_ref, near_ref, across_ref, far_ref, beyond_ref, coarse_ref):
    samples, nodes = right_ref.shape
    unfold(pieces_ref.shape[0], lambda side, d: (pieces_ref, others_ref)[side][d], coarse_ref)
    active, react, inverse_mass, obs, jacobi = lines(diag_ref)
    z = smooth(right_ref[...].astype(F32), coarse_ref, inverse_ref, vectors_ref, active, jacobi)
    z_ref[...] = z
    edges = edge_ref[...]
    scaled = (dot(z.astype(BF16), dense_ref[...]) + react * z) * inverse_mass
    scaled_ref[...] = scaled
    level1 = levels(z, edges).astype(BF16)
    level2 = levels(scaled, edges).astype(BF16)
    slots = edges.shape[0] // 2

    def send(east_ref, west_ref):
        for ref, cols in ((east_ref, slice(0, slots)), (west_ref, slice(slots, 2 * slots))):
            ref[0:samples, :] = level1[:, cols]
            ref[samples:, :] = level2[:, cols]

    def send_far(east_ref, west_ref):
        east_ref[...] = level1[:, 0:slots]
        west_ref[...] = level1[:, slots:]

    by_lon(0, near_ref, across_ref, send)
    by_lon(1, far_ref, beyond_ref, send_far)


def image_kernel(across_ref, beyond_ref, near_ref, far_ref, own_far_ref, own_beyond_ref, across_corr_ref, near_corr_ref,
                 z_ref, scaled_ref, dense_ref, edge_ref, diag_ref, right_ref, vectors_ref,
                 image_ref, chunks_ref):
    samples, nodes = z_ref.shape
    active, react, inverse_mass, obs, jacobi = lines(diag_ref)
    z = z_ref[...]
    edges = edge_ref[...]
    from_east, from_west = pick(0, near_ref[...], across_ref[...])
    fixed = near_corr_ref.shape[0] - edges.shape[0] - vectors_ref.shape[0] - samples
    corr = slice(fixed, fixed + edges.shape[0])
    corr_east, corr_west = pick(0, near_corr_ref[corr, :], across_corr_ref[corr, :])
    beyond_east, beyond_west = pick(1, far_ref[...], beyond_ref[...])
    own_east, own_west = pick(1, own_far_ref[...], own_beyond_ref[...])
    arrived = jnp.concatenate([from_east[0:samples], from_west[0:samples]], axis=1)
    inner = scaled_ref[...] + dot(arrived, edges) * inverse_mass
    east_terms = jnp.concatenate([beyond_east, own_east], axis=1)
    west_terms = jnp.concatenate([own_west, beyond_west], axis=1)
    second_east = from_east[samples:].astype(F32) + dot(east_terms, corr_east)
    second_west = from_west[samples:].astype(F32) + dot(west_terms, corr_west)
    arrived2 = jnp.concatenate([second_east, second_west], axis=1).astype(BF16)
    stiff = dot(inner.astype(BF16), dense_ref[...]) + dot(arrived2, edges) + react * inner
    image = active * (stiff + obs * z)
    image_ref[...] = image
    level = levels(image * jacobi, edges).astype(BF16)
    coarse = fold(dot(vectors_ref[...], image.astype(BF16), 1, 1))
    high = coarse.astype(BF16)
    low = (coarse - high.astype(F32)).astype(BF16)
    sums = row_of(row_sum(active * right_ref[...].astype(F32), z), row_sum(z, image))
    row = lax.broadcasted_iota(jnp.int32, (SUM_ROWS, LANES), 0)
    tail = jnp.zeros((SUM_ROWS, LANES), F32)
    for i in range(3):
        part = sums.astype(BF16).astype(F32)
        tail = jnp.where(row == i, part, tail)
        sums = sums - part
    count, rows, _ = chunks_ref.shape
    slots = level.shape[1] // 2
    common = jnp.concatenate([high, low, tail.astype(BF16), level[:, 0:slots]], axis=0)
    chunks_ref[...] = jnp.broadcast_to(common[None], chunks_ref.shape)
    before = lax.rem(lax.axis_index("lon") + count - 1, count)
    chunks_ref[before, rows - samples :, :] = level[:, slots:]


def middle_kernel(pieces_ref, others_ref, second_ref, second_others_ref,
                  across_ref, near_ref, inverse_ref, right_ref, image_ref, vectors_ref,
                  dense_ref, edge_ref, diag_ref, z_ref, sums_ref, chunks_ref, coarse_ref):
    samples, nodes = right_ref.shape
    count, half, _ = pieces_ref.shape
    tail = slice(2 * half, 2 * half + SUM_ROWS)

    def add(d, total):
        return total + second_ref[d, tail, :].astype(F32) + second_others_ref[d, tail, :].astype(F32)

    parts = lax.fori_loop(0, count, add, jnp.zeros((SUM_ROWS, LANES), F32), unroll=min(count, 8))
    sums = parts[2:3] + parts[1:2] + parts[0:1]
    step = sums[:, 0 : LANES // 2] / sums[:, LANES // 2 :]
    step = jnp.concatenate([step, step], axis=1)

    def piece(side, d):
        first, change = ((pieces_ref, second_ref), (others_ref, second_others_ref))[side]
        moved = change[d, 0:half, :].astype(F32) + change[d, half : 2 * half, :].astype(F32)
        return (first[d].astype(F32) - step * moved).astype(BF16)

    unfold(count, piece, coarse_ref)
    active, react, inverse_mass, obs, jacobi = lines(diag_ref)
    image = image_ref[...]
    edges = edge_ref[...]
    step_column = column_of(step)[0:samples]
    residual = active * right_ref[...].astype(F32) - step_column * image
    z = smooth(residual, coarse_ref, inverse_ref, vectors_ref, active, jacobi)
    z_ref[...] = z

    kept, width = inverse_ref.shape
    fixed = width // LANES * kept + edges.shape[0]

    def arriving(static, change):
        inverse = jnp.concatenate([static[j * kept : (j + 1) * kept] for j in range(width // LANES)], axis=1)
        fix = dot(inverse, coarse_ref[...]).astype(BF16)
        spread = dot(fix, static[fixed : fixed + kept], 0, 0)
        return (static[fixed + kept :].astype(F32) - step_column * change.astype(F32) + spread).astype(BF16)

    lon = lax.axis_index("lon")
    ahead, before = lax.rem(lon + 1, count), lax.rem(lon + count - 1, count)
    east_static, west_static = pick(0, near_ref[...], across_ref[...])
    from_east = arriving(east_static, second_ref[ahead, 2 * half + SUM_ROWS :, :])
    from_west = arriving(west_static, second_ref[before, 2 * half + SUM_ROWS :, :])
    arrived = jnp.concatenate([from_east, from_west], axis=1)
    stiff = dot(z.astype(BF16), dense_ref[...]) + react * z + dot(arrived, edges)
    curve = jnp.sum(stiff * stiff * inverse_mass + obs * z * z, axis=1, keepdims=True)
    products = row_of(row_sum(residual, z), row_sum(z, image))
    row = lax.broadcasted_iota(jnp.int32, (8, LANES), 0)
    chunk = jnp.where(row == 0, products, row_of(curve, curve))
    chunks_ref[...] = jnp.broadcast_to(chunk[None], chunks_ref.shape)
    sums_ref[...] = jnp.broadcast_to(sums, sums_ref.shape)


def finish_kernel(sums_ref, chunks_ref, first_ref, second_ref, out_ref):
    samples = first_ref.shape[0]
    half = LANES // 2
    totals = jnp.sum(chunks_ref[...], axis=0)
    norm0, curve0 = sums_ref[1:2, 0:half], sums_ref[1:2, half:]
    norm1, cross = totals[0:1, 0:half], totals[0:1, half:]
    curve = totals[1:2, 0:half]
    beta = norm1 / norm0
    step0 = norm0 / curve0
    step1 = norm1 / (curve + beta * (2.0 * cross + beta * curve0))
    scales = column_of(jnp.concatenate([step0 + step1 * beta, step1], axis=1))
    out_ref[...] = scales[0:samples] * first_ref[...] + scales[samples : 2 * samples] * second_ref[...]


def exchange(chunks, axes):
    return lax.all_to_all(chunks, axes, split_axis=0, concat_axis=0, tiled=True)


def other_band(array):
    return lax.ppermute(array, "lat", [(0, 1), (1, 0)])


def swap(array, reach, inner):
    size = lax.axis_size("lon")
    pairs = []
    for i in range(size):
        up = (i // reach) % 2 == (0 if inner else 1)
        pairs.append((i, (i + (reach if up else -reach)) % size))
    return lax.ppermute(array, "lon", pairs)


def body(
    right_side,
    stiffness_blocks,
    block_pattern,
    reaction,
    lumped_mass,
    obs_precision,
    coupling,
    east_rows,
    west_rows,
    iface_count,
    node_count,
    deflation,
    coarse_inverse,
):
    samples, nodes = right_side.shape
    slots = coupling.shape[0]
    vectors = deflation.shape[0]
    sectors = lax.axis_size("lon")
    domains = sectors * lax.axis_size("lat")
    half = vectors // 2
    react, mass, obs = reaction[None], lumped_mass[None], obs_precision[None]
    field = ((samples, nodes), F32)
    coarse_scratch = pltpu.VMEM((domains * vectors, samples), BF16)
    apply_cost = 2 * samples * nodes * nodes
    static = ((coarse_inverse.size // LANES + 2 * slots + vectors + samples, slots), BF16)
    inputs = (right_side, deflation, react, mass, obs, coupling, east_rows, west_rows, stiffness_blocks, coarse_inverse)
    line = pltpu.VMEM((1, nodes), F32)
    chunks, diag, edge, near_static, across_static, right, basis, stored, inverse = call(
        load_kernel,
        [((sectors, half, LANES), BF16), ((8, nodes), F32), ((2 * slots, nodes), BF16), static, static]
        + [(a.shape, a.dtype) for a in (right_side, deflation, stiffness_blocks, coarse_inverse)],
        [SMEM] + [HBM] * len(inputs),
        [jnp.concatenate([node_count, iface_count])] + [pltpu.with_memory_space_constraint(a, pltpu.HBM) for a in inputs],
        2 * samples * vectors * nodes,
        [line, line, line] + [pltpu.VMEM(a.shape, a.dtype) for a in (coupling, east_rows, west_rows)]
        + [pltpu.SemaphoreType.DMA((len(inputs),))],
    )
    pieces, stored, across_static, near_static = lax.optimization_barrier(
        (exchange(chunks, "lon"), stored, swap(across_static, 1, False), swap(near_static, 1, True))
    )
    pattern = pltpu.with_memory_space_constraint(block_pattern.T, pltpu.HBM)
    (dense,) = call(
        prep_kernel,
        [((nodes, nodes), BF16)],
        [HBM, VMEM],
        (pattern, stored),
        apply_cost,
        [pltpu.SMEM((2, block_pattern.shape[0]), jnp.int32), pltpu.VMEM((nodes, nodes), F32), pltpu.SemaphoreType.DMA],
    )
    others = other_band(pieces)
    z0, scaled, near, across, far, beyond = call(
        start_kernel,
        [field] * 2 + [((2 * samples, slots), BF16)] * 2 + [((samples, slots), BF16)] * 2,
        [VMEM] * 8,
        (pieces, others, inverse, right, basis, dense, edge, diag),
        apply_cost,
        [coarse_scratch],
    )
    across = swap(across, 1, False)
    got_beyond = swap(beyond, 2, False)
    near = swap(near, 1, True)
    got_far = swap(far, 2, True)
    image, chunks = call(
        image_kernel,
        [field, ((sectors, 2 * half + SUM_ROWS + samples, LANES), BF16)],
        [VMEM] * 15,
        (across, got_beyond, near, got_far, far, beyond, across_static, near_static, z0, scaled, dense, edge, diag, right, basis),
        apply_cost,
    )
    second = exchange(chunks, "lon")
    second_others = other_band(second)
    z1, sums, chunks = call(
        middle_kernel,
        [field, ((8, LANES), F32), ((domains, 8, LANES), F32)],
        [VMEM] * 13,
        (pieces, others, second, second_others, across_static, near_static,
         inverse, right, image, basis, dense, edge, diag),
        apply_cost,
        [coarse_scratch],
    )
    totals = exchange(chunks, ("lon", "lat"))
    (out,) = call(finish_kernel, [field], [VMEM] * 4, (sums, totals, z0, z1), 4 * samples * nodes)
    return out


def solution(mesh):
    placed = (
        P(None, ("grp", "lon", "lat")),
        P(("grp", "lon", "lat"), None, None),
        P(("grp", "lon", "lat"), None),
        P(("grp", "lon", "lat")),
        P(("grp", "lon", "lat")),
        P(("grp", "lon", "lat")),
        P(("grp", "lon", "lat"), None),
        P(("grp", "lon", "lat"), None),
        P(("grp", "lon", "lat"), None),
        P(("grp", "lon", "lat")),
        P(("grp", "lon", "lat")),
        P(None, ("grp", "lon", "lat")),
        P(("grp", "lon", "lat"), None),
    )
    return jax.shard_map(
        body, mesh=mesh, in_specs=placed, out_specs=P(None, ("grp", "lon", "lat")), check_vma=False
    )
```

```python
import jax
import jax.numpy as jnp
import numpy as np
from jax import lax
from jax.experimental import pallas as pl
from jax.experimental.pallas import tpu as pltpu
from jax.sharding import PartitionSpec as P

F32 = jnp.float32
BF16 = jnp.bfloat16
VMEM = pl.BlockSpec(memory_space=pltpu.VMEM)
HBM = pl.BlockSpec(memory_space=pltpu.HBM)
SMEM = pl.BlockSpec(memory_space=pltpu.SMEM)
LANES = 128
SUM_ROWS = 16


def dot(a, b, ca=1, cb=0):
    return lax.dot_general(a, b, (((ca,), (cb,)), ((), ())), preferred_element_type=F32)


def call(kernel, outs, specs, args, flops, scratch=()):
    moved = sum(int(np.prod(a.shape)) * a.dtype.itemsize for a in args)
    return pl.pallas_call(
        kernel,
        out_shape=[jax.ShapeDtypeStruct(s, t) for s, t in outs],
        in_specs=specs,
        out_specs=[VMEM] * len(outs),
        scratch_shapes=list(scratch),
        compiler_params=pltpu.CompilerParams(vmem_limit_bytes=32 * 1024 * 1024),
        cost_estimate=pl.CostEstimate(flops=flops, bytes_accessed=moved, transcendentals=0),
    )(*args)


def fold(values):
    half = values.shape[0] // 2
    return jnp.concatenate([values[:half], values[half:]], axis=1)


def column_of(row):
    return jnp.transpose(jnp.broadcast_to(row, (LANES, LANES)))[:, 0:1]


def row_of(first, second):
    both = jnp.concatenate([first, second], axis=0)
    return jnp.transpose(jnp.broadcast_to(both, (LANES, LANES)))[0:1]


def row_sum(first, second):
    return jnp.sum(first * second, axis=1, keepdims=True)


def levels(values, edges):
    return dot(values.astype(BF16), edges, 1, 1)


def by_lon(shift_by, first_ref, second_ref, write):
    bit = (lax.axis_index("lon") >> shift_by) & 1
    pl.when(bit == 0)(lambda: write(first_ref, second_ref))
    pl.when(bit == 1)(lambda: write(second_ref, first_ref))


def pick(shift_by, first, second):
    bit = (lax.axis_index("lon") >> shift_by) & 1
    keep = jnp.full((1, 1), bit, jnp.int32) == 0
    first, second = first.astype(F32), second.astype(F32)
    return jnp.where(keep, first, second).astype(BF16), jnp.where(keep, second, first).astype(BF16)


def lines(diag_ref):
    return tuple(diag_ref[i : i + 1, :] for i in range(5))


def load_kernel(count_ref, right_hbm, vectors_hbm, react_hbm, mass_hbm, obs_hbm, coupling_hbm, east_hbm, west_hbm,
                blocks_hbm, inverse_hbm,
                chunks_ref, diag_ref, edge_ref, near_ref, across_ref, right_ref, vectors_ref, blocks_ref, inverse_ref,
                react_ref, mass_ref, obs_ref, coupling_ref, east_ref, west_ref, sems):
    pairs = (
        (right_hbm, right_ref), (vectors_hbm, vectors_ref), (react_hbm, react_ref), (mass_hbm, mass_ref),
        (obs_hbm, obs_ref), (coupling_hbm, coupling_ref), (east_hbm, east_ref), (west_hbm, west_ref),
        (inverse_hbm, inverse_ref), (blocks_hbm, blocks_ref),
    )
    copies = [pltpu.make_async_copy(src, dst, sems.at[i]) for i, (src, dst) in enumerate(pairs)]
    for copy in copies:
        copy.start()
    for copy in copies[:9]:
        copy.wait()
    nodes = right_ref.shape[1]
    slots = coupling_ref.shape[0]
    active = (lax.broadcasted_iota(jnp.int32, (1, nodes), 1) < count_ref[0]).astype(F32)
    right = active * right_ref[...].astype(F32)
    coarse = fold(dot(vectors_ref[...], right.astype(BF16), 1, 1)).astype(BF16)
    chunks_ref[...] = jnp.broadcast_to(coarse[None], chunks_ref.shape)
    react, mass, obs = react_ref[...], mass_ref[...], obs_ref[...]
    inverse_mass, jacobi = 1.0 / mass, 1.0 / (obs + react * react / mass)
    row = lax.broadcasted_iota(jnp.int32, (8, nodes), 0)
    diag = jnp.zeros((8, nodes), F32)
    for i, line in enumerate((active, react, inverse_mass, obs, jacobi)):
        diag = jnp.where(row == i, line, diag)
    diag_ref[...] = diag

    node = lax.broadcasted_iota(jnp.int32, (slots, nodes), 1).astype(F32)
    east_hot = jnp.where(node == column_of(east_ref[...].astype(F32)), 1.0, 0.0).astype(BF16)
    west_hot = jnp.where(node == column_of(west_ref[...].astype(F32)), 1.0, 0.0).astype(BF16)
    live_a = lax.broadcasted_iota(jnp.int32, (slots, slots), 0) < count_ref[1]
    live_b = lax.broadcasted_iota(jnp.int32, (slots, slots), 1) < count_ref[1]
    link = jnp.where(live_a & live_b, coupling_ref[...], jnp.zeros((slots, slots), BF16))
    edges = jnp.concatenate([dot(link, east_hot, 0, 0).astype(BF16), west_hot], axis=0)
    edge_ref[...] = edges
    rows = [
        (edges.astype(F32) * inverse_mass).astype(BF16),
        vectors_ref[...] * active.astype(BF16),
        (jacobi * right).astype(BF16),
    ]
    level = dot(jnp.concatenate(rows, axis=0), edges, 1, 1).astype(BF16)
    kept, width = inverse_ref.shape
    fixed = width // LANES * kept

    def send(east_ref, west_ref):
        for ref, cols in ((east_ref, slice(0, slots)), (west_ref, slice(slots, 2 * slots))):
            for j in range(width // LANES):
                ref[j * kept : (j + 1) * kept, :] = inverse_ref[:, j * LANES : (j + 1) * LANES]
            ref[fixed:, :] = level[:, cols]

    by_lon(0, near_ref, across_ref, send)
    copies[9].wait()


def prep_kernel(pattern_hbm, blocks_ref, dense_ref, pattern_ref, total_ref, sem):
    copy = pltpu.make_async_copy(pattern_hbm, pattern_ref, sem)
    copy.start()
    nodes = dense_ref.shape[0]
    count, block, _ = blocks_ref.shape

    def clear(i, carry):
        total_ref[pl.ds(pl.multiple_of(i * block, block), block), :] = jnp.zeros((block, nodes), F32)
        return carry

    lax.fori_loop(0, nodes // block, clear, 0)
    copy.wait()
    unit = (
        lax.broadcasted_iota(jnp.int32, (block, block), 0) == lax.broadcasted_iota(jnp.int32, (block, block), 1)
    ).astype(F32).astype(BF16)

    def place(k, carry):
        rows = pl.ds(pl.multiple_of(pattern_ref[0, k] * block, block), block)
        cols = pl.ds(pl.multiple_of(pattern_ref[1, k] * block, block), block)
        values = blocks_ref[k]
        total_ref[rows, cols] += values.astype(F32)
        total_ref[cols, rows] += dot(unit, values, 1, 1)
        return carry

    lax.fori_loop(0, count, place, 0, unroll=8)

    def narrow(i, carry):
        rows = pl.ds(pl.multiple_of(i * block, block), block)
        dense_ref[rows, :] = total_ref[rows, :].astype(BF16)
        return carry

    lax.fori_loop(0, nodes // block, narrow, 0)


def unfold(count, piece, coarse_ref):
    half = coarse_ref.shape[0] // count // 4
    lat = lax.axis_index("lat")

    def move(d, carry):
        for side in range(2):
            values = piece(side, d)
            at = pl.multiple_of((2 * d + (lat if side == 0 else 1 - lat)) * 2 * half, 2 * half)
            coarse_ref[pl.ds(at, half), :] = values[:, 0 : LANES // 2]
            coarse_ref[pl.ds(at + half, half), :] = values[:, LANES // 2 :]
        return carry

    lax.fori_loop(0, count, move, 0, unroll=min(count, 8))


def smooth(field, coarse_ref, inverse_ref, vectors_ref, active, jacobi):
    fix = dot(inverse_ref[...], coarse_ref[...]).astype(BF16)
    return active * (field * jacobi + dot(fix, vectors_ref[...], 0, 0))


def start_kernel(pieces_ref, others_ref, inverse_ref, right_ref, vectors_ref, dense_ref, edge_ref, diag_ref,
                 z_ref, scaled_ref, own_ref, near_ref, across_ref, far_ref, beyond_ref, coarse_ref):
    samples, nodes = right_ref.shape
    unfold(pieces_ref.shape[0], lambda side, d: (pieces_ref, others_ref)[side][d], coarse_ref)
    active, react, inverse_mass, obs, jacobi = lines(diag_ref)
    z = smooth(right_ref[...].astype(F32), coarse_ref, inverse_ref, vectors_ref, active, jacobi)
    z_ref[...] = z
    edges = edge_ref[...]
    scaled = (dot(z.astype(BF16), dense_ref[...]) + react * z) * inverse_mass
    scaled_ref[...] = scaled
    level1 = levels(z, edges).astype(BF16)
    level2 = levels(scaled, edges).astype(BF16)
    own_ref[...] = level1
    slots = edges.shape[0] // 2

    def send(east_ref, west_ref):
        for ref, cols in ((east_ref, slice(0, slots)), (west_ref, slice(slots, 2 * slots))):
            ref[0:samples, :] = level1[:, cols]
            ref[samples:, :] = level2[:, cols]

    by_lon(0, near_ref, across_ref, send)
    by_lon(1, far_ref, beyond_ref, send)


def image_kernel(across_ref, beyond_ref, near_ref, far_ref, own_ref, across_corr_ref, near_corr_ref,
                 z_ref, scaled_ref, dense_ref, edge_ref, diag_ref, right_ref, vectors_ref,
                 image_ref, chunks_ref):
    samples, nodes = z_ref.shape
    active, react, inverse_mass, obs, jacobi = lines(diag_ref)
    z = z_ref[...]
    edges = edge_ref[...]
    from_east, from_west = pick(0, near_ref[...], across_ref[...])
    fixed = near_corr_ref.shape[0] - edges.shape[0] - vectors_ref.shape[0] - samples
    corr = slice(fixed, fixed + edges.shape[0])
    corr_east, corr_west = pick(0, near_corr_ref[corr, :], across_corr_ref[corr, :])
    beyond_east, beyond_west = pick(1, far_ref[0:samples, :], beyond_ref[0:samples, :])
    slots = edges.shape[0] // 2
    own_east, own_west = own_ref[:, 0:slots], own_ref[:, slots:]
    arrived = jnp.concatenate([from_east[0:samples], from_west[0:samples]], axis=1)
    inner = scaled_ref[...] + dot(arrived, edges) * inverse_mass
    east_terms = jnp.concatenate([beyond_east, own_east], axis=1)
    west_terms = jnp.concatenate([own_west, beyond_west], axis=1)
    second_east = from_east[samples:].astype(F32) + dot(east_terms, corr_east)
    second_west = from_west[samples:].astype(F32) + dot(west_terms, corr_west)
    arrived2 = jnp.concatenate([second_east, second_west], axis=1).astype(BF16)
    stiff = dot(inner.astype(BF16), dense_ref[...]) + dot(arrived2, edges) + react * inner
    image = active * (stiff + obs * z)
    image_ref[...] = image
    level = levels(image * jacobi, edges).astype(BF16)
    coarse = fold(dot(vectors_ref[...], image.astype(BF16), 1, 1))
    high = coarse.astype(BF16)
    low = (coarse - high.astype(F32)).astype(BF16)
    sums = row_of(row_sum(active * right_ref[...].astype(F32), z), row_sum(z, image))
    row = lax.broadcasted_iota(jnp.int32, (SUM_ROWS, LANES), 0)
    tail = jnp.zeros((SUM_ROWS, LANES), F32)
    for i in range(3):
        part = sums.astype(BF16).astype(F32)
        tail = jnp.where(row == i, part, tail)
        sums = sums - part
    count, rows, _ = chunks_ref.shape
    slots = level.shape[1] // 2
    common = jnp.concatenate([high, low, tail.astype(BF16), level[:, 0:slots]], axis=0)
    chunks_ref[...] = jnp.broadcast_to(common[None], chunks_ref.shape)
    before = lax.rem(lax.axis_index("lon") + count - 1, count)
    chunks_ref[before, rows - samples :, :] = level[:, slots:]


def middle_kernel(pieces_ref, others_ref, second_ref, second_others_ref,
                  across_ref, near_ref, inverse_ref, right_ref, image_ref, vectors_ref,
                  dense_ref, edge_ref, diag_ref, z_ref, sums_ref, chunks_ref, coarse_ref):
    samples, nodes = right_ref.shape
    count, half, _ = pieces_ref.shape
    tail = slice(2 * half, 2 * half + SUM_ROWS)

    def add(d, total):
        return total + second_ref[d, tail, :].astype(F32) + second_others_ref[d, tail, :].astype(F32)

    parts = lax.fori_loop(0, count, add, jnp.zeros((SUM_ROWS, LANES), F32), unroll=min(count, 8))
    sums = parts[2:3] + parts[1:2] + parts[0:1]
    step = sums[:, 0 : LANES // 2] / sums[:, LANES // 2 :]
    step = jnp.concatenate([step, step], axis=1)

    def piece(side, d):
        first, change = ((pieces_ref, second_ref), (others_ref, second_others_ref))[side]
        moved = change[d, 0:half, :].astype(F32) + change[d, half : 2 * half, :].astype(F32)
        return (first[d].astype(F32) - step * moved).astype(BF16)

    unfold(count, piece, coarse_ref)
    active, react, inverse_mass, obs, jacobi = lines(diag_ref)
    image = image_ref[...]
    edges = edge_ref[...]
    step_column = column_of(step)[0:samples]
    residual = active * right_ref[...].astype(F32) - step_column * image
    z = smooth(residual, coarse_ref, inverse_ref, vectors_ref, active, jacobi)
    z_ref[...] = z

    kept, width = inverse_ref.shape
    fixed = width // LANES * kept + edges.shape[0]

    def arriving(static, change):
        inverse = jnp.concatenate([static[j * kept : (j + 1) * kept] for j in range(width // LANES)], axis=1)
        fix = dot(inverse, coarse_ref[...]).astype(BF16)
        spread = dot(fix, static[fixed : fixed + kept], 0, 0)
        return (static[fixed + kept :].astype(F32) - step_column * change.astype(F32) + spread).astype(BF16)

    lon = lax.axis_index("lon")
    odd = lon & 1
    ahead, before = lax.rem(lon + 1, count), lax.rem(lon + count - 1, count)
    change = slice(2 * half + SUM_ROWS, second_ref.shape[1])
    from_near = arriving(near_ref[...], second_ref[ahead + odd * (before - ahead), change, :])
    from_across = arriving(across_ref[...], second_ref[before + odd * (ahead - before), change, :])
    from_east, from_west = pick(0, from_near, from_across)
    arrived = jnp.concatenate([from_east, from_west], axis=1)
    stiff = dot(z.astype(BF16), dense_ref[...]) + react * z + dot(arrived, edges)
    curve = jnp.sum(stiff * stiff * inverse_mass + obs * z * z, axis=1, keepdims=True)
    products = row_of(row_sum(residual, z), row_sum(z, image))
    row = lax.broadcasted_iota(jnp.int32, (8, LANES), 0)
    chunk = jnp.where(row == 0, products, row_of(curve, curve))
    chunks_ref[...] = jnp.broadcast_to(chunk[None], chunks_ref.shape)
    sums_ref[...] = jnp.broadcast_to(sums, sums_ref.shape)


def finish_kernel(sums_ref, chunks_ref, first_ref, second_ref, out_ref):
    samples = first_ref.shape[0]
    half = LANES // 2
    totals = jnp.sum(chunks_ref[...], axis=0)
    norm0, curve0 = sums_ref[1:2, 0:half], sums_ref[1:2, half:]
    norm1, cross = totals[0:1, 0:half], totals[0:1, half:]
    curve = totals[1:2, 0:half]
    beta = norm1 / norm0
    step0 = norm0 / curve0
    step1 = norm1 / (curve + beta * (2.0 * cross + beta * curve0))
    scales = column_of(jnp.concatenate([step0 + step1 * beta, step1], axis=1))
    out_ref[...] = scales[0:samples] * first_ref[...] + scales[samples : 2 * samples] * second_ref[...]


def exchange(chunks, axes):
    return lax.all_to_all(chunks, axes, split_axis=0, concat_axis=0, tiled=True)


def other_band(array):
    return lax.ppermute(array, "lat", [(0, 1), (1, 0)])


def swap(array, reach, inner):
    size = lax.axis_size("lon")
    pairs = []
    for i in range(size):
        up = (i // reach) % 2 == (0 if inner else 1)
        pairs.append((i, (i + (reach if up else -reach)) % size))
    return lax.ppermute(array, "lon", pairs)


def body(
    right_side,
    stiffness_blocks,
    block_pattern,
    reaction,
    lumped_mass,
    obs_precision,
    coupling,
    east_rows,
    west_rows,
    iface_count,
    node_count,
    deflation,
    coarse_inverse,
):
    samples, nodes = right_side.shape
    slots = coupling.shape[0]
    vectors = deflation.shape[0]
    sectors = lax.axis_size("lon")
    domains = sectors * lax.axis_size("lat")
    half = vectors // 2
    react, mass, obs = reaction[None], lumped_mass[None], obs_precision[None]
    field = ((samples, nodes), F32)
    coarse_scratch = pltpu.VMEM((domains * vectors, samples), BF16)
    apply_cost = 2 * samples * nodes * nodes
    static = ((coarse_inverse.size // LANES + 2 * slots + vectors + samples, slots), BF16)
    inputs = (right_side, deflation, react, mass, obs, coupling, east_rows, west_rows, stiffness_blocks, coarse_inverse)
    line = pltpu.VMEM((1, nodes), F32)
    chunks, diag, edge, near_static, across_static, right, basis, stored, inverse = call(
        load_kernel,
        [((sectors, half, LANES), BF16), ((8, nodes), F32), ((2 * slots, nodes), BF16), static, static]
        + [(a.shape, a.dtype) for a in (right_side, deflation, stiffness_blocks, coarse_inverse)],
        [SMEM] + [HBM] * len(inputs),
        [jnp.concatenate([node_count, iface_count])] + [pltpu.with_memory_space_constraint(a, pltpu.HBM) for a in inputs],
        2 * samples * vectors * nodes,
        [line, line, line] + [pltpu.VMEM(a.shape, a.dtype) for a in (coupling, east_rows, west_rows)]
        + [pltpu.SemaphoreType.DMA((len(inputs),))],
    )
    pieces, stored, across_static, near_static = lax.optimization_barrier(
        (exchange(chunks, "lon"), stored, swap(across_static, 1, False), swap(near_static, 1, True))
    )
    pattern = pltpu.with_memory_space_constraint(block_pattern.T, pltpu.HBM)
    (dense,) = call(
        prep_kernel,
        [((nodes, nodes), BF16)],
        [HBM, VMEM],
        (pattern, stored),
        apply_cost,
        [pltpu.SMEM((2, block_pattern.shape[0]), jnp.int32), pltpu.VMEM((nodes, nodes), F32), pltpu.SemaphoreType.DMA],
    )
    others = other_band(pieces)
    z0, scaled, own, near, across, far, beyond = call(
        start_kernel,
        [field] * 2 + [((samples, 2 * slots), BF16)] + [((2 * samples, slots), BF16)] * 4,
        [VMEM] * 8,
        (pieces, others, inverse, right, basis, dense, edge, diag),
        apply_cost,
        [coarse_scratch],
    )
    across = swap(across, 1, False)
    got_beyond = swap(beyond, 2, False)
    near = swap(near, 1, True)
    got_far = swap(far, 2, True)
    image, chunks = call(
        image_kernel,
        [field, ((sectors, 2 * half + SUM_ROWS + samples, LANES), BF16)],
        [VMEM] * 14,
        (across, got_beyond, near, got_far, own, across_static, near_static, z0, scaled, dense, edge, diag, right, basis),
        apply_cost,
    )
    second = exchange(chunks, "lon")
    second_others = other_band(second)
    z1, sums, chunks = call(
        middle_kernel,
        [field, ((8, LANES), F32), ((domains, 8, LANES), F32)],
        [VMEM] * 13,
        (pieces, others, second, second_others, across_static, near_static,
         inverse, right, image, basis, dense, edge, diag),
        apply_cost,
        [coarse_scratch],
    )
    totals = exchange(chunks, ("lon", "lat"))
    (out,) = call(finish_kernel, [field], [VMEM] * 4, (sums, totals, z0, z1), 4 * samples * nodes)
    return out


def solution(mesh):
    placed = (
        P(None, ("grp", "lon", "lat")),
        P(("grp", "lon", "lat"), None, None),
        P(("grp", "lon", "lat"), None),
        P(("grp", "lon", "lat")),
        P(("grp", "lon", "lat")),
        P(("grp", "lon", "lat")),
        P(("grp", "lon", "lat"), None),
        P(("grp", "lon", "lat"), None),
        P(("grp", "lon", "lat"), None),
        P(("grp", "lon", "lat")),
        P(("grp", "lon", "lat")),
        P(None, ("grp", "lon", "lat")),
        P(("grp", "lon", "lat"), None),
    )
    return jax.shard_map(
        body, mesh=mesh, in_specs=placed, out_specs=P(None, ("grp", "lon", "lat")), check_vma=False
    )
```

```python
import jax
import jax.numpy as jnp
import numpy as np
from jax import lax
from jax.experimental import pallas as pl
from jax.experimental.pallas import tpu as pltpu
from jax.sharding import PartitionSpec as P

F32 = jnp.float32
BF16 = jnp.bfloat16
VMEM = pl.BlockSpec(memory_space=pltpu.VMEM)
HBM = pl.BlockSpec(memory_space=pltpu.HBM)
SMEM = pl.BlockSpec(memory_space=pltpu.SMEM)
LANES = 128
SUM_ROWS = 16


def dot(a, b, ca=1, cb=0):
    return lax.dot_general(a, b, (((ca,), (cb,)), ((), ())), preferred_element_type=F32)


def call(kernel, outs, specs, args, flops, scratch=()):
    moved = sum(int(np.prod(a.shape)) * a.dtype.itemsize for a in args)
    return pl.pallas_call(
        kernel,
        out_shape=[jax.ShapeDtypeStruct(s, t) for s, t in outs],
        in_specs=specs,
        out_specs=[VMEM] * len(outs),
        scratch_shapes=list(scratch),
        compiler_params=pltpu.CompilerParams(vmem_limit_bytes=32 * 1024 * 1024),
        cost_estimate=pl.CostEstimate(flops=flops, bytes_accessed=moved, transcendentals=0),
    )(*args)


def fold(values):
    half = values.shape[0] // 2
    return jnp.concatenate([values[:half], values[half:]], axis=1)


def column_of(row):
    return jnp.transpose(jnp.broadcast_to(row, (LANES, LANES)))[:, 0:1]


def row_of(first, second):
    both = jnp.concatenate([first, second], axis=0)
    return jnp.transpose(jnp.broadcast_to(both, (LANES, LANES)))[0:1]


def row_sum(first, second):
    return jnp.sum(first * second, axis=1, keepdims=True)


def levels(values, edges):
    return dot(values.astype(BF16), edges, 1, 1)


def by_lon(shift_by, first_ref, second_ref, write):
    bit = (lax.axis_index("lon") >> shift_by) & 1
    pl.when(bit == 0)(lambda: write(first_ref, second_ref))
    pl.when(bit == 1)(lambda: write(second_ref, first_ref))


def pick(shift_by, first, second):
    bit = (lax.axis_index("lon") >> shift_by) & 1
    keep = jnp.full((1, 1), bit, jnp.int32) == 0
    first, second = first.astype(F32), second.astype(F32)
    return jnp.where(keep, first, second).astype(BF16), jnp.where(keep, second, first).astype(BF16)


def lines(diag_ref):
    return tuple(diag_ref[i : i + 1, :] for i in range(5))


def load_kernel(node_count_ref, iface_count_ref, coupling_hbm, east_hbm, west_hbm, react_hbm, mass_hbm, obs_hbm,
                right_hbm, vectors_hbm, inverse_hbm, blocks_hbm,
                chunks_ref, diag_ref, edge_ref, near_ref, across_ref, right_ref, vectors_ref, blocks_ref,
                inverse_ref, react_ref, mass_ref, obs_ref, coupling_ref, east_ref, west_ref, sems):
    pairs = (
        (coupling_hbm, coupling_ref), (east_hbm, east_ref), (west_hbm, west_ref), (react_hbm, react_ref),
        (mass_hbm, mass_ref), (obs_hbm, obs_ref), (right_hbm, right_ref), (vectors_hbm, vectors_ref),
        (inverse_hbm, inverse_ref), (blocks_hbm, blocks_ref),
    )
    copies = [pltpu.make_async_copy(src, dst, sems.at[i]) for i, (src, dst) in enumerate(pairs)]
    for copy in copies:
        copy.start()
    nodes = right_ref.shape[1]
    slots = coupling_ref.shape[0]
    for copy in copies[:6]:
        copy.wait()
    active = (lax.broadcasted_iota(jnp.int32, (1, nodes), 1) < node_count_ref[0]).astype(F32)
    react, mass, obs = react_ref[...], mass_ref[...], obs_ref[...]
    inverse_mass, jacobi = 1.0 / mass, 1.0 / (obs + react * react / mass)
    row = lax.broadcasted_iota(jnp.int32, (8, nodes), 0)
    diag = jnp.zeros((8, nodes), F32)
    for i, line in enumerate((active, react, inverse_mass, obs, jacobi)):
        diag = jnp.where(row == i, line, diag)
    diag_ref[...] = diag

    node = lax.broadcasted_iota(jnp.int32, (slots, nodes), 1).astype(F32)
    east_hot = jnp.where(node == column_of(east_ref[...].astype(F32)), 1.0, 0.0).astype(BF16)
    west_hot = jnp.where(node == column_of(west_ref[...].astype(F32)), 1.0, 0.0).astype(BF16)
    live_a = lax.broadcasted_iota(jnp.int32, (slots, slots), 0) < iface_count_ref[0]
    live_b = lax.broadcasted_iota(jnp.int32, (slots, slots), 1) < iface_count_ref[0]
    link = jnp.where(live_a & live_b, coupling_ref[...], jnp.zeros((slots, slots), BF16))
    edges = jnp.concatenate([dot(link, east_hot, 0, 0).astype(BF16), west_hot], axis=0)
    edge_ref[...] = edges
    for copy in copies[6:9]:
        copy.wait()
    right = active * right_ref[...].astype(F32)
    coarse = fold(dot(vectors_ref[...], right.astype(BF16), 1, 1)).astype(BF16)
    chunks_ref[...] = jnp.broadcast_to(coarse[None], chunks_ref.shape)
    rows = [
        (edges.astype(F32) * inverse_mass).astype(BF16),
        vectors_ref[...] * active.astype(BF16),
        (jacobi * right).astype(BF16),
    ]
    level = dot(jnp.concatenate(rows, axis=0), edges, 1, 1).astype(BF16)
    kept, width = inverse_ref.shape
    fixed = width // LANES * kept

    def send(east_ref, west_ref):
        for ref, cols in ((east_ref, slice(0, slots)), (west_ref, slice(slots, 2 * slots))):
            for j in range(width // LANES):
                ref[j * kept : (j + 1) * kept, :] = inverse_ref[:, j * LANES : (j + 1) * LANES]
            ref[fixed:, :] = level[:, cols]

    by_lon(0, near_ref, across_ref, send)
    copies[9].wait()


def prep_kernel(pattern_hbm, blocks_ref, dense_ref, pattern_ref, total_ref, sem):
    copy = pltpu.make_async_copy(pattern_hbm, pattern_ref, sem)
    copy.start()
    nodes = dense_ref.shape[0]
    count, block, _ = blocks_ref.shape

    def clear(i, carry):
        total_ref[pl.ds(pl.multiple_of(i * block, block), block), :] = jnp.zeros((block, nodes), F32)
        return carry

    lax.fori_loop(0, nodes // block, clear, 0)
    copy.wait()
    unit = (
        lax.broadcasted_iota(jnp.int32, (block, block), 0) == lax.broadcasted_iota(jnp.int32, (block, block), 1)
    ).astype(F32).astype(BF16)

    def place(k, carry):
        rows = pl.ds(pl.multiple_of(pattern_ref[0, k] * block, block), block)
        cols = pl.ds(pl.multiple_of(pattern_ref[1, k] * block, block), block)
        values = blocks_ref[k]
        total_ref[rows, cols] += values.astype(F32)
        total_ref[cols, rows] += dot(unit, values, 1, 1)
        return carry

    lax.fori_loop(0, count, place, 0, unroll=8)

    def narrow(i, carry):
        rows = pl.ds(pl.multiple_of(i * block, block), block)
        dense_ref[rows, :] = total_ref[rows, :].astype(BF16)
        return carry

    lax.fori_loop(0, nodes // block, narrow, 0)


def unfold(count, piece, coarse_ref):
    half = coarse_ref.shape[0] // count // 4
    lat = lax.axis_index("lat")

    def move(d, carry):
        for side in range(2):
            values = piece(side, d)
            at = pl.multiple_of((2 * d + (lat if side == 0 else 1 - lat)) * 2 * half, 2 * half)
            coarse_ref[pl.ds(at, half), :] = values[:, 0 : LANES // 2]
            coarse_ref[pl.ds(at + half, half), :] = values[:, LANES // 2 :]
        return carry

    lax.fori_loop(0, count, move, 0, unroll=min(count, 8))


def smooth(field, coarse_ref, inverse_ref, vectors_ref, active, jacobi):
    fix = dot(inverse_ref[...], coarse_ref[...]).astype(BF16)
    return active * (field * jacobi + dot(fix, vectors_ref[...], 0, 0))


def start_kernel(pieces_ref, others_ref, inverse_ref, right_ref, vectors_ref, dense_ref, edge_ref, diag_ref,
                 z_ref, scaled_ref, near_ref, across_ref, far_ref, beyond_ref, coarse_ref):
    samples, nodes = right_ref.shape
    unfold(pieces_ref.shape[0], lambda side, d: (pieces_ref, others_ref)[side][d], coarse_ref)
    active, react, inverse_mass, obs, jacobi = lines(diag_ref)
    z = smooth(right_ref[...].astype(F32), coarse_ref, inverse_ref, vectors_ref, active, jacobi)
    z_ref[...] = z
    edges = edge_ref[...]
    scaled = (dot(z.astype(BF16), dense_ref[...]) + react * z) * inverse_mass
    scaled_ref[...] = scaled
    level1 = levels(z, edges).astype(BF16)
    level2 = levels(scaled, edges).astype(BF16)
    slots = edges.shape[0] // 2

    def send(east_ref, west_ref):
        for ref, cols in ((east_ref, slice(0, slots)), (west_ref, slice(slots, 2 * slots))):
            ref[0:samples, :] = level1[:, cols]
            ref[samples:, :] = level2[:, cols]

    def send_far(east_ref, west_ref):
        east_ref[...] = level1[:, 0:slots]
        west_ref[...] = level1[:, slots:]

    by_lon(0, near_ref, across_ref, send)
    by_lon(1, far_ref, beyond_ref, send_far)


def image_kernel(across_ref, beyond_ref, near_ref, far_ref, own_far_ref, own_beyond_ref, across_corr_ref, near_corr_ref,
                 z_ref, scaled_ref, dense_ref, edge_ref, diag_ref, right_ref, vectors_ref,
                 image_ref, chunks_ref):
    samples, nodes = z_ref.shape
    active, react, inverse_mass, obs, jacobi = lines(diag_ref)
    z = z_ref[...]
    edges = edge_ref[...]
    from_east, from_west = pick(0, near_ref[...], across_ref[...])
    fixed = near_corr_ref.shape[0] - edges.shape[0] - vectors_ref.shape[0] - samples
    corr = slice(fixed, fixed + edges.shape[0])
    corr_east, corr_west = pick(0, near_corr_ref[corr, :], across_corr_ref[corr, :])
    beyond_east, beyond_west = pick(1, far_ref[...], beyond_ref[...])
    own_east, own_west = pick(1, own_far_ref[...], own_beyond_ref[...])
    arrived = jnp.concatenate([from_east[0:samples], from_west[0:samples]], axis=1)
    inner = scaled_ref[...] + dot(arrived, edges) * inverse_mass
    east_terms = jnp.concatenate([beyond_east, own_east], axis=1)
    west_terms = jnp.concatenate([own_west, beyond_west], axis=1)
    second_east = from_east[samples:].astype(F32) + dot(east_terms, corr_east)
    second_west = from_west[samples:].astype(F32) + dot(west_terms, corr_west)
    arrived2 = jnp.concatenate([second_east, second_west], axis=1).astype(BF16)
    stiff = dot(inner.astype(BF16), dense_ref[...]) + dot(arrived2, edges) + react * inner
    image = active * (stiff + obs * z)
    image_ref[...] = image
    level = levels(image * jacobi, edges).astype(BF16)
    coarse = fold(dot(vectors_ref[...], image.astype(BF16), 1, 1))
    high = coarse.astype(BF16)
    low = (coarse - high.astype(F32)).astype(BF16)
    sums = row_of(row_sum(active * right_ref[...].astype(F32), z), row_sum(z, image))
    row = lax.broadcasted_iota(jnp.int32, (SUM_ROWS, LANES), 0)
    tail = jnp.zeros((SUM_ROWS, LANES), F32)
    for i in range(3):
        part = sums.astype(BF16).astype(F32)
        tail = jnp.where(row == i, part, tail)
        sums = sums - part
    count, rows, _ = chunks_ref.shape
    slots = level.shape[1] // 2
    common = jnp.concatenate([high, low, tail.astype(BF16), level[:, 0:slots]], axis=0)
    chunks_ref[...] = jnp.broadcast_to(common[None], chunks_ref.shape)
    before = lax.rem(lax.axis_index("lon") + count - 1, count)
    chunks_ref[before, rows - samples :, :] = level[:, slots:]


def middle_kernel(pieces_ref, others_ref, second_ref, second_others_ref,
                  across_ref, near_ref, inverse_ref, right_ref, image_ref, vectors_ref,
                  dense_ref, edge_ref, diag_ref, z_ref, sums_ref, chunks_ref, coarse_ref):
    samples, nodes = right_ref.shape
    count, half, _ = pieces_ref.shape
    tail = slice(2 * half, 2 * half + SUM_ROWS)

    def add(d, total):
        return total + second_ref[d, tail, :].astype(F32) + second_others_ref[d, tail, :].astype(F32)

    parts = lax.fori_loop(0, count, add, jnp.zeros((SUM_ROWS, LANES), F32), unroll=min(count, 8))
    sums = parts[2:3] + parts[1:2] + parts[0:1]
    step = sums[:, 0 : LANES // 2] / sums[:, LANES // 2 :]
    step = jnp.concatenate([step, step], axis=1)

    def piece(side, d):
        first, change = ((pieces_ref, second_ref), (others_ref, second_others_ref))[side]
        moved = change[d, 0:half, :].astype(F32) + change[d, half : 2 * half, :].astype(F32)
        return (first[d].astype(F32) - step * moved).astype(BF16)

    unfold(count, piece, coarse_ref)
    active, react, inverse_mass, obs, jacobi = lines(diag_ref)
    image = image_ref[...]
    edges = edge_ref[...]
    step_column = column_of(step)[0:samples]
    residual = active * right_ref[...].astype(F32) - step_column * image
    z = smooth(residual, coarse_ref, inverse_ref, vectors_ref, active, jacobi)
    z_ref[...] = z

    kept, width = inverse_ref.shape
    fixed = width // LANES * kept + edges.shape[0]

    def arriving(static, change):
        inverse = jnp.concatenate([static[j * kept : (j + 1) * kept] for j in range(width // LANES)], axis=1)
        fix = dot(inverse, coarse_ref[...]).astype(BF16)
        spread = dot(fix, static[fixed : fixed + kept], 0, 0)
        return (static[fixed + kept :].astype(F32) - step_column * change.astype(F32) + spread).astype(BF16)

    lon = lax.axis_index("lon")
    odd = lon & 1
    ahead, before = lax.rem(lon + 1, count), lax.rem(lon + count - 1, count)
    change = slice(2 * half + SUM_ROWS, second_ref.shape[1])
    from_near = arriving(near_ref[...], second_ref[ahead + odd * (before - ahead), change, :])
    from_across = arriving(across_ref[...], second_ref[before + odd * (ahead - before), change, :])
    from_east, from_west = pick(0, from_near, from_across)
    arrived = jnp.concatenate([from_east, from_west], axis=1)
    stiff = dot(z.astype(BF16), dense_ref[...]) + react * z + dot(arrived, edges)
    curve = jnp.sum(stiff * stiff * inverse_mass + obs * z * z, axis=1, keepdims=True)
    products = row_of(row_sum(residual, z), row_sum(z, image))
    row = lax.broadcasted_iota(jnp.int32, (8, LANES), 0)
    chunk = jnp.where(row == 0, products, row_of(curve, curve))
    chunks_ref[...] = jnp.broadcast_to(chunk[None], chunks_ref.shape)
    sums_ref[...] = jnp.broadcast_to(sums, sums_ref.shape)


def finish_kernel(sums_ref, chunks_ref, first_ref, second_ref, out_ref):
    samples = first_ref.shape[0]
    half = LANES // 2
    totals = jnp.sum(chunks_ref[...], axis=0)
    norm0, curve0 = sums_ref[1:2, 0:half], sums_ref[1:2, half:]
    norm1, cross = totals[0:1, 0:half], totals[0:1, half:]
    curve = totals[1:2, 0:half]
    beta = norm1 / norm0
    step0 = norm0 / curve0
    step1 = norm1 / (curve + beta * (2.0 * cross + beta * curve0))
    scales = column_of(jnp.concatenate([step0 + step1 * beta, step1], axis=1))
    out_ref[...] = scales[0:samples] * first_ref[...] + scales[samples : 2 * samples] * second_ref[...]


def exchange(chunks, axes):
    return lax.all_to_all(chunks, axes, split_axis=0, concat_axis=0, tiled=True)


def other_band(array):
    return lax.ppermute(array, "lat", [(0, 1), (1, 0)])


def swap(array, reach, inner):
    size = lax.axis_size("lon")
    pairs = []
    for i in range(size):
        up = (i // reach) % 2 == (0 if inner else 1)
        pairs.append((i, (i + (reach if up else -reach)) % size))
    return lax.ppermute(array, "lon", pairs)


def body(
    right_side,
    stiffness_blocks,
    block_pattern,
    reaction,
    lumped_mass,
    obs_precision,
    coupling,
    east_rows,
    west_rows,
    iface_count,
    node_count,
    deflation,
    coarse_inverse,
):
    samples, nodes = right_side.shape
    slots = coupling.shape[0]
    vectors = deflation.shape[0]
    sectors = lax.axis_size("lon")
    domains = sectors * lax.axis_size("lat")
    half = vectors // 2
    react, mass, obs = reaction[None], lumped_mass[None], obs_precision[None]
    field = ((samples, nodes), F32)
    coarse_scratch = pltpu.VMEM((domains * vectors, samples), BF16)
    apply_cost = 2 * samples * nodes * nodes
    static = ((coarse_inverse.size // LANES + 2 * slots + vectors + samples, slots), BF16)
    inputs = (coupling, east_rows, west_rows, react, mass, obs, right_side, deflation, coarse_inverse, stiffness_blocks)
    line = pltpu.VMEM((1, nodes), F32)
    chunks, diag, edge, near_static, across_static, right, basis, stored, inverse = call(
        load_kernel,
        [((sectors, half, LANES), BF16), ((8, nodes), F32), ((2 * slots, nodes), BF16), static, static]
        + [(a.shape, a.dtype) for a in (right_side, deflation, stiffness_blocks, coarse_inverse)],
        [SMEM, SMEM] + [HBM] * len(inputs),
        [node_count, iface_count] + [pltpu.with_memory_space_constraint(a, pltpu.HBM) for a in inputs],
        2 * samples * vectors * nodes,
        [line, line, line] + [pltpu.VMEM(a.shape, a.dtype) for a in (coupling, east_rows, west_rows)]
        + [pltpu.SemaphoreType.DMA((len(inputs),))],
    )
    pieces, stored, across_static, near_static = lax.optimization_barrier(
        (exchange(chunks, "lon"), stored, swap(across_static, 1, False), swap(near_static, 1, True))
    )
    pattern = pltpu.with_memory_space_constraint(block_pattern.T, pltpu.HBM)
    (dense,) = call(
        prep_kernel,
        [((nodes, nodes), BF16)],
        [HBM, VMEM],
        (pattern, stored),
        apply_cost,
        [pltpu.SMEM((2, block_pattern.shape[0]), jnp.int32), pltpu.VMEM((nodes, nodes), F32), pltpu.SemaphoreType.DMA],
    )
    others = other_band(pieces)
    z0, scaled, near, across, far, beyond = call(
        start_kernel,
        [field] * 2 + [((2 * samples, slots), BF16)] * 2 + [((samples, slots), BF16)] * 2,
        [VMEM] * 8,
        (pieces, others, inverse, right, basis, dense, edge, diag),
        apply_cost,
        [coarse_scratch],
    )
    across = swap(across, 1, False)
    got_beyond = swap(beyond, 2, False)
    near = swap(near, 1, True)
    got_far = swap(far, 2, True)
    image, chunks = call(
        image_kernel,
        [field, ((sectors, 2 * half + SUM_ROWS + samples, LANES), BF16)],
        [VMEM] * 15,
        (across, got_beyond, near, got_far, far, beyond, across_static, near_static, z0, scaled, dense, edge, diag, right, basis),
        apply_cost,
    )
    second = exchange(chunks, "lon")
    second_others = other_band(second)
    z1, sums, chunks = call(
        middle_kernel,
        [field, ((8, LANES), F32), ((domains, 8, LANES), F32)],
        [VMEM] * 13,
        (pieces, others, second, second_others, across_static, near_static,
         inverse, right, image, basis, dense, edge, diag),
        apply_cost,
        [coarse_scratch],
    )
    totals = exchange(chunks, ("lon", "lat"))
    (out,) = call(finish_kernel, [field], [VMEM] * 4, (sums, totals, z0, z1), 4 * samples * nodes)
    return out


def solution(mesh):
    placed = (
        P(None, ("grp", "lon", "lat")),
        P(("grp", "lon", "lat"), None, None),
        P(("grp", "lon", "lat"), None),
        P(("grp", "lon", "lat")),
        P(("grp", "lon", "lat")),
        P(("grp", "lon", "lat")),
        P(("grp", "lon", "lat"), None),
        P(("grp", "lon", "lat"), None),
        P(("grp", "lon", "lat"), None),
        P(("grp", "lon", "lat")),
        P(("grp", "lon", "lat")),
        P(None, ("grp", "lon", "lat")),
        P(("grp", "lon", "lat"), None),
    )
    return jax.shard_map(
        body, mesh=mesh, in_specs=placed, out_specs=P(None, ("grp", "lon", "lat")), check_vma=False
    )
```

```python
import jax
import jax.numpy as jnp
import numpy as np
from jax import lax
from jax.experimental import pallas as pl
from jax.experimental.pallas import tpu as pltpu
from jax.sharding import PartitionSpec as P

F32 = jnp.float32
BF16 = jnp.bfloat16
VMEM = pl.BlockSpec(memory_space=pltpu.VMEM)
HBM = pl.BlockSpec(memory_space=pltpu.HBM)
SMEM = pl.BlockSpec(memory_space=pltpu.SMEM)
LANES = 128
SUM_ROWS = 16


def dot(a, b, ca=1, cb=0):
    return lax.dot_general(a, b, (((ca,), (cb,)), ((), ())), preferred_element_type=F32)


def call(kernel, outs, specs, args, flops, scratch=()):
    moved = sum(int(np.prod(a.shape)) * a.dtype.itemsize for a in args)
    return pl.pallas_call(
        kernel,
        out_shape=[jax.ShapeDtypeStruct(s, t) for s, t in outs],
        in_specs=specs,
        out_specs=[VMEM] * len(outs),
        scratch_shapes=list(scratch),
        compiler_params=pltpu.CompilerParams(vmem_limit_bytes=32 * 1024 * 1024),
        cost_estimate=pl.CostEstimate(flops=flops, bytes_accessed=moved, transcendentals=0),
    )(*args)


def fold(values):
    half = values.shape[0] // 2
    return jnp.concatenate([values[:half], values[half:]], axis=1)


def column_of(row):
    return jnp.transpose(jnp.broadcast_to(row, (LANES, LANES)))[:, 0:1]


def row_of(first, second):
    both = jnp.concatenate([first, second], axis=0)
    return jnp.transpose(jnp.broadcast_to(both, (LANES, LANES)))[0:1]


def row_sum(first, second):
    return jnp.sum(first * second, axis=1, keepdims=True)


def levels(values, edges):
    return dot(values.astype(BF16), edges, 1, 1)


def by_lon(shift_by, first_ref, second_ref, write):
    bit = (lax.axis_index("lon") >> shift_by) & 1
    pl.when(bit == 0)(lambda: write(first_ref, second_ref))
    pl.when(bit == 1)(lambda: write(second_ref, first_ref))


def pick(shift_by, first, second):
    bit = (lax.axis_index("lon") >> shift_by) & 1
    keep = jnp.full((1, 1), bit, jnp.int32) == 0
    first, second = first.astype(F32), second.astype(F32)
    return jnp.where(keep, first, second).astype(BF16), jnp.where(keep, second, first).astype(BF16)


def lines(diag_ref):
    return tuple(diag_ref[i : i + 1, :] for i in range(5))


def load_kernel(node_count_ref, iface_count_ref, coupling_hbm, east_hbm, west_hbm, react_hbm, mass_hbm, obs_hbm,
                right_hbm, vectors_hbm, inverse_hbm, blocks_hbm,
                chunks_ref, diag_ref, edge_ref, near_ref, across_ref, right_ref, vectors_ref, blocks_ref,
                inverse_ref, react_ref, mass_ref, obs_ref, coupling_ref, east_ref, west_ref, sems):
    pairs = (
        (coupling_hbm, coupling_ref), (east_hbm, east_ref), (west_hbm, west_ref), (react_hbm, react_ref),
        (mass_hbm, mass_ref), (obs_hbm, obs_ref), (right_hbm, right_ref), (vectors_hbm, vectors_ref),
        (inverse_hbm, inverse_ref), (blocks_hbm, blocks_ref),
    )
    copies = [pltpu.make_async_copy(src, dst, sems.at[i]) for i, (src, dst) in enumerate(pairs)]
    for copy in copies:
        copy.start()
    nodes = right_ref.shape[1]
    slots = coupling_ref.shape[0]
    for copy in copies[:6]:
        copy.wait()
    active = (lax.broadcasted_iota(jnp.int32, (1, nodes), 1) < node_count_ref[0]).astype(F32)
    react, mass, obs = react_ref[...], mass_ref[...], obs_ref[...]
    inverse_mass, jacobi = 1.0 / mass, 1.0 / (obs + react * react / mass)
    row = lax.broadcasted_iota(jnp.int32, (8, nodes), 0)
    diag = jnp.zeros((8, nodes), F32)
    for i, line in enumerate((active, react, inverse_mass, obs, jacobi)):
        diag = jnp.where(row == i, line, diag)
    diag_ref[...] = diag

    node = lax.broadcasted_iota(jnp.int32, (slots, nodes), 1).astype(F32)
    east_hot = jnp.where(node == column_of(east_ref[...].astype(F32)), 1.0, 0.0).astype(BF16)
    west_hot = jnp.where(node == column_of(west_ref[...].astype(F32)), 1.0, 0.0).astype(BF16)
    live_a = lax.broadcasted_iota(jnp.int32, (slots, slots), 0) < iface_count_ref[0]
    live_b = lax.broadcasted_iota(jnp.int32, (slots, slots), 1) < iface_count_ref[0]
    link = jnp.where(live_a & live_b, coupling_ref[...], jnp.zeros((slots, slots), BF16))
    edges = jnp.concatenate([dot(link, east_hot, 0, 0).astype(BF16), west_hot], axis=0)
    edge_ref[...] = edges
    for copy in copies[6:9]:
        copy.wait()
    right = active * right_ref[...].astype(F32)
    coarse = fold(dot(vectors_ref[...], right.astype(BF16), 1, 1)).astype(BF16)
    chunks_ref[...] = jnp.broadcast_to(coarse[None], chunks_ref.shape)
    rows = [
        (edges.astype(F32) * inverse_mass).astype(BF16),
        vectors_ref[...] * active.astype(BF16),
        (jacobi * right).astype(BF16),
    ]
    level = dot(jnp.concatenate(rows, axis=0), edges, 1, 1).astype(BF16)
    kept, width = inverse_ref.shape
    fixed = width // LANES * kept

    def send(east_ref, west_ref):
        for ref, cols in ((east_ref, slice(0, slots)), (west_ref, slice(slots, 2 * slots))):
            for j in range(width // LANES):
                ref[j * kept : (j + 1) * kept, :] = inverse_ref[:, j * LANES : (j + 1) * LANES]
            ref[fixed:, :] = level[:, cols]

    by_lon(0, near_ref, across_ref, send)
    copies[9].wait()


def prep_kernel(pattern_hbm, blocks_ref, dense_ref, pattern_ref, total_ref, sem):
    copy = pltpu.make_async_copy(pattern_hbm, pattern_ref, sem)
    copy.start()
    nodes = dense_ref.shape[0]
    count, block, _ = blocks_ref.shape

    def clear(i, carry):
        total_ref[pl.ds(pl.multiple_of(i * block, block), block), :] = jnp.zeros((block, nodes), F32)
        return carry

    lax.fori_loop(0, nodes // block, clear, 0)
    copy.wait()
    unit = (
        lax.broadcasted_iota(jnp.int32, (block, block), 0) == lax.broadcasted_iota(jnp.int32, (block, block), 1)
    ).astype(F32).astype(BF16)

    def place(k, carry):
        rows = pl.ds(pl.multiple_of(pattern_ref[0, k] * block, block), block)
        cols = pl.ds(pl.multiple_of(pattern_ref[1, k] * block, block), block)
        values = blocks_ref[k]
        total_ref[rows, cols] += values.astype(F32)
        total_ref[cols, rows] += dot(unit, values, 1, 1)
        return carry

    lax.fori_loop(0, count, place, 0, unroll=True)

    def narrow(i, carry):
        rows = pl.ds(pl.multiple_of(i * block, block), block)
        dense_ref[rows, :] = total_ref[rows, :].astype(BF16)
        return carry

    lax.fori_loop(0, nodes // block, narrow, 0)


def unfold(count, piece, coarse_ref):
    half = coarse_ref.shape[0] // count // 4
    lat = lax.axis_index("lat")

    def move(d, carry):
        for side in range(2):
            values = piece(side, d)
            at = pl.multiple_of((2 * d + (lat if side == 0 else 1 - lat)) * 2 * half, 2 * half)
            coarse_ref[pl.ds(at, half), :] = values[:, 0 : LANES // 2]
            coarse_ref[pl.ds(at + half, half), :] = values[:, LANES // 2 :]
        return carry

    lax.fori_loop(0, count, move, 0, unroll=min(count, 8))


def smooth(field, coarse_ref, inverse_ref, vectors_ref, active, jacobi):
    fix = dot(inverse_ref[...], coarse_ref[...]).astype(BF16)
    return active * (field * jacobi + dot(fix, vectors_ref[...], 0, 0))


def start_kernel(pieces_ref, others_ref, inverse_ref, right_ref, vectors_ref, dense_ref, edge_ref, diag_ref,
                 z_ref, scaled_ref, near_ref, across_ref, far_ref, beyond_ref, coarse_ref):
    samples, nodes = right_ref.shape
    unfold(pieces_ref.shape[0], lambda side, d: (pieces_ref, others_ref)[side][d], coarse_ref)
    active, react, inverse_mass, obs, jacobi = lines(diag_ref)
    z = smooth(right_ref[...].astype(F32), coarse_ref, inverse_ref, vectors_ref, active, jacobi)
    z_ref[...] = z
    edges = edge_ref[...]
    scaled = (dot(z.astype(BF16), dense_ref[...]) + react * z) * inverse_mass
    scaled_ref[...] = scaled
    level = levels(jnp.concatenate([z, scaled], axis=0), edges).astype(BF16)
    level1, level2 = level[0:samples], level[samples:]
    slots = edges.shape[0] // 2

    def send(east_ref, west_ref):
        for ref, cols in ((east_ref, slice(0, slots)), (west_ref, slice(slots, 2 * slots))):
            ref[0:samples, :] = level1[:, cols]
            ref[samples:, :] = level2[:, cols]

    def send_far(east_ref, west_ref):
        east_ref[...] = level1[:, 0:slots]
        west_ref[...] = level1[:, slots:]

    by_lon(0, near_ref, across_ref, send)
    by_lon(1, far_ref, beyond_ref, send_far)


def image_kernel(across_ref, beyond_ref, near_ref, far_ref, own_far_ref, own_beyond_ref, across_corr_ref, near_corr_ref,
                 z_ref, scaled_ref, dense_ref, edge_ref, diag_ref, right_ref, vectors_ref,
                 image_ref, chunks_ref):
    samples, nodes = z_ref.shape
    active, react, inverse_mass, obs, jacobi = lines(diag_ref)
    z = z_ref[...]
    edges = edge_ref[...]
    fixed = near_corr_ref.shape[0] - edges.shape[0] - vectors_ref.shape[0] - samples
    corr = slice(fixed, fixed + edges.shape[0])
    arrived = jnp.concatenate(pick(0, near_ref[0:samples, :], across_ref[0:samples, :]), axis=1)
    inner = scaled_ref[...] + dot(arrived, edges) * inverse_mass
    beyond_east, beyond_west = pick(1, far_ref[...], beyond_ref[...])
    own_east, own_west = pick(1, own_far_ref[...], own_beyond_ref[...])
    near_terms, across_terms = pick(
        0,
        jnp.concatenate([beyond_east, own_east], axis=1),
        jnp.concatenate([own_west, beyond_west], axis=1),
    )
    second_near = near_ref[samples:, :].astype(F32) + dot(near_terms, near_corr_ref[corr, :])
    second_across = across_ref[samples:, :].astype(F32) + dot(across_terms, across_corr_ref[corr, :])
    arrived2 = jnp.concatenate(pick(0, second_near, second_across), axis=1)
    stiff = dot(inner.astype(BF16), dense_ref[...]) + dot(arrived2, edges) + react * inner
    image = active * (stiff + obs * z)
    image_ref[...] = image
    level = levels(image * jacobi, edges).astype(BF16)
    coarse = fold(dot(vectors_ref[...], image.astype(BF16), 1, 1))
    high = coarse.astype(BF16)
    low = (coarse - high.astype(F32)).astype(BF16)
    sums = row_of(row_sum(active * right_ref[...].astype(F32), z), row_sum(z, image))
    row = lax.broadcasted_iota(jnp.int32, (SUM_ROWS, LANES), 0)
    tail = jnp.zeros((SUM_ROWS, LANES), F32)
    for i in range(3):
        part = sums.astype(BF16).astype(F32)
        tail = jnp.where(row == i, part, tail)
        sums = sums - part
    count, rows, _ = chunks_ref.shape
    slots = level.shape[1] // 2
    common = jnp.concatenate([high, low, tail.astype(BF16), level[:, 0:slots]], axis=0)
    chunks_ref[...] = jnp.broadcast_to(common[None], chunks_ref.shape)
    before = lax.rem(lax.axis_index("lon") + count - 1, count)
    chunks_ref[before, rows - samples :, :] = level[:, slots:]


def middle_kernel(pieces_ref, others_ref, second_ref, second_others_ref,
                  across_ref, near_ref, inverse_ref, right_ref, image_ref, vectors_ref,
                  dense_ref, edge_ref, diag_ref, z_ref, sums_ref, chunks_ref, coarse_ref):
    samples, nodes = right_ref.shape
    count, half, _ = pieces_ref.shape
    tail = slice(2 * half, 2 * half + SUM_ROWS)

    def add(d, total):
        return total + second_ref[d, tail, :].astype(F32) + second_others_ref[d, tail, :].astype(F32)

    parts = lax.fori_loop(0, count, add, jnp.zeros((SUM_ROWS, LANES), F32), unroll=min(count, 8))
    sums = parts[2:3] + parts[1:2] + parts[0:1]
    step = sums[:, 0 : LANES // 2] / sums[:, LANES // 2 :]
    step = jnp.concatenate([step, step], axis=1)

    def piece(side, d):
        first, change = ((pieces_ref, second_ref), (others_ref, second_others_ref))[side]
        moved = change[d, 0:half, :].astype(F32) + change[d, half : 2 * half, :].astype(F32)
        return (first[d].astype(F32) - step * moved).astype(BF16)

    unfold(count, piece, coarse_ref)
    active, react, inverse_mass, obs, jacobi = lines(diag_ref)
    image = image_ref[...]
    edges = edge_ref[...]
    step_column = column_of(step)[0:samples]
    residual = active * right_ref[...].astype(F32) - step_column * image
    kept, width = inverse_ref.shape
    fixed = width // LANES * kept + edges.shape[0]

    def rows_of(static_ref):
        return jnp.concatenate([static_ref[j * kept : (j + 1) * kept, :] for j in range(width // LANES)], axis=1)

    inverses = jnp.concatenate([inverse_ref[...], rows_of(near_ref), rows_of(across_ref)], axis=0)
    fixes = dot(inverses, coarse_ref[...]).astype(BF16)
    z = active * (residual * jacobi + dot(fixes[0:kept], vectors_ref[...], 0, 0))
    z_ref[...] = z

    def arriving(static_ref, fix, change):
        smooth_level = static_ref[fixed + kept :, :].astype(F32) - step_column * change.astype(F32)
        return (smooth_level + dot(fix, static_ref[fixed : fixed + kept, :], 0, 0)).astype(BF16)

    lon = lax.axis_index("lon")
    odd = lon & 1
    ahead, before = lax.rem(lon + 1, count), lax.rem(lon + count - 1, count)
    change = slice(2 * half + SUM_ROWS, second_ref.shape[1])
    from_near = arriving(near_ref, fixes[kept : 2 * kept], second_ref[ahead + odd * (before - ahead), change, :])
    from_across = arriving(across_ref, fixes[2 * kept :], second_ref[before + odd * (ahead - before), change, :])
    from_east, from_west = pick(0, from_near, from_across)
    arrived = jnp.concatenate([from_east, from_west], axis=1)
    stiff = dot(z.astype(BF16), dense_ref[...]) + react * z + dot(arrived, edges)
    curve = jnp.sum(stiff * stiff * inverse_mass + obs * z * z, axis=1, keepdims=True)
    products = row_of(row_sum(residual, z), row_sum(z, image))
    row = lax.broadcasted_iota(jnp.int32, (8, LANES), 0)
    chunk = jnp.where(row == 0, products, row_of(curve, curve))
    chunks_ref[...] = jnp.broadcast_to(chunk[None], chunks_ref.shape)
    sums_ref[...] = jnp.broadcast_to(sums, sums_ref.shape)


def finish_kernel(sums_ref, chunks_ref, first_ref, second_ref, out_ref):
    samples = first_ref.shape[0]
    half = LANES // 2
    totals = jnp.sum(chunks_ref[...], axis=0)
    norm0, curve0 = sums_ref[1:2, 0:half], sums_ref[1:2, half:]
    norm1, cross = totals[0:1, 0:half], totals[0:1, half:]
    curve = totals[1:2, 0:half]
    beta = norm1 / norm0
    step0 = norm0 / curve0
    step1 = norm1 / (curve + beta * (2.0 * cross + beta * curve0))
    scales = column_of(jnp.concatenate([step0 + step1 * beta, step1], axis=1))
    out_ref[...] = scales[0:samples] * first_ref[...] + scales[samples : 2 * samples] * second_ref[...]


def exchange(chunks, axes):
    return lax.all_to_all(chunks, axes, split_axis=0, concat_axis=0, tiled=True)


def other_band(array):
    return lax.ppermute(array, "lat", [(0, 1), (1, 0)])


def swap(array, reach, inner):
    size = lax.axis_size("lon")
    pairs = []
    for i in range(size):
        up = (i // reach) % 2 == (0 if inner else 1)
        pairs.append((i, (i + (reach if up else -reach)) % size))
    return lax.ppermute(array, "lon", pairs)


def body(
    right_side,
    stiffness_blocks,
    block_pattern,
    reaction,
    lumped_mass,
    obs_precision,
    coupling,
    east_rows,
    west_rows,
    iface_count,
    node_count,
    deflation,
    coarse_inverse,
):
    samples, nodes = right_side.shape
    slots = coupling.shape[0]
    vectors = deflation.shape[0]
    sectors = lax.axis_size("lon")
    domains = sectors * lax.axis_size("lat")
    half = vectors // 2
    react, mass, obs = reaction[None], lumped_mass[None], obs_precision[None]
    field = ((samples, nodes), F32)
    coarse_scratch = pltpu.VMEM((domains * vectors, samples), BF16)
    apply_cost = 2 * samples * nodes * nodes
    static = ((coarse_inverse.size // LANES + 2 * slots + vectors + samples, slots), BF16)
    inputs = (coupling, east_rows, west_rows, react, mass, obs, right_side, deflation, coarse_inverse, stiffness_blocks)
    line = pltpu.VMEM((1, nodes), F32)
    chunks, diag, edge, near_static, across_static, right, basis, stored, inverse = call(
        load_kernel,
        [((sectors, half, LANES), BF16), ((8, nodes), F32), ((2 * slots, nodes), BF16), static, static]
        + [(a.shape, a.dtype) for a in (right_side, deflation, stiffness_blocks, coarse_inverse)],
        [SMEM, SMEM] + [HBM] * len(inputs),
        [node_count, iface_count] + [pltpu.with_memory_space_constraint(a, pltpu.HBM) for a in inputs],
        2 * samples * vectors * nodes,
        [line, line, line] + [pltpu.VMEM(a.shape, a.dtype) for a in (coupling, east_rows, west_rows)]
        + [pltpu.SemaphoreType.DMA((len(inputs),))],
    )
    pieces, stored, across_static, near_static = lax.optimization_barrier(
        (exchange(chunks, "lon"), stored, swap(across_static, 1, False), swap(near_static, 1, True))
    )
    pattern = pltpu.with_memory_space_constraint(block_pattern.T, pltpu.HBM)
    (dense,) = call(
        prep_kernel,
        [((nodes, nodes), BF16)],
        [HBM, VMEM],
        (pattern, stored),
        apply_cost,
        [pltpu.SMEM((2, block_pattern.shape[0]), jnp.int32), pltpu.VMEM((nodes, nodes), F32), pltpu.SemaphoreType.DMA],
    )
    others = other_band(pieces)
    z0, scaled, near, across, far, beyond = call(
        start_kernel,
        [field] * 2 + [((2 * samples, slots), BF16)] * 2 + [((samples, slots), BF16)] * 2,
        [VMEM] * 8,
        (pieces, others, inverse, right, basis, dense, edge, diag),
        apply_cost,
        [coarse_scratch],
    )
    across = swap(across, 1, False)
    got_beyond = swap(beyond, 2, False)
    near = swap(near, 1, True)
    got_far = swap(far, 2, True)
    image, chunks = call(
        image_kernel,
        [field, ((sectors, 2 * half + SUM_ROWS + samples, LANES), BF16)],
        [VMEM] * 15,
        (across, got_beyond, near, got_far, far, beyond, across_static, near_static, z0, scaled, dense, edge, diag, right, basis),
        apply_cost,
    )
    second = exchange(chunks, "lon")
    second_others = other_band(second)
    z1, sums, chunks = call(
        middle_kernel,
        [field, ((8, LANES), F32), ((domains, 8, LANES), F32)],
        [VMEM] * 13,
        (pieces, others, second, second_others, across_static, near_static,
         inverse, right, image, basis, dense, edge, diag),
        apply_cost,
        [coarse_scratch],
    )
    totals = exchange(chunks, ("lon", "lat"))
    (out,) = call(finish_kernel, [field], [VMEM] * 4, (sums, totals, z0, z1), 4 * samples * nodes)
    return out


def solution(mesh):
    placed = (
        P(None, ("grp", "lon", "lat")),
        P(("grp", "lon", "lat"), None, None),
        P(("grp", "lon", "lat"), None),
        P(("grp", "lon", "lat")),
        P(("grp", "lon", "lat")),
        P(("grp", "lon", "lat")),
        P(("grp", "lon", "lat"), None),
        P(("grp", "lon", "lat"), None),
        P(("grp", "lon", "lat"), None),
        P(("grp", "lon", "lat")),
        P(("grp", "lon", "lat")),
        P(None, ("grp", "lon", "lat")),
        P(("grp", "lon", "lat"), None),
    )
    return jax.shard_map(
        body, mesh=mesh, in_specs=placed, out_specs=P(None, ("grp", "lon", "lat")), check_vma=False
    )
```

```python
import jax
import jax.numpy as jnp
import numpy as np
from jax import lax
from jax.experimental import pallas as pl
from jax.experimental.pallas import tpu as pltpu
from jax.sharding import PartitionSpec as P

F32 = jnp.float32
BF16 = jnp.bfloat16
VMEM = pl.BlockSpec(memory_space=pltpu.VMEM)
HBM = pl.BlockSpec(memory_space=pltpu.HBM)
SMEM = pl.BlockSpec(memory_space=pltpu.SMEM)
LANES = 128
SUM_ROWS = 16


def dot(a, b, ca=1, cb=0):
    return lax.dot_general(a, b, (((ca,), (cb,)), ((), ())), preferred_element_type=F32)


def call(kernel, outs, specs, args, flops, scratch=()):
    moved = sum(int(np.prod(a.shape)) * a.dtype.itemsize for a in args)
    return pl.pallas_call(
        kernel,
        out_shape=[jax.ShapeDtypeStruct(s, t) for s, t in outs],
        in_specs=specs,
        out_specs=[VMEM] * len(outs),
        scratch_shapes=list(scratch),
        compiler_params=pltpu.CompilerParams(vmem_limit_bytes=32 * 1024 * 1024),
        cost_estimate=pl.CostEstimate(flops=flops, bytes_accessed=moved, transcendentals=0),
    )(*args)


def fold(values):
    half = values.shape[0] // 2
    return jnp.concatenate([values[:half], values[half:]], axis=1)


def column_of(row):
    return jnp.transpose(jnp.broadcast_to(row, (LANES, LANES)))[:, 0:1]


def row_of(first, second):
    both = jnp.concatenate([first, second], axis=0)
    return jnp.transpose(jnp.broadcast_to(both, (LANES, LANES)))[0:1]


def row_sum(first, second):
    return jnp.sum(first * second, axis=1, keepdims=True)


def levels(values, edges):
    return dot(values.astype(BF16), edges, 1, 1)


def by_lon(shift_by, first_ref, second_ref, write):
    bit = (lax.axis_index("lon") >> shift_by) & 1
    pl.when(bit == 0)(lambda: write(first_ref, second_ref))
    pl.when(bit == 1)(lambda: write(second_ref, first_ref))


def pick(shift_by, first, second):
    bit = (lax.axis_index("lon") >> shift_by) & 1
    keep = jnp.full((1, 1), bit, jnp.int32) == 0
    first, second = first.astype(F32), second.astype(F32)
    return jnp.where(keep, first, second).astype(BF16), jnp.where(keep, second, first).astype(BF16)


def lines(diag_ref):
    return tuple(diag_ref[i : i + 1, :] for i in range(5))


def load_kernel(node_count_ref, iface_count_ref, coupling_hbm, east_hbm, west_hbm, react_hbm, mass_hbm, obs_hbm,
                right_hbm, vectors_hbm, inverse_hbm, blocks_hbm, pattern_hbm,
                chunks_ref, diag_ref, edge_ref, near_ref, across_ref, right_ref, vectors_ref, blocks_ref,
                inverse_ref, pattern_ref, react_ref, mass_ref, obs_ref, coupling_ref, east_ref, west_ref, sems):
    pairs = (
        (coupling_hbm, coupling_ref), (east_hbm, east_ref), (west_hbm, west_ref), (react_hbm, react_ref),
        (mass_hbm, mass_ref), (obs_hbm, obs_ref), (right_hbm, right_ref), (vectors_hbm, vectors_ref),
        (inverse_hbm, inverse_ref), (blocks_hbm, blocks_ref), (pattern_hbm, pattern_ref),
    )
    copies = [pltpu.make_async_copy(src, dst, sems.at[i]) for i, (src, dst) in enumerate(pairs)]
    for copy in copies:
        copy.start()
    nodes = right_ref.shape[1]
    slots = coupling_ref.shape[0]
    for copy in copies[:6]:
        copy.wait()
    active = (lax.broadcasted_iota(jnp.int32, (1, nodes), 1) < node_count_ref[0]).astype(F32)
    react, mass, obs = react_ref[...], mass_ref[...], obs_ref[...]
    inverse_mass, jacobi = 1.0 / mass, 1.0 / (obs + react * react / mass)
    row = lax.broadcasted_iota(jnp.int32, (8, nodes), 0)
    diag = jnp.zeros((8, nodes), F32)
    for i, line in enumerate((active, react, inverse_mass, obs, jacobi)):
        diag = jnp.where(row == i, line, diag)
    diag_ref[...] = diag

    node = lax.broadcasted_iota(jnp.int32, (slots, nodes), 1).astype(F32)
    east_hot = jnp.where(node == column_of(east_ref[...].astype(F32)), 1.0, 0.0).astype(BF16)
    west_hot = jnp.where(node == column_of(west_ref[...].astype(F32)), 1.0, 0.0).astype(BF16)
    live_a = lax.broadcasted_iota(jnp.int32, (slots, slots), 0) < iface_count_ref[0]
    live_b = lax.broadcasted_iota(jnp.int32, (slots, slots), 1) < iface_count_ref[0]
    link = jnp.where(live_a & live_b, coupling_ref[...], jnp.zeros((slots, slots), BF16))
    edges = jnp.concatenate([dot(link, east_hot, 0, 0).astype(BF16), west_hot], axis=0)
    edge_ref[...] = edges
    for copy in copies[6:9]:
        copy.wait()
    right = active * right_ref[...].astype(F32)
    coarse = fold(dot(vectors_ref[...], right.astype(BF16), 1, 1)).astype(BF16)
    chunks_ref[...] = jnp.broadcast_to(coarse[None], chunks_ref.shape)
    rows = [
        (edges.astype(F32) * inverse_mass).astype(BF16),
        vectors_ref[...] * active.astype(BF16),
        (jacobi * right).astype(BF16),
    ]
    level = dot(jnp.concatenate(rows, axis=0), edges, 1, 1).astype(BF16)
    kept, width = inverse_ref.shape
    fixed = width // LANES * kept

    def send(east_ref, west_ref):
        for ref, cols in ((east_ref, slice(0, slots)), (west_ref, slice(slots, 2 * slots))):
            for j in range(width // LANES):
                ref[j * kept : (j + 1) * kept, :] = inverse_ref[:, j * LANES : (j + 1) * LANES]
            ref[fixed:, :] = level[:, cols]

    by_lon(0, near_ref, across_ref, send)
    for copy in copies[9:]:
        copy.wait()


def prep_kernel(pattern_vmem, blocks_ref, dense_ref, pattern_ref, total_ref, sem):
    copy = pltpu.make_async_copy(pattern_vmem, pattern_ref, sem)
    copy.start()
    nodes = dense_ref.shape[0]
    count, block, _ = blocks_ref.shape

    def clear(i, carry):
        total_ref[pl.ds(pl.multiple_of(i * block, block), block), :] = jnp.zeros((block, nodes), F32)
        return carry

    lax.fori_loop(0, nodes // block, clear, 0)
    copy.wait()
    unit = (
        lax.broadcasted_iota(jnp.int32, (block, block), 0) == lax.broadcasted_iota(jnp.int32, (block, block), 1)
    ).astype(F32).astype(BF16)

    def place(k, carry):
        rows = pl.ds(pl.multiple_of(pattern_ref[0, k] * block, block), block)
        cols = pl.ds(pl.multiple_of(pattern_ref[1, k] * block, block), block)
        values = blocks_ref[k]
        total_ref[rows, cols] += values.astype(F32)
        total_ref[cols, rows] += dot(unit, values, 1, 1)
        return carry

    lax.fori_loop(0, count, place, 0, unroll=True)

    def narrow(i, carry):
        rows = pl.ds(pl.multiple_of(i * block, block), block)
        dense_ref[rows, :] = total_ref[rows, :].astype(BF16)
        return carry

    lax.fori_loop(0, nodes // block, narrow, 0)


def unfold(count, piece, coarse_ref):
    half = coarse_ref.shape[0] // count // 4
    lat = lax.axis_index("lat")

    def move(d, carry):
        for side in range(2):
            values = piece(side, d)
            at = pl.multiple_of((2 * d + (lat if side == 0 else 1 - lat)) * 2 * half, 2 * half)
            coarse_ref[pl.ds(at, half), :] = values[:, 0 : LANES // 2]
            coarse_ref[pl.ds(at + half, half), :] = values[:, LANES // 2 :]
        return carry

    lax.fori_loop(0, count, move, 0, unroll=min(count, 8))


def smooth(field, coarse_ref, inverse_ref, vectors_ref, active, jacobi):
    fix = dot(inverse_ref[...], coarse_ref[...]).astype(BF16)
    return active * (field * jacobi + dot(fix, vectors_ref[...], 0, 0))


def start_kernel(pieces_ref, others_ref, inverse_ref, right_ref, vectors_ref, dense_ref, edge_ref, diag_ref,
                 z_ref, scaled_ref, near_ref, across_ref, far_ref, beyond_ref, coarse_ref):
    samples, nodes = right_ref.shape
    unfold(pieces_ref.shape[0], lambda side, d: (pieces_ref, others_ref)[side][d], coarse_ref)
    active, react, inverse_mass, obs, jacobi = lines(diag_ref)
    z = smooth(right_ref[...].astype(F32), coarse_ref, inverse_ref, vectors_ref, active, jacobi)
    z_ref[...] = z
    edges = edge_ref[...]
    scaled = (dot(z.astype(BF16), dense_ref[...]) + react * z) * inverse_mass
    scaled_ref[...] = scaled
    level = levels(jnp.concatenate([z, scaled], axis=0), edges).astype(BF16)
    level1, level2 = level[0:samples], level[samples:]
    slots = edges.shape[0] // 2

    def send(east_ref, west_ref):
        for ref, cols in ((east_ref, slice(0, slots)), (west_ref, slice(slots, 2 * slots))):
            ref[0:samples, :] = level1[:, cols]
            ref[samples:, :] = level2[:, cols]

    def send_far(east_ref, west_ref):
        east_ref[...] = level1[:, 0:slots]
        west_ref[...] = level1[:, slots:]

    by_lon(0, near_ref, across_ref, send)
    by_lon(1, far_ref, beyond_ref, send_far)


def image_kernel(across_ref, beyond_ref, near_ref, far_ref, own_far_ref, own_beyond_ref, across_corr_ref, near_corr_ref,
                 z_ref, scaled_ref, dense_ref, edge_ref, diag_ref, right_ref, vectors_ref,
                 image_ref, chunks_ref):
    samples, nodes = z_ref.shape
    active, react, inverse_mass, obs, jacobi = lines(diag_ref)
    z = z_ref[...]
    edges = edge_ref[...]
    fixed = near_corr_ref.shape[0] - edges.shape[0] - vectors_ref.shape[0] - samples
    corr = slice(fixed, fixed + edges.shape[0])
    arrived = jnp.concatenate(pick(0, near_ref[0:samples, :], across_ref[0:samples, :]), axis=1)
    inner = scaled_ref[...] + dot(arrived, edges) * inverse_mass
    beyond_east, beyond_west = pick(1, far_ref[...], beyond_ref[...])
    own_east, own_west = pick(1, own_far_ref[...], own_beyond_ref[...])
    near_terms, across_terms = pick(
        0,
        jnp.concatenate([beyond_east, own_east], axis=1),
        jnp.concatenate([own_west, beyond_west], axis=1),
    )
    second_near = near_ref[samples:, :].astype(F32) + dot(near_terms, near_corr_ref[corr, :])
    second_across = across_ref[samples:, :].astype(F32) + dot(across_terms, across_corr_ref[corr, :])
    arrived2 = jnp.concatenate(pick(0, second_near, second_across), axis=1)
    stiff = dot(inner.astype(BF16), dense_ref[...]) + dot(arrived2, edges) + react * inner
    image = active * (stiff + obs * z)
    image_ref[...] = image
    level = levels(image * jacobi, edges).astype(BF16)
    coarse = fold(dot(vectors_ref[...], image.astype(BF16), 1, 1))
    high = coarse.astype(BF16)
    low = (coarse - high.astype(F32)).astype(BF16)
    sums = row_of(row_sum(active * right_ref[...].astype(F32), z), row_sum(z, image))
    row = lax.broadcasted_iota(jnp.int32, (SUM_ROWS, LANES), 0)
    tail = jnp.zeros((SUM_ROWS, LANES), F32)
    for i in range(3):
        part = sums.astype(BF16).astype(F32)
        tail = jnp.where(row == i, part, tail)
        sums = sums - part
    count, rows, _ = chunks_ref.shape
    slots = level.shape[1] // 2
    common = jnp.concatenate([high, low, tail.astype(BF16), level[:, 0:slots]], axis=0)
    chunks_ref[...] = jnp.broadcast_to(common[None], chunks_ref.shape)
    before = lax.rem(lax.axis_index("lon") + count - 1, count)
    chunks_ref[before, rows - samples :, :] = level[:, slots:]


def middle_kernel(pieces_ref, others_ref, second_ref, second_others_ref,
                  across_ref, near_ref, inverse_ref, right_ref, image_ref, vectors_ref,
                  dense_ref, edge_ref, diag_ref, z_ref, sums_ref, chunks_ref, coarse_ref):
    samples, nodes = right_ref.shape
    count, half, _ = pieces_ref.shape
    tail = slice(2 * half, 2 * half + SUM_ROWS)

    def add(d, total):
        return total + second_ref[d, tail, :].astype(F32) + second_others_ref[d, tail, :].astype(F32)

    parts = lax.fori_loop(0, count, add, jnp.zeros((SUM_ROWS, LANES), F32), unroll=min(count, 8))
    sums = parts[2:3] + parts[1:2] + parts[0:1]
    step = sums[:, 0 : LANES // 2] / sums[:, LANES // 2 :]
    step = jnp.concatenate([step, step], axis=1)

    def piece(side, d):
        first, change = ((pieces_ref, second_ref), (others_ref, second_others_ref))[side]
        moved = change[d, 0:half, :].astype(F32) + change[d, half : 2 * half, :].astype(F32)
        return (first[d].astype(F32) - step * moved).astype(BF16)

    unfold(count, piece, coarse_ref)
    active, react, inverse_mass, obs, jacobi = lines(diag_ref)
    image = image_ref[...]
    edges = edge_ref[...]
    step_column = column_of(step)[0:samples]
    residual = active * right_ref[...].astype(F32) - step_column * image
    kept, width = inverse_ref.shape
    fixed = width // LANES * kept + edges.shape[0]

    def rows_of(static_ref):
        return jnp.concatenate([static_ref[j * kept : (j + 1) * kept, :] for j in range(width // LANES)], axis=1)

    inverses = jnp.concatenate([inverse_ref[...], rows_of(near_ref), rows_of(across_ref)], axis=0)
    fixes = dot(inverses, coarse_ref[...]).astype(BF16)
    z = active * (residual * jacobi + dot(fixes[0:kept], vectors_ref[...], 0, 0))
    z_ref[...] = z

    def arriving(static_ref, fix, change):
        smooth_level = static_ref[fixed + kept :, :].astype(F32) - step_column * change.astype(F32)
        return (smooth_level + dot(fix, static_ref[fixed : fixed + kept, :], 0, 0)).astype(BF16)

    lon = lax.axis_index("lon")
    odd = lon & 1
    ahead, before = lax.rem(lon + 1, count), lax.rem(lon + count - 1, count)
    change = slice(2 * half + SUM_ROWS, second_ref.shape[1])
    from_near = arriving(near_ref, fixes[kept : 2 * kept], second_ref[ahead + odd * (before - ahead), change, :])
    from_across = arriving(across_ref, fixes[2 * kept :], second_ref[before + odd * (ahead - before), change, :])
    from_east, from_west = pick(0, from_near, from_across)
    arrived = jnp.concatenate([from_east, from_west], axis=1)
    stiff = dot(z.astype(BF16), dense_ref[...]) + react * z + dot(arrived, edges)
    curve = jnp.sum(stiff * stiff * inverse_mass + obs * z * z, axis=1, keepdims=True)
    products = row_of(row_sum(residual, z), row_sum(z, image))
    row = lax.broadcasted_iota(jnp.int32, (8, LANES), 0)
    chunk = jnp.where(row == 0, products, row_of(curve, curve))
    chunks_ref[...] = jnp.broadcast_to(chunk[None], chunks_ref.shape)
    sums_ref[...] = jnp.broadcast_to(sums, sums_ref.shape)


def finish_kernel(sums_ref, chunks_ref, first_ref, second_ref, out_ref):
    samples = first_ref.shape[0]
    half = LANES // 2
    totals = jnp.sum(chunks_ref[...], axis=0)
    norm0, curve0 = sums_ref[1:2, 0:half], sums_ref[1:2, half:]
    norm1, cross = totals[0:1, 0:half], totals[0:1, half:]
    curve = totals[1:2, 0:half]
    beta = norm1 / norm0
    step0 = norm0 / curve0
    step1 = norm1 / (curve + beta * (2.0 * cross + beta * curve0))
    scales = column_of(jnp.concatenate([step0 + step1 * beta, step1], axis=1))
    out_ref[...] = scales[0:samples] * first_ref[...] + scales[samples : 2 * samples] * second_ref[...]


def exchange(chunks, axes):
    return lax.all_to_all(chunks, axes, split_axis=0, concat_axis=0, tiled=True)


def other_band(array):
    return lax.ppermute(array, "lat", [(0, 1), (1, 0)])


def swap(array, reach, inner):
    size = lax.axis_size("lon")
    pairs = []
    for i in range(size):
        up = (i // reach) % 2 == (0 if inner else 1)
        pairs.append((i, (i + (reach if up else -reach)) % size))
    return lax.ppermute(array, "lon", pairs)


def body(
    right_side,
    stiffness_blocks,
    block_pattern,
    reaction,
    lumped_mass,
    obs_precision,
    coupling,
    east_rows,
    west_rows,
    iface_count,
    node_count,
    deflation,
    coarse_inverse,
):
    samples, nodes = right_side.shape
    slots = coupling.shape[0]
    vectors = deflation.shape[0]
    sectors = lax.axis_size("lon")
    domains = sectors * lax.axis_size("lat")
    half = vectors // 2
    react, mass, obs = reaction[None], lumped_mass[None], obs_precision[None]
    field = ((samples, nodes), F32)
    coarse_scratch = pltpu.VMEM((domains * vectors, samples), BF16)
    apply_cost = 2 * samples * nodes * nodes
    static = ((coarse_inverse.size // LANES + 2 * slots + vectors + samples, slots), BF16)
    inputs = (coupling, east_rows, west_rows, react, mass, obs, right_side, deflation, coarse_inverse, stiffness_blocks,
              block_pattern.T)
    line = pltpu.VMEM((1, nodes), F32)
    chunks, diag, edge, near_static, across_static, right, basis, stored, inverse, pattern = call(
        load_kernel,
        [((sectors, half, LANES), BF16), ((8, nodes), F32), ((2 * slots, nodes), BF16), static, static]
        + [(a.shape, a.dtype) for a in (right_side, deflation, stiffness_blocks, coarse_inverse, inputs[-1])],
        [SMEM, SMEM] + [HBM] * len(inputs),
        [node_count, iface_count] + [pltpu.with_memory_space_constraint(a, pltpu.HBM) for a in inputs],
        2 * samples * vectors * nodes,
        [line, line, line] + [pltpu.VMEM(a.shape, a.dtype) for a in (coupling, east_rows, west_rows)]
        + [pltpu.SemaphoreType.DMA((len(inputs),))],
    )
    pieces, stored, across_static, near_static = lax.optimization_barrier(
        (exchange(chunks, "lon"), stored, swap(across_static, 1, False), swap(near_static, 1, True))
    )
    (dense,) = call(
        prep_kernel,
        [((nodes, nodes), BF16)],
        [VMEM, VMEM],
        (pattern, stored),
        apply_cost,
        [pltpu.SMEM((2, block_pattern.shape[0]), jnp.int32), pltpu.VMEM((nodes, nodes), F32), pltpu.SemaphoreType.DMA],
    )
    others = other_band(pieces)
    z0, scaled, near, across, far, beyond = call(
        start_kernel,
        [field] * 2 + [((2 * samples, slots), BF16)] * 2 + [((samples, slots), BF16)] * 2,
        [VMEM] * 8,
        (pieces, others, inverse, right, basis, dense, edge, diag),
        apply_cost,
        [coarse_scratch],
    )
    across = swap(across, 1, False)
    got_beyond = swap(beyond, 2, False)
    near = swap(near, 1, True)
    got_far = swap(far, 2, True)
    image, chunks = call(
        image_kernel,
        [field, ((sectors, 2 * half + SUM_ROWS + samples, LANES), BF16)],
        [VMEM] * 15,
        (across, got_beyond, near, got_far, far, beyond, across_static, near_static, z0, scaled, dense, edge, diag, right, basis),
        apply_cost,
    )
    second = exchange(chunks, "lon")
    second_others = other_band(second)
    z1, sums, chunks = call(
        middle_kernel,
        [field, ((8, LANES), F32), ((domains, 8, LANES), F32)],
        [VMEM] * 13,
        (pieces, others, second, second_others, across_static, near_static,
         inverse, right, image, basis, dense, edge, diag),
        apply_cost,
        [coarse_scratch],
    )
    totals = exchange(chunks, ("lon", "lat"))
    (out,) = call(finish_kernel, [field], [VMEM] * 4, (sums, totals, z0, z1), 4 * samples * nodes)
    return out


def solution(mesh):
    placed = (
        P(None, ("grp", "lon", "lat")),
        P(("grp", "lon", "lat"), None, None),
        P(("grp", "lon", "lat"), None),
        P(("grp", "lon", "lat")),
        P(("grp", "lon", "lat")),
        P(("grp", "lon", "lat")),
        P(("grp", "lon", "lat"), None),
        P(("grp", "lon", "lat"), None),
        P(("grp", "lon", "lat"), None),
        P(("grp", "lon", "lat")),
        P(("grp", "lon", "lat")),
        P(None, ("grp", "lon", "lat")),
        P(("grp", "lon", "lat"), None),
    )
    return jax.shard_map(
        body, mesh=mesh, in_specs=placed, out_specs=P(None, ("grp", "lon", "lat")), check_vma=False
    )
```

```python
import jax
import jax.numpy as jnp
import numpy as np
from jax import lax
from jax.experimental import pallas as pl
from jax.experimental.pallas import tpu as pltpu
from jax.sharding import PartitionSpec as P

F32 = jnp.float32
BF16 = jnp.bfloat16
VMEM = pl.BlockSpec(memory_space=pltpu.VMEM)
HBM = pl.BlockSpec(memory_space=pltpu.HBM)
SMEM = pl.BlockSpec(memory_space=pltpu.SMEM)
LANES = 128
SUM_ROWS = 16


def dot(a, b, ca=1, cb=0):
    return lax.dot_general(a, b, (((ca,), (cb,)), ((), ())), preferred_element_type=F32)


def call(kernel, outs, specs, args, flops, scratch=()):
    moved = sum(int(np.prod(a.shape)) * a.dtype.itemsize for a in args)
    return pl.pallas_call(
        kernel,
        out_shape=[jax.ShapeDtypeStruct(s, t) for s, t in outs],
        in_specs=specs,
        out_specs=[VMEM] * len(outs),
        scratch_shapes=list(scratch),
        compiler_params=pltpu.CompilerParams(vmem_limit_bytes=32 * 1024 * 1024),
        cost_estimate=pl.CostEstimate(flops=flops, bytes_accessed=moved, transcendentals=0),
    )(*args)


def fold(values):
    half = values.shape[0] // 2
    return jnp.concatenate([values[:half], values[half:]], axis=1)


def column_of(row):
    return jnp.transpose(jnp.broadcast_to(row, (LANES, LANES)))[:, 0:1]


def row_of(first, second):
    both = jnp.concatenate([first, second], axis=0)
    return jnp.transpose(jnp.broadcast_to(both, (LANES, LANES)))[0:1]


def row_sum(first, second):
    return jnp.sum(first * second, axis=1, keepdims=True)


def levels(values, edges):
    return dot(values.astype(BF16), edges, 1, 1)


def by_lon(shift_by, first_ref, second_ref, write):
    bit = (lax.axis_index("lon") >> shift_by) & 1
    pl.when(bit == 0)(lambda: write(first_ref, second_ref))
    pl.when(bit == 1)(lambda: write(second_ref, first_ref))


def pick(shift_by, first, second):
    bit = (lax.axis_index("lon") >> shift_by) & 1
    keep = jnp.full((1, 1), bit, jnp.int32) == 0
    first, second = first.astype(F32), second.astype(F32)
    return jnp.where(keep, first, second).astype(BF16), jnp.where(keep, second, first).astype(BF16)


def lines(diag_ref):
    return tuple(diag_ref[i : i + 1, :] for i in range(5))


def load_kernel(node_count_ref, iface_count_ref, coupling_hbm, east_hbm, west_hbm, react_hbm, mass_hbm, obs_hbm,
                right_hbm, vectors_hbm, inverse_hbm, blocks_hbm, pattern_hbm,
                chunks_ref, diag_ref, edge_ref, near_ref, across_ref, right_ref, vectors_ref, blocks_ref,
                inverse_ref, pattern_ref, react_ref, mass_ref, obs_ref, coupling_ref, east_ref, west_ref, sems):
    pairs = (
        (coupling_hbm, coupling_ref), (east_hbm, east_ref), (west_hbm, west_ref), (react_hbm, react_ref),
        (mass_hbm, mass_ref), (obs_hbm, obs_ref), (right_hbm, right_ref), (vectors_hbm, vectors_ref),
        (inverse_hbm, inverse_ref), (blocks_hbm, blocks_ref), (pattern_hbm, pattern_ref),
    )
    copies = [pltpu.make_async_copy(src, dst, sems.at[i]) for i, (src, dst) in enumerate(pairs)]
    for copy in copies:
        copy.start()
    nodes = right_ref.shape[1]
    slots = coupling_ref.shape[0]
    for copy in copies[:6]:
        copy.wait()
    active = (lax.broadcasted_iota(jnp.int32, (1, nodes), 1) < node_count_ref[0]).astype(F32)
    react, mass, obs = react_ref[...], mass_ref[...], obs_ref[...]
    inverse_mass, jacobi = 1.0 / mass, 1.0 / (obs + react * react / mass)
    row = lax.broadcasted_iota(jnp.int32, (8, nodes), 0)
    diag = jnp.zeros((8, nodes), F32)
    for i, line in enumerate((active, react, inverse_mass, obs, jacobi)):
        diag = jnp.where(row == i, line, diag)
    diag_ref[...] = diag

    node = lax.broadcasted_iota(jnp.int32, (slots, nodes), 1).astype(F32)
    east_hot = jnp.where(node == column_of(east_ref[...].astype(F32)), 1.0, 0.0).astype(BF16)
    west_hot = jnp.where(node == column_of(west_ref[...].astype(F32)), 1.0, 0.0).astype(BF16)
    live_a = lax.broadcasted_iota(jnp.int32, (slots, slots), 0) < iface_count_ref[0]
    live_b = lax.broadcasted_iota(jnp.int32, (slots, slots), 1) < iface_count_ref[0]
    link = jnp.where(live_a & live_b, coupling_ref[...], jnp.zeros((slots, slots), BF16))
    edges = jnp.concatenate([dot(link, east_hot, 0, 0).astype(BF16), west_hot], axis=0)
    edge_ref[...] = edges
    for copy in copies[6:9]:
        copy.wait()
    right = active * right_ref[...].astype(F32)
    coarse = fold(dot(vectors_ref[...], right.astype(BF16), 1, 1)).astype(BF16)
    chunks_ref[...] = jnp.broadcast_to(coarse[None], chunks_ref.shape)
    rows = [
        (edges.astype(F32) * inverse_mass).astype(BF16),
        vectors_ref[...] * active.astype(BF16),
        (jacobi * right).astype(BF16),
    ]
    level = dot(jnp.concatenate(rows, axis=0), edges, 1, 1).astype(BF16)
    kept, width = inverse_ref.shape
    fixed = width // LANES * kept

    def send(east_ref, west_ref):
        for ref, cols in ((east_ref, slice(0, slots)), (west_ref, slice(slots, 2 * slots))):
            for j in range(width // LANES):
                ref[j * kept : (j + 1) * kept, :] = inverse_ref[:, j * LANES : (j + 1) * LANES]
            ref[fixed:, :] = level[:, cols]

    by_lon(0, near_ref, across_ref, send)
    for copy in copies[9:]:
        copy.wait()


def prep_kernel(pattern_vmem, blocks_ref, dense_ref, pattern_ref, total_ref, sem):
    copy = pltpu.make_async_copy(pattern_vmem, pattern_ref, sem)
    copy.start()
    nodes = dense_ref.shape[0]
    count, block, _ = blocks_ref.shape

    def clear(i, carry):
        total_ref[pl.ds(pl.multiple_of(i * block, block), block), :] = jnp.zeros((block, nodes), F32)
        return carry

    lax.fori_loop(0, nodes // block, clear, 0)
    copy.wait()
    unit = (
        lax.broadcasted_iota(jnp.int32, (block, block), 0) == lax.broadcasted_iota(jnp.int32, (block, block), 1)
    ).astype(F32).astype(BF16)

    def place(k, carry):
        rows = pl.ds(pl.multiple_of(pattern_ref[0, k] * block, block), block)
        cols = pl.ds(pl.multiple_of(pattern_ref[1, k] * block, block), block)
        values = blocks_ref[k]
        total_ref[rows, cols] += values.astype(F32)
        total_ref[cols, rows] += dot(unit, values, 1, 1)
        return carry

    lax.fori_loop(0, count, place, 0, unroll=True)

    def narrow(i, carry):
        rows = pl.ds(pl.multiple_of(i * block, block), block)
        dense_ref[rows, :] = total_ref[rows, :].astype(BF16)
        return carry

    lax.fori_loop(0, nodes // block, narrow, 0)


def unfold(count, piece, coarse_ref):
    half = coarse_ref.shape[0] // count // 4
    lat = lax.axis_index("lat")

    def move(d, carry):
        for side in range(2):
            values = piece(side, d)
            at = pl.multiple_of((2 * d + (lat if side == 0 else 1 - lat)) * 2 * half, 2 * half)
            coarse_ref[pl.ds(at, half), :] = values[:, 0 : LANES // 2]
            coarse_ref[pl.ds(at + half, half), :] = values[:, LANES // 2 :]
        return carry

    lax.fori_loop(0, count, move, 0, unroll=min(count, 8))


def smooth(field, coarse_ref, inverse_ref, vectors_ref, active, jacobi):
    fix = dot(inverse_ref[...], coarse_ref[...]).astype(BF16)
    return active * (field * jacobi + dot(fix, vectors_ref[...], 0, 0))


def start_kernel(pieces_ref, others_ref, inverse_ref, right_ref, vectors_ref, dense_ref, edge_ref, diag_ref,
                 z_ref, scaled_ref, near_ref, across_ref, far_ref, beyond_ref, coarse_ref):
    samples, nodes = right_ref.shape
    unfold(pieces_ref.shape[0], lambda side, d: (pieces_ref, others_ref)[side][d], coarse_ref)
    active, react, inverse_mass, obs, jacobi = lines(diag_ref)
    z = smooth(right_ref[...].astype(F32), coarse_ref, inverse_ref, vectors_ref, active, jacobi)
    z_ref[...] = z
    edges = edge_ref[...]
    scaled = (dot(z.astype(BF16), dense_ref[...]) + react * z) * inverse_mass
    scaled_ref[...] = scaled
    level = levels(jnp.concatenate([z, scaled], axis=0), edges).astype(BF16)
    level1, level2 = level[0:samples], level[samples:]
    slots = edges.shape[0] // 2

    def send(east_ref, west_ref):
        for ref, cols in ((east_ref, slice(0, slots)), (west_ref, slice(slots, 2 * slots))):
            ref[0:samples, :] = level1[:, cols]
            ref[samples:, :] = level2[:, cols]

    def send_far(east_ref, west_ref):
        east_ref[...] = level1[:, 0:slots]
        west_ref[...] = level1[:, slots:]

    by_lon(0, near_ref, across_ref, send)
    by_lon(1, far_ref, beyond_ref, send_far)


def image_kernel(across_ref, beyond_ref, near_ref, far_ref, own_far_ref, own_beyond_ref, across_corr_ref, near_corr_ref,
                 z_ref, scaled_ref, dense_ref, edge_ref, diag_ref, right_ref, vectors_ref,
                 image_ref, chunks_ref):
    samples, nodes = z_ref.shape
    active, react, inverse_mass, obs, jacobi = lines(diag_ref)
    z = z_ref[...]
    edges = edge_ref[...]
    fixed = near_corr_ref.shape[0] - edges.shape[0] - vectors_ref.shape[0] - samples
    corr = slice(fixed, fixed + edges.shape[0])
    arrived = jnp.concatenate(pick(0, near_ref[0:samples, :], across_ref[0:samples, :]), axis=1)
    inner = scaled_ref[...] + dot(arrived, edges) * inverse_mass
    beyond_east, beyond_west = pick(1, far_ref[...], beyond_ref[...])
    own_east, own_west = pick(1, own_far_ref[...], own_beyond_ref[...])
    near_terms, across_terms = pick(
        0,
        jnp.concatenate([beyond_east, own_east], axis=1),
        jnp.concatenate([own_west, beyond_west], axis=1),
    )
    second_near = near_ref[samples:, :].astype(F32) + dot(near_terms, near_corr_ref[corr, :])
    second_across = across_ref[samples:, :].astype(F32) + dot(across_terms, across_corr_ref[corr, :])
    arrived2 = jnp.concatenate(pick(0, second_near, second_across), axis=1)
    stiff = dot(inner.astype(BF16), dense_ref[...]) + dot(arrived2, edges) + react * inner
    image = active * (stiff + obs * z)
    image_ref[...] = image
    level = levels(image * jacobi, edges).astype(BF16)
    coarse = fold(dot(vectors_ref[...], image.astype(BF16), 1, 1))
    high = coarse.astype(BF16)
    low = (coarse - high.astype(F32)).astype(BF16)
    sums = row_of(row_sum(active * right_ref[...].astype(F32), z), row_sum(z, image))
    row = lax.broadcasted_iota(jnp.int32, (SUM_ROWS, LANES), 0)
    tail = jnp.zeros((SUM_ROWS, LANES), F32)
    for i in range(3):
        part = sums.astype(BF16).astype(F32)
        tail = jnp.where(row == i, part, tail)
        sums = sums - part
    count, rows, _ = chunks_ref.shape
    slots = level.shape[1] // 2
    common = jnp.concatenate([high, low, tail.astype(BF16), level[:, 0:slots]], axis=0)
    chunks_ref[...] = jnp.broadcast_to(common[None], chunks_ref.shape)
    before = lax.rem(lax.axis_index("lon") + count - 1, count)
    chunks_ref[before, rows - samples :, :] = level[:, slots:]


def middle_kernel(pieces_ref, others_ref, second_ref, second_others_ref,
                  across_ref, near_ref, inverse_ref, right_ref, image_ref, vectors_ref,
                  dense_ref, edge_ref, diag_ref, z_ref, sums_ref, chunks_ref, coarse_ref):
    samples, nodes = right_ref.shape
    count, half, _ = pieces_ref.shape
    tail = slice(2 * half, 2 * half + SUM_ROWS)

    def add(d, total):
        return total + second_ref[d, tail, :].astype(F32) + second_others_ref[d, tail, :].astype(F32)

    parts = lax.fori_loop(0, count, add, jnp.zeros((SUM_ROWS, LANES), F32), unroll=min(count, 8))
    sums = parts[2:3] + parts[1:2] + parts[0:1]
    step = sums[:, 0 : LANES // 2] / sums[:, LANES // 2 :]
    step = jnp.concatenate([step, step], axis=1)

    def piece(side, d):
        first, change = ((pieces_ref, second_ref), (others_ref, second_others_ref))[side]
        moved = change[d, 0:half, :].astype(F32) + change[d, half : 2 * half, :].astype(F32)
        return (first[d].astype(F32) - step * moved).astype(BF16)

    unfold(count, piece, coarse_ref)
    active, react, inverse_mass, obs, jacobi = lines(diag_ref)
    image = image_ref[...]
    edges = edge_ref[...]
    step_column = column_of(step)[0:samples]
    residual = active * right_ref[...].astype(F32) - step_column * image
    kept, width = inverse_ref.shape
    fixed = width // LANES * kept + edges.shape[0]

    def rows_of(static_ref):
        return jnp.concatenate([static_ref[j * kept : (j + 1) * kept, :] for j in range(width // LANES)], axis=1)

    inverses = jnp.concatenate([inverse_ref[...], rows_of(near_ref), rows_of(across_ref)], axis=0)
    fixes = dot(inverses, coarse_ref[...]).astype(BF16)
    z = active * (residual * jacobi + dot(fixes[0:kept], vectors_ref[...], 0, 0))
    z_ref[...] = z

    def arriving(static_ref, fix, change):
        smooth_level = static_ref[fixed + kept :, :].astype(F32) - step_column * change.astype(F32)
        return (smooth_level + dot(fix, static_ref[fixed : fixed + kept, :], 0, 0)).astype(BF16)

    lon = lax.axis_index("lon")
    odd = lon & 1
    ahead, before = lax.rem(lon + 1, count), lax.rem(lon + count - 1, count)
    change = slice(2 * half + SUM_ROWS, second_ref.shape[1])
    from_near = arriving(near_ref, fixes[kept : 2 * kept], second_ref[ahead + odd * (before - ahead), change, :])
    from_across = arriving(across_ref, fixes[2 * kept :], second_ref[before + odd * (ahead - before), change, :])
    from_east, from_west = pick(0, from_near, from_across)
    arrived = jnp.concatenate([from_east, from_west], axis=1)
    stiff = dot(z.astype(BF16), dense_ref[...]) + react * z + dot(arrived, edges)
    curve = jnp.sum(stiff * stiff * inverse_mass + obs * z * z, axis=1, keepdims=True)
    products = row_of(row_sum(residual, z), row_sum(z, image))
    row = lax.broadcasted_iota(jnp.int32, (8, LANES), 0)
    chunk = jnp.where(row == 0, products, row_of(curve, curve))
    chunks_ref[...] = jnp.broadcast_to(chunk[None], chunks_ref.shape)
    sums_ref[...] = jnp.broadcast_to(sums, sums_ref.shape)


def finish_kernel(sums_ref, chunks_ref, first_ref, second_ref, out_ref):
    samples = first_ref.shape[0]
    half = LANES // 2
    totals = jnp.sum(chunks_ref[...], axis=0)
    norm0, curve0 = sums_ref[1:2, 0:half], sums_ref[1:2, half:]
    norm1, cross = totals[0:1, 0:half], totals[0:1, half:]
    curve = totals[1:2, 0:half]
    beta = norm1 / norm0
    step0 = norm0 / curve0
    step1 = norm1 / (curve + beta * (2.0 * cross + beta * curve0))
    scales = column_of(jnp.concatenate([step0 + step1 * beta, step1], axis=1))
    out_ref[...] = scales[0:samples] * first_ref[...] + scales[samples : 2 * samples] * second_ref[...]


def exchange(chunks, axes):
    return lax.all_to_all(chunks, axes, split_axis=0, concat_axis=0, tiled=True)


def other_band(array):
    return lax.ppermute(array, "lat", [(0, 1), (1, 0)])


def swap(array, reach, inner):
    size = lax.axis_size("lon")
    pairs = []
    for i in range(size):
        up = (i // reach) % 2 == (0 if inner else 1)
        pairs.append((i, (i + (reach if up else -reach)) % size))
    return lax.ppermute(array, "lon", pairs)


def body(
    right_side,
    stiffness_blocks,
    block_pattern,
    reaction,
    lumped_mass,
    obs_precision,
    coupling,
    east_rows,
    west_rows,
    iface_count,
    node_count,
    deflation,
    coarse_inverse,
):
    samples, nodes = right_side.shape
    slots = coupling.shape[0]
    vectors = deflation.shape[0]
    sectors = lax.axis_size("lon")
    domains = sectors * lax.axis_size("lat")
    half = vectors // 2
    react, mass, obs = reaction[None], lumped_mass[None], obs_precision[None]
    field = ((samples, nodes), F32)
    coarse_scratch = pltpu.VMEM((domains * vectors, samples), BF16)
    apply_cost = 2 * samples * nodes * nodes
    static = ((coarse_inverse.size // LANES + 2 * slots + vectors + samples, slots), BF16)
    inputs = (coupling, east_rows, west_rows, react, mass, obs, right_side, deflation, coarse_inverse, stiffness_blocks,
              block_pattern.T)
    line = pltpu.VMEM((1, nodes), F32)
    chunks, diag, edge, near_static, across_static, right, basis, stored, inverse, pattern = call(
        load_kernel,
        [((sectors, half, LANES), BF16), ((8, nodes), F32), ((2 * slots, nodes), BF16), static, static]
        + [(a.shape, a.dtype) for a in (right_side, deflation, stiffness_blocks, coarse_inverse, inputs[-1])],
        [SMEM, SMEM] + [HBM] * len(inputs),
        [node_count, iface_count] + [pltpu.with_memory_space_constraint(a, pltpu.HBM) for a in inputs],
        2 * samples * vectors * nodes,
        [line, line, line] + [pltpu.VMEM(a.shape, a.dtype) for a in (coupling, east_rows, west_rows)]
        + [pltpu.SemaphoreType.DMA((len(inputs),))],
    )
    near_static = swap(near_static, 1, True)
    across_static = swap(across_static, 1, False)
    near_static, across_static, pieces, stored = lax.optimization_barrier(
        (near_static, across_static, exchange(chunks, "lon"), stored)
    )
    (dense,) = call(
        prep_kernel,
        [((nodes, nodes), BF16)],
        [VMEM, VMEM],
        (pattern, stored),
        apply_cost,
        [pltpu.SMEM((2, block_pattern.shape[0]), jnp.int32), pltpu.VMEM((nodes, nodes), F32), pltpu.SemaphoreType.DMA],
    )
    others = other_band(pieces)
    z0, scaled, near, across, far, beyond = call(
        start_kernel,
        [field] * 2 + [((2 * samples, slots), BF16)] * 2 + [((samples, slots), BF16)] * 2,
        [VMEM] * 8,
        (pieces, others, inverse, right, basis, dense, edge, diag),
        apply_cost,
        [coarse_scratch],
    )
    across = swap(across, 1, False)
    got_beyond = swap(beyond, 2, False)
    near = swap(near, 1, True)
    got_far = swap(far, 2, True)
    image, chunks = call(
        image_kernel,
        [field, ((sectors, 2 * half + SUM_ROWS + samples, LANES), BF16)],
        [VMEM] * 15,
        (across, got_beyond, near, got_far, far, beyond, across_static, near_static, z0, scaled, dense, edge, diag, right, basis),
        apply_cost,
    )
    second = exchange(chunks, "lon")
    second_others = other_band(second)
    z1, sums, chunks = call(
        middle_kernel,
        [field, ((8, LANES), F32), ((domains, 8, LANES), F32)],
        [VMEM] * 13,
        (pieces, others, second, second_others, across_static, near_static,
         inverse, right, image, basis, dense, edge, diag),
        apply_cost,
        [coarse_scratch],
    )
    totals = exchange(chunks, ("lon", "lat"))
    (out,) = call(finish_kernel, [field], [VMEM] * 4, (sums, totals, z0, z1), 4 * samples * nodes)
    return out


def solution(mesh):
    placed = (
        P(None, ("grp", "lon", "lat")),
        P(("grp", "lon", "lat"), None, None),
        P(("grp", "lon", "lat"), None),
        P(("grp", "lon", "lat")),
        P(("grp", "lon", "lat")),
        P(("grp", "lon", "lat")),
        P(("grp", "lon", "lat"), None),
        P(("grp", "lon", "lat"), None),
        P(("grp", "lon", "lat"), None),
        P(("grp", "lon", "lat")),
        P(("grp", "lon", "lat")),
        P(None, ("grp", "lon", "lat")),
        P(("grp", "lon", "lat"), None),
    )
    return jax.shard_map(
        body, mesh=mesh, in_specs=placed, out_specs=P(None, ("grp", "lon", "lat")), check_vma=False
    )
```

```python
import jax
import jax.numpy as jnp
import numpy as np
from jax import lax
from jax.experimental import pallas as pl
from jax.experimental.pallas import tpu as pltpu
from jax.sharding import PartitionSpec as P

F32 = jnp.float32
BF16 = jnp.bfloat16
VMEM = pl.BlockSpec(memory_space=pltpu.VMEM)
HBM = pl.BlockSpec(memory_space=pltpu.HBM)
SMEM = pl.BlockSpec(memory_space=pltpu.SMEM)
LANES = 128
SUM_ROWS = 16


def dot(a, b, ca=1, cb=0):
    return lax.dot_general(a, b, (((ca,), (cb,)), ((), ())), preferred_element_type=F32)


def call(kernel, outs, specs, args, flops, scratch=()):
    moved = sum(int(np.prod(a.shape)) * a.dtype.itemsize for a in args)
    return pl.pallas_call(
        kernel,
        out_shape=[jax.ShapeDtypeStruct(s, t) for s, t in outs],
        in_specs=specs,
        out_specs=[VMEM] * len(outs),
        scratch_shapes=list(scratch),
        compiler_params=pltpu.CompilerParams(vmem_limit_bytes=32 * 1024 * 1024),
        cost_estimate=pl.CostEstimate(flops=flops, bytes_accessed=moved, transcendentals=0),
    )(*args)


def fold(values):
    half = values.shape[0] // 2
    return jnp.concatenate([values[:half], values[half:]], axis=1)


def column_of(row):
    return jnp.transpose(jnp.broadcast_to(row, (LANES, LANES)))[:, 0:1]


def row_of(first, second):
    both = jnp.concatenate([first, second], axis=0)
    return jnp.transpose(jnp.broadcast_to(both, (LANES, LANES)))[0:1]


def row_sum(first, second):
    return jnp.sum(first * second, axis=1, keepdims=True)


def levels(values, edges):
    return dot(values.astype(BF16), edges, 1, 1)


def by_lon(shift_by, first_ref, second_ref, write):
    bit = (lax.axis_index("lon") >> shift_by) & 1
    pl.when(bit == 0)(lambda: write(first_ref, second_ref))
    pl.when(bit == 1)(lambda: write(second_ref, first_ref))


def pick(shift_by, first, second):
    bit = (lax.axis_index("lon") >> shift_by) & 1
    keep = jnp.full((1, 1), bit, jnp.int32) == 0
    first, second = first.astype(F32), second.astype(F32)
    return jnp.where(keep, first, second).astype(BF16), jnp.where(keep, second, first).astype(BF16)


def lines(diag_ref):
    return tuple(diag_ref[i : i + 1, :] for i in range(5))


def load_kernel(node_count_ref, iface_count_ref, coupling_hbm, east_hbm, west_hbm, react_hbm, mass_hbm, obs_hbm,
                right_hbm, vectors_hbm, inverse_hbm, blocks_hbm, pattern_hbm,
                chunks_ref, diag_ref, edge_ref, near_ref, across_ref, right_ref, vectors_ref, blocks_ref,
                inverse_ref, pattern_ref, react_ref, mass_ref, obs_ref, coupling_ref, east_ref, west_ref, sems):
    pairs = (
        (coupling_hbm, coupling_ref), (east_hbm, east_ref), (west_hbm, west_ref), (react_hbm, react_ref),
        (mass_hbm, mass_ref), (obs_hbm, obs_ref), (right_hbm, right_ref), (vectors_hbm, vectors_ref),
        (inverse_hbm, inverse_ref), (blocks_hbm, blocks_ref), (pattern_hbm, pattern_ref),
    )
    copies = [pltpu.make_async_copy(src, dst, sems.at[i]) for i, (src, dst) in enumerate(pairs)]
    for copy in copies:
        copy.start()
    nodes = right_ref.shape[1]
    slots = coupling_ref.shape[0]
    for copy in copies[:6]:
        copy.wait()
    active = (lax.broadcasted_iota(jnp.int32, (1, nodes), 1) < node_count_ref[0]).astype(F32)
    react, mass, obs = react_ref[...], mass_ref[...], obs_ref[...]
    inverse_mass, jacobi = 1.0 / mass, 1.0 / (obs + react * react / mass)
    row = lax.broadcasted_iota(jnp.int32, (8, nodes), 0)
    diag = jnp.zeros((8, nodes), F32)
    for i, line in enumerate((active, react, inverse_mass, obs, jacobi)):
        diag = jnp.where(row == i, line, diag)
    diag_ref[...] = diag

    node = lax.broadcasted_iota(jnp.int32, (slots, nodes), 1).astype(F32)
    east_hot = jnp.where(node == column_of(east_ref[...].astype(F32)), 1.0, 0.0).astype(BF16)
    west_hot = jnp.where(node == column_of(west_ref[...].astype(F32)), 1.0, 0.0).astype(BF16)
    live_a = lax.broadcasted_iota(jnp.int32, (slots, slots), 0) < iface_count_ref[0]
    live_b = lax.broadcasted_iota(jnp.int32, (slots, slots), 1) < iface_count_ref[0]
    link = jnp.where(live_a & live_b, coupling_ref[...], jnp.zeros((slots, slots), BF16))
    edges = jnp.concatenate([dot(link, east_hot, 0, 0).astype(BF16), west_hot], axis=0)
    edge_ref[...] = edges
    for copy in copies[6:9]:
        copy.wait()
    right = active * right_ref[...].astype(F32)
    coarse = fold(dot(vectors_ref[...], right.astype(BF16), 1, 1)).astype(BF16)
    chunks_ref[...] = jnp.broadcast_to(coarse[None], chunks_ref.shape)
    rows = [
        (edges.astype(F32) * inverse_mass).astype(BF16),
        vectors_ref[...] * active.astype(BF16),
        (jacobi * right).astype(BF16),
    ]
    level = dot(jnp.concatenate(rows, axis=0), edges, 1, 1).astype(BF16)
    kept, width = inverse_ref.shape
    fixed = width // LANES * kept

    def send(east_ref, west_ref):
        for ref, cols in ((east_ref, slice(0, slots)), (west_ref, slice(slots, 2 * slots))):
            for j in range(width // LANES):
                ref[j * kept : (j + 1) * kept, :] = inverse_ref[:, j * LANES : (j + 1) * LANES]
            ref[fixed:, :] = level[:, cols]

    by_lon(0, near_ref, across_ref, send)
    for copy in copies[9:]:
        copy.wait()


def prep_kernel(pattern_vmem, blocks_ref, dense_ref, pattern_ref, total_ref, sem):
    copy = pltpu.make_async_copy(pattern_vmem, pattern_ref, sem)
    copy.start()
    nodes = dense_ref.shape[0]
    count, block, _ = blocks_ref.shape

    def clear(i, carry):
        total_ref[pl.ds(pl.multiple_of(i * block, block), block), :] = jnp.zeros((block, nodes), F32)
        return carry

    lax.fori_loop(0, nodes // block, clear, 0)
    copy.wait()
    unit = (
        lax.broadcasted_iota(jnp.int32, (block, block), 0) == lax.broadcasted_iota(jnp.int32, (block, block), 1)
    ).astype(F32).astype(BF16)

    def place(k, carry):
        rows = pl.ds(pl.multiple_of(pattern_ref[0, k] * block, block), block)
        cols = pl.ds(pl.multiple_of(pattern_ref[1, k] * block, block), block)
        values = blocks_ref[k]
        total_ref[rows, cols] += values.astype(F32)
        total_ref[cols, rows] += dot(unit, values, 1, 1)
        return carry

    lax.fori_loop(0, count, place, 0, unroll=True)

    def narrow(i, carry):
        rows = pl.ds(pl.multiple_of(i * block, block), block)
        dense_ref[rows, :] = total_ref[rows, :].astype(BF16)
        return carry

    lax.fori_loop(0, nodes // block, narrow, 0)


def unfold(count, piece, coarse_ref):
    half = coarse_ref.shape[0] // count // 4
    lat = lax.axis_index("lat")

    def move(d, carry):
        for side in range(2):
            values = piece(side, d)
            at = pl.multiple_of((2 * d + (lat if side == 0 else 1 - lat)) * 2 * half, 2 * half)
            coarse_ref[pl.ds(at, half), :] = values[:, 0 : LANES // 2]
            coarse_ref[pl.ds(at + half, half), :] = values[:, LANES // 2 :]
        return carry

    lax.fori_loop(0, count, move, 0, unroll=min(count, 8))


def smooth(field, coarse_ref, inverse_ref, vectors_ref, active, jacobi):
    fix = dot(inverse_ref[...], coarse_ref[...]).astype(BF16)
    return active * (field * jacobi + dot(fix, vectors_ref[...], 0, 0))


def start_kernel(pieces_ref, others_ref, inverse_ref, right_ref, vectors_ref, dense_ref, edge_ref, diag_ref,
                 z_ref, scaled_ref, near_ref, across_ref, far_ref, beyond_ref, coarse_ref):
    samples, nodes = right_ref.shape
    unfold(pieces_ref.shape[0], lambda side, d: (pieces_ref, others_ref)[side][d], coarse_ref)
    active, react, inverse_mass, obs, jacobi = lines(diag_ref)
    z = smooth(right_ref[...].astype(F32), coarse_ref, inverse_ref, vectors_ref, active, jacobi)
    z_ref[...] = z
    edges = edge_ref[...]
    scaled = (dot(z.astype(BF16), dense_ref[...]) + react * z) * inverse_mass
    scaled_ref[...] = scaled
    level = levels(jnp.concatenate([z, scaled], axis=0), edges).astype(BF16)
    level1, level2 = level[0:samples], level[samples:]
    slots = edges.shape[0] // 2

    def send(east_ref, west_ref):
        for ref, cols in ((east_ref, slice(0, slots)), (west_ref, slice(slots, 2 * slots))):
            ref[0:samples, :] = level1[:, cols]
            ref[samples:, :] = level2[:, cols]

    def send_far(east_ref, west_ref):
        east_ref[...] = level1[:, 0:slots]
        west_ref[...] = level1[:, slots:]

    by_lon(0, near_ref, across_ref, send)
    by_lon(1, far_ref, beyond_ref, send_far)


def image_kernel(near_ref, across_ref, beyond_ref, far_ref, own_far_ref, own_beyond_ref, across_corr_ref, near_corr_ref,
                 z_ref, scaled_ref, dense_ref, edge_ref, diag_ref, right_ref, vectors_ref,
                 image_ref, chunks_ref):
    samples, nodes = z_ref.shape
    active, react, inverse_mass, obs, jacobi = lines(diag_ref)
    z = z_ref[...]
    edges = edge_ref[...]
    fixed = near_corr_ref.shape[0] - edges.shape[0] - vectors_ref.shape[0] - samples
    corr = slice(fixed, fixed + edges.shape[0])
    arrived = jnp.concatenate(pick(0, near_ref[0:samples, :], across_ref[0:samples, :]), axis=1)
    inner = scaled_ref[...] + dot(arrived, edges) * inverse_mass
    beyond_east, beyond_west = pick(1, far_ref[...], beyond_ref[...])
    own_east, own_west = pick(1, own_far_ref[...], own_beyond_ref[...])
    near_terms, across_terms = pick(
        0,
        jnp.concatenate([beyond_east, own_east], axis=1),
        jnp.concatenate([own_west, beyond_west], axis=1),
    )
    second_near = near_ref[samples:, :].astype(F32) + dot(near_terms, near_corr_ref[corr, :])
    second_across = across_ref[samples:, :].astype(F32) + dot(across_terms, across_corr_ref[corr, :])
    arrived2 = jnp.concatenate(pick(0, second_near, second_across), axis=1)
    stiff = dot(inner.astype(BF16), dense_ref[...]) + dot(arrived2, edges) + react * inner
    image = active * (stiff + obs * z)
    image_ref[...] = image
    level = levels(image * jacobi, edges).astype(BF16)
    coarse = fold(dot(vectors_ref[...], image.astype(BF16), 1, 1))
    high = coarse.astype(BF16)
    low = (coarse - high.astype(F32)).astype(BF16)
    sums = row_of(row_sum(active * right_ref[...].astype(F32), z), row_sum(z, image))
    row = lax.broadcasted_iota(jnp.int32, (SUM_ROWS, LANES), 0)
    tail = jnp.zeros((SUM_ROWS, LANES), F32)
    for i in range(3):
        part = sums.astype(BF16).astype(F32)
        tail = jnp.where(row == i, part, tail)
        sums = sums - part
    count, rows, _ = chunks_ref.shape
    slots = level.shape[1] // 2
    common = jnp.concatenate([high, low, tail.astype(BF16), level[:, 0:slots]], axis=0)
    chunks_ref[...] = jnp.broadcast_to(common[None], chunks_ref.shape)
    before = lax.rem(lax.axis_index("lon") + count - 1, count)
    chunks_ref[before, rows - samples :, :] = level[:, slots:]


def middle_kernel(pieces_ref, others_ref, second_ref, second_others_ref,
                  across_ref, near_ref, inverse_ref, right_ref, image_ref, vectors_ref,
                  dense_ref, edge_ref, diag_ref, z_ref, sums_ref, chunks_ref, coarse_ref):
    samples, nodes = right_ref.shape
    count, half, _ = pieces_ref.shape
    tail = slice(2 * half, 2 * half + SUM_ROWS)

    def add(d, total):
        return total + second_ref[d, tail, :].astype(F32) + second_others_ref[d, tail, :].astype(F32)

    parts = lax.fori_loop(0, count, add, jnp.zeros((SUM_ROWS, LANES), F32), unroll=min(count, 8))
    sums = parts[2:3] + parts[1:2] + parts[0:1]
    step = sums[:, 0 : LANES // 2] / sums[:, LANES // 2 :]
    step = jnp.concatenate([step, step], axis=1)

    def piece(side, d):
        first, change = ((pieces_ref, second_ref), (others_ref, second_others_ref))[side]
        moved = change[d, 0:half, :].astype(F32) + change[d, half : 2 * half, :].astype(F32)
        return (first[d].astype(F32) - step * moved).astype(BF16)

    unfold(count, piece, coarse_ref)
    active, react, inverse_mass, obs, jacobi = lines(diag_ref)
    image = image_ref[...]
    edges = edge_ref[...]
    step_column = column_of(step)[0:samples]
    residual = active * right_ref[...].astype(F32) - step_column * image
    kept, width = inverse_ref.shape
    fixed = width // LANES * kept + edges.shape[0]

    def rows_of(static_ref):
        return jnp.concatenate([static_ref[j * kept : (j + 1) * kept, :] for j in range(width // LANES)], axis=1)

    inverses = jnp.concatenate([inverse_ref[...], rows_of(near_ref), rows_of(across_ref)], axis=0)
    fixes = dot(inverses, coarse_ref[...]).astype(BF16)
    z = active * (residual * jacobi + dot(fixes[0:kept], vectors_ref[...], 0, 0))
    z_ref[...] = z

    def arriving(static_ref, fix, change):
        smooth_level = static_ref[fixed + kept :, :].astype(F32) - step_column * change.astype(F32)
        return (smooth_level + dot(fix, static_ref[fixed : fixed + kept, :], 0, 0)).astype(BF16)

    lon = lax.axis_index("lon")
    odd = lon & 1
    ahead, before = lax.rem(lon + 1, count), lax.rem(lon + count - 1, count)
    change = slice(2 * half + SUM_ROWS, second_ref.shape[1])
    from_near = arriving(near_ref, fixes[kept : 2 * kept], second_ref[ahead + odd * (before - ahead), change, :])
    from_across = arriving(across_ref, fixes[2 * kept :], second_ref[before + odd * (ahead - before), change, :])
    from_east, from_west = pick(0, from_near, from_across)
    arrived = jnp.concatenate([from_east, from_west], axis=1)
    stiff = dot(z.astype(BF16), dense_ref[...]) + react * z + dot(arrived, edges)
    curve = jnp.sum(stiff * stiff * inverse_mass + obs * z * z, axis=1, keepdims=True)
    products = row_of(row_sum(residual, z), row_sum(z, image))
    row = lax.broadcasted_iota(jnp.int32, (8, LANES), 0)
    chunk = jnp.where(row == 0, products, row_of(curve, curve))
    chunks_ref[...] = jnp.broadcast_to(chunk[None], chunks_ref.shape)
    sums_ref[...] = jnp.broadcast_to(sums, sums_ref.shape)


def finish_kernel(sums_ref, chunks_ref, first_ref, second_ref, out_ref):
    samples = first_ref.shape[0]
    half = LANES // 2
    totals = jnp.sum(chunks_ref[...], axis=0)
    norm0, curve0 = sums_ref[1:2, 0:half], sums_ref[1:2, half:]
    norm1, cross = totals[0:1, 0:half], totals[0:1, half:]
    curve = totals[1:2, 0:half]
    beta = norm1 / norm0
    step0 = norm0 / curve0
    step1 = norm1 / (curve + beta * (2.0 * cross + beta * curve0))
    scales = column_of(jnp.concatenate([step0 + step1 * beta, step1], axis=1))
    out_ref[...] = scales[0:samples] * first_ref[...] + scales[samples : 2 * samples] * second_ref[...]


def exchange(chunks, axes):
    return lax.all_to_all(chunks, axes, split_axis=0, concat_axis=0, tiled=True)


def other_band(array):
    return lax.ppermute(array, "lat", [(0, 1), (1, 0)])


def swap(array, reach, inner):
    size = lax.axis_size("lon")
    pairs = []
    for i in range(size):
        up = (i // reach) % 2 == (0 if inner else 1)
        pairs.append((i, (i + (reach if up else -reach)) % size))
    return lax.ppermute(array, "lon", pairs)


def body(
    right_side,
    stiffness_blocks,
    block_pattern,
    reaction,
    lumped_mass,
    obs_precision,
    coupling,
    east_rows,
    west_rows,
    iface_count,
    node_count,
    deflation,
    coarse_inverse,
):
    samples, nodes = right_side.shape
    slots = coupling.shape[0]
    vectors = deflation.shape[0]
    sectors = lax.axis_size("lon")
    domains = sectors * lax.axis_size("lat")
    half = vectors // 2
    react, mass, obs = reaction[None], lumped_mass[None], obs_precision[None]
    field = ((samples, nodes), F32)
    coarse_scratch = pltpu.VMEM((domains * vectors, samples), BF16)
    apply_cost = 2 * samples * nodes * nodes
    static = ((coarse_inverse.size // LANES + 2 * slots + vectors + samples, slots), BF16)
    inputs = (coupling, east_rows, west_rows, react, mass, obs, right_side, deflation, coarse_inverse, stiffness_blocks,
              block_pattern.T)
    line = pltpu.VMEM((1, nodes), F32)
    chunks, diag, edge, near_static, across_static, right, basis, stored, inverse, pattern = call(
        load_kernel,
        [((sectors, half, LANES), BF16), ((8, nodes), F32), ((2 * slots, nodes), BF16), static, static]
        + [(a.shape, a.dtype) for a in (right_side, deflation, stiffness_blocks, coarse_inverse, inputs[-1])],
        [SMEM, SMEM] + [HBM] * len(inputs),
        [node_count, iface_count] + [pltpu.with_memory_space_constraint(a, pltpu.HBM) for a in inputs],
        2 * samples * vectors * nodes,
        [line, line, line] + [pltpu.VMEM(a.shape, a.dtype) for a in (coupling, east_rows, west_rows)]
        + [pltpu.SemaphoreType.DMA((len(inputs),))],
    )
    near_static = swap(near_static, 1, True)
    across_static = swap(across_static, 1, False)
    near_static, across_static, pieces, stored = lax.optimization_barrier(
        (near_static, across_static, exchange(chunks, "lon"), stored)
    )
    (dense,) = call(
        prep_kernel,
        [((nodes, nodes), BF16)],
        [VMEM, VMEM],
        (pattern, stored),
        apply_cost,
        [pltpu.SMEM((2, block_pattern.shape[0]), jnp.int32), pltpu.VMEM((nodes, nodes), F32), pltpu.SemaphoreType.DMA],
    )
    others = other_band(pieces)
    z0, scaled, near, across, far, beyond = call(
        start_kernel,
        [field] * 2 + [((2 * samples, slots), BF16)] * 2 + [((samples, slots), BF16)] * 2,
        [VMEM] * 8,
        (pieces, others, inverse, right, basis, dense, edge, diag),
        apply_cost,
        [coarse_scratch],
    )
    across = swap(across, 1, False)
    got_beyond = swap(beyond, 2, False)
    near = swap(near, 1, True)
    got_far = swap(far, 2, True)
    image, chunks = call(
        image_kernel,
        [field, ((sectors, 2 * half + SUM_ROWS + samples, LANES), BF16)],
        [VMEM] * 15,
        (near, across, got_beyond, got_far, far, beyond, across_static, near_static, z0, scaled, dense, edge, diag, right, basis),
        apply_cost,
    )
    second = exchange(chunks, "lon")
    second_others = other_band(second)
    z1, sums, chunks = call(
        middle_kernel,
        [field, ((8, LANES), F32), ((domains, 8, LANES), F32)],
        [VMEM] * 13,
        (pieces, others, second, second_others, across_static, near_static,
         inverse, right, image, basis, dense, edge, diag),
        apply_cost,
        [coarse_scratch],
    )
    totals = exchange(chunks, ("lon", "lat"))
    (out,) = call(finish_kernel, [field], [VMEM] * 4, (sums, totals, z0, z1), 4 * samples * nodes)
    return out


def solution(mesh):
    placed = (
        P(None, ("grp", "lon", "lat")),
        P(("grp", "lon", "lat"), None, None),
        P(("grp", "lon", "lat"), None),
        P(("grp", "lon", "lat")),
        P(("grp", "lon", "lat")),
        P(("grp", "lon", "lat")),
        P(("grp", "lon", "lat"), None),
        P(("grp", "lon", "lat"), None),
        P(("grp", "lon", "lat"), None),
        P(("grp", "lon", "lat")),
        P(("grp", "lon", "lat")),
        P(None, ("grp", "lon", "lat")),
        P(("grp", "lon", "lat"), None),
    )
    return jax.shard_map(
        body, mesh=mesh, in_specs=placed, out_specs=P(None, ("grp", "lon", "lat")), check_vma=False
    )
```
